32 devices in a mesh: dp: 8 (over y, x, core), feat: 4 (over z).
Axes of the slice: x: 2, y: 2, z: 4, core: 2. Of those that a mesh axis runs over, the one named last changes fastest.
Arguments:
- view_features: bfloat16 [2, 1024, 8192], P(None, 'dp', 'feat'), may hold values from 0 to 55, as said below
- weight: float32 [8192, 8192], P('dp', 'feat'), may hold values from -64 to 64
- velocity: float32 [8192, 8192], P('dp', 'feat'), may hold values from -6 to 6
Outputs:
- new_weight: float32 [8192, 8192], P('dp', 'feat')
- new_velocity: float32 [8192, 8192], P('dp', 'feat')
The draws below stay inside these ranges and needn't reach their ends.
Inputs may be any that keep to these rules, and one draw needn't show every extreme that they name: `view_features`: nonnegative features.
All inputs are finite; a program needn't handle non-finite values.
Results may differ from the reference program's by a relative error of at most 0.039.
Values may be sent and summed in bfloat16 or wider, within the bound.
No kernel may reach another device: no remote copies, remote signals or barrier semaphores. Data moves between devices by JAX's collectives and lax.ppermute only.
A program may use at most 128 MiB of HBM per device.

```python
import math
import jax
import jax.numpy as jnp
from jax import lax

D = 8192
IMAGES = 1024
N_DP = 8
N_FEAT = 4


def draw_view_features(key, part):
    key_shared, key_own, key_column = jax.random.split(key, 3)
    position = jnp.arange(IMAGES, dtype=jnp.float32) / max(IMAGES - 1, 1)
    column = jnp.exp(jax.random.uniform(key_column, (1, 1, D), jnp.float32, math.log(0.5), math.log(2.0)))
    shared = jax.random.truncated_normal(key_shared, -4.0, 4.0, (1, IMAGES, D), jnp.float32)
    own = jax.random.truncated_normal(key_own, -4.0, 4.0, (2, IMAGES, D), jnp.float32)
    row_scale = jnp.exp(math.log(3.0) * position)[None, :, None]
    mixed = jnp.maximum(0.95 * shared + 0.3 * own + 0.6, 0.0) * row_scale * column
    return mixed.astype(jnp.bfloat16)


def draw_weight(key, part):
    key_base, key_common = jax.random.split(key, 2)
    span = max(D - 1, 1)
    row_pos = jnp.arange(D, dtype=jnp.float32)[:, None] / span
    col_pos = jnp.arange(D, dtype=jnp.float32)[None, :] / span
    base = jax.random.truncated_normal(key_base, -4.0, 4.0, (D, D), jnp.float32)
    common = jax.random.truncated_normal(key_common, -4.0, 4.0, (D, 1), jnp.float32)
    factor = math.log(3.0)
    return (0.7 * base + 0.7 * common) * jnp.exp(0.5 * factor * (row_pos + col_pos))


def steps_of(key, extent, cuts, low, high):
    level = 1.0
    for dim, parts in cuts:
        draws = jax.random.uniform(jax.random.fold_in(jax.random.fold_in(key, 6), dim), (parts,), jnp.float32, low / len(cuts), high / len(cuts))
        level = level * jnp.repeat(jnp.exp(draws), extent[dim] // parts).reshape((-1,) + (1,) * (len(extent) - 1 - dim))
    return level


def gaussian(own_key, shape, scale, reach, cuts=(), kind=jnp.bfloat16):
    entries = jax.random.normal(own_key, shape, jnp.float32) * scale
    if len(cuts) > 0:
        entries = steps_of(own_key, shape, cuts, -0.22, 0.18) * entries
    return jnp.clip(entries, min=-reach, max=reach).astype(kind)


def setup_inputs(seed: int = 0) -> dict:
    streams_of = jax.random.split(jax.random.key(seed), 4)
    return {
        "view_features": draw_view_features(jax.random.fold_in(streams_of[3], 71), 0),
        "weight": draw_weight(jax.random.fold_in(streams_of[3], 71), 0),
        "velocity": gaussian(streams_of[2], (D, D), 1.0, 6.0, ((0, 8), (1, 4)), jnp.float32),
    }


EPSILON = 1e-05
NORM_EPSILON = 1e-06
REDUNDANCY = 0.0051
MOMENTUM = 0.9
LEARN_RATE = 0.2

def round_half(value):
    return lax.optimization_barrier(value.astype(jnp.bfloat16)).astype(jnp.float32)

def reference(view_features, weight, velocity):
    block_dp = D // N_DP
    block_feat = D // N_FEAT
    highest = lax.Precision.HIGHEST
    flat_views = view_features.reshape(2 * IMAGES, D).astype(jnp.float32)
    weight_half = round_half(weight)

    def forward_block(index_block, running):
        start_at = (index_block * block_dp).astype(jnp.int32)
        part_views = lax.dynamic_slice_in_dim(flat_views, start_at, block_dp, 1)
        part_weight = lax.dynamic_slice_in_dim(weight_half, start_at, block_dp, 0)
        return running + round_half(jnp.dot(part_views, part_weight, precision=highest))
    outputs = lax.fori_loop(0, N_DP, forward_block, jnp.zeros((2 * IMAGES, D), jnp.float32))
    outputs = outputs.reshape(2, IMAGES, D)
    average = lax.optimization_barrier(jnp.mean(outputs, axis=1, keepdims=True))
    centered = outputs - average
    variance = lax.optimization_barrier(jnp.mean(centered * centered, axis=1, keepdims=True))
    inverse = lax.rsqrt(variance + EPSILON)
    normed = centered * inverse
    normed_half = round_half(normed)
    first_view = normed_half[0]
    second_view = normed_half[1]
    correlation = jnp.dot(first_view.T, second_view, precision=highest) / IMAGES
    diagonal = jnp.eye(D, dtype=bool)
    scaled = round_half(jnp.where(diagonal, -2.0 * (1.0 - correlation), 2.0 * REDUNDANCY * correlation) / IMAGES)

    def first_block(index_block, running):
        start_at = (index_block * block_feat).astype(jnp.int32)
        part_second = lax.dynamic_slice_in_dim(second_view, start_at, block_feat, 1)
        part_scaled = lax.dynamic_slice_in_dim(scaled, start_at, block_feat, 1)
        return running + round_half(jnp.dot(part_second, part_scaled.T, precision=highest))

    def second_block(index_block, running):
        start_at = (index_block * block_dp).astype(jnp.int32)
        part_first = lax.dynamic_slice_in_dim(first_view, start_at, block_dp, 1)
        part_scaled = lax.dynamic_slice_in_dim(scaled, start_at, block_dp, 0)
        return running + round_half(jnp.dot(part_first, part_scaled, precision=highest))
    first_grad = lax.fori_loop(0, N_FEAT, first_block, jnp.zeros((IMAGES, D), jnp.float32))
    second_grad = lax.fori_loop(0, N_DP, second_block, jnp.zeros((IMAGES, D), jnp.float32))
    grads = jnp.stack([first_grad, second_grad])
    grad_mean = lax.optimization_barrier(jnp.mean(grads, axis=1, keepdims=True))
    grad_cross = lax.optimization_barrier(jnp.mean(grads * normed, axis=1, keepdims=True))
    out_grad = round_half(inverse * (grads - grad_mean - normed * grad_cross))
    weight_grad = jnp.dot(flat_views.T, out_grad.reshape(2 * IMAGES, D), precision=highest)
    weight_norm = jnp.sqrt(jnp.sum(weight * weight))
    grad_norm = jnp.sqrt(jnp.sum(weight_grad * weight_grad))
    trust = weight_norm / (grad_norm + NORM_EPSILON)
    new_velocity = MOMENTUM * velocity + trust * weight_grad
    new_weight = weight - LEARN_RATE * new_velocity
    return (new_weight, new_velocity)
```

```python
import jax
import jax.numpy as jnp
from jax import lax
from jax.sharding import PartitionSpec as P

EPSILON = 1e-05
NORM_EPSILON = 1e-06
REDUNDANCY = 0.0051
MOMENTUM = 0.9
LEARN_RATE = 0.2


def per_device(view_features, weight, velocity):
    n_dp = lax.axis_size("dp")
    n_feat = lax.axis_size("feat")
    images_dev = view_features.shape[1]
    dp_width = weight.shape[0]
    batch = images_dev * n_dp
    per_feat = n_dp // n_feat
    weight_half = weight.astype(jnp.bfloat16)

    columns, normed, half, inverse, gram = [None] * 2, [None] * 2, [None] * 2, [None] * 2, [None] * 2
    for v in (1, 0):
        pieces = view_features[v].reshape(images_dev, per_feat, dp_width).transpose(1, 0, 2)
        rows = lax.all_gather(pieces, "feat", axis=0, tiled=True)
        columns[v] = lax.all_to_all(rows, "dp", split_axis=0, concat_axis=0, tiled=True).reshape(
            batch, dp_width
        )
        local_mean = jnp.mean(columns[v].astype(jnp.float32), 0).astype(jnp.bfloat16)
        offset = jnp.einsum("kf,k->f", weight_half, local_mean, preferred_element_type=jnp.float32)
        block = jnp.einsum(
            "kf,nk->fn", weight_half, columns[v], preferred_element_type=jnp.float32
        )
        block = (block - offset[:, None]).astype(jnp.bfloat16)
        outputs = lax.psum_scatter(block, "dp", scatter_dimension=0, tiled=True).astype(jnp.float32)
        centered = outputs - jnp.mean(outputs, 1, keepdims=True)
        variance = jnp.mean(centered * centered, 1, keepdims=True)
        inverse[v] = lax.rsqrt(variance + EPSILON)
        normed[v] = centered * inverse[v]
        half[v] = normed[v].astype(jnp.bfloat16)
        partial = jnp.einsum("fn,fm->nm", half[v], half[v], preferred_element_type=jnp.float32)
        gram[v] = lax.psum(partial.astype(jnp.bfloat16), ("dp", "feat"))

    first, second = half[0].astype(jnp.float32), half[1].astype(jnp.float32)
    diagonal = jnp.sum(first * second, 1, keepdims=True) / batch
    extra = (-2.0 * (1.0 - diagonal) - 2.0 * REDUNDANCY * diagonal) / batch
    weight_grad = 0.0
    for v in (0, 1):
        grads = jnp.einsum("nm,fm->fn", gram[1 - v], half[v], preferred_element_type=jnp.float32)
        grads = grads * (2.0 * REDUNDANCY / (batch * batch)) + extra * (second, first)[v]
        grad_mean = jnp.mean(grads, 1, keepdims=True)
        grad_cross = jnp.mean(grads * normed[v], 1, keepdims=True)
        out_grad = (inverse[v] * (grads - grad_mean - normed[v] * grad_cross)).astype(jnp.bfloat16)
        gathered = lax.all_gather(out_grad, "dp", axis=0, tiled=True)
        weight_grad += jnp.einsum(
            "nk,fn->kf", columns[v], gathered, preferred_element_type=jnp.float32
        )
    weight_local = jnp.sum(weight * weight)
    grad_local = jnp.sum(weight_grad * weight_grad)
    weight_sq, grad_sq = lax.psum((weight_local, grad_local), ("dp", "feat"))
    trust = jnp.sqrt(weight_sq) / (jnp.sqrt(grad_sq) + NORM_EPSILON)
    new_velocity = MOMENTUM * velocity + trust * weight_grad
    new_weight = weight - LEARN_RATE * new_velocity
    return (new_weight, new_velocity)


def solution(mesh):
    in_specs = (P(None, "dp", "feat"), P("dp", "feat"), P("dp", "feat"))
    out_specs = (P("dp", "feat"), P("dp", "feat"))
    return jax.shard_map(
        per_device, mesh=mesh, in_specs=in_specs, out_specs=out_specs, check_vma=False
    )
```

```python
import jax
import jax.numpy as jnp
from jax import lax
from jax.experimental import pallas as pl
from jax.experimental.pallas import tpu as pltpu
from jax.sharding import PartitionSpec as P

EPSILON = 1e-05
NORM_EPSILON = 1e-06
REDUNDANCY = 0.0051
MOMENTUM = 0.9
LEARN_RATE = 0.2


def swap(value, axis, bit):
    count = lax.axis_size(axis)
    return lax.ppermute(value, axis, [(i, i ^ (1 << bit)) for i in range(count)])


def bits_of(axis):
    return lax.axis_size(axis).bit_length() - 1


def bit_value(axis, bit):
    return (lax.axis_index(axis) >> bit) & 1


def pick(stack, index):
    return lax.dynamic_index_in_dim(stack, index, 0, keepdims=False)


def join(mine, other, bit):
    return jnp.where(
        bit == 0, jnp.concatenate([mine, other], 0), jnp.concatenate([other, mine], 0)
    )


def add_up(mine, other):
    return mine.astype(jnp.float32) + other.astype(jnp.float32)


def scatter_sum(block, order, last=jnp.float32):
    for place, bit in enumerate(order):
        mine = bit_value("dp", bit)
        halves = block.reshape((2, block.shape[0] // 2) + block.shape[1:])
        other = swap(pick(halves, 1 - mine), "dp", bit)
        kind = last if place == len(order) - 1 else jnp.bfloat16
        block = add_up(pick(halves, mine), other).astype(kind)
    return block


def gather_all(piece, order):
    for bit in reversed(order):
        piece = join(piece, swap(piece, "dp", bit), bit_value("dp", bit))
    return piece


def sum_feat(value):
    for bit in range(bits_of("feat")):
        value = add_up(value, swap(value, "feat", bit)).astype(value.dtype)
    return value


def sum_everywhere(value):
    for axis in ("dp", "feat"):
        for bit in range(bits_of(axis)):
            value = value + swap(value, axis, bit)
    return value


def weight_grad_kernel(first_ref, second_ref, grad_first_ref, grad_second_ref, out_ref, square_ref):
    contract = (((1,), (1,)), ((), ()))
    total = lax.dot_general(
        first_ref[...], grad_first_ref[...], contract, preferred_element_type=jnp.float32
    )
    total += lax.dot_general(
        second_ref[...], grad_second_ref[...], contract, preferred_element_type=jnp.float32
    )
    out_ref[...] = total
    square = total * total
    folded = jnp.sum(square.reshape(-1, 8, square.shape[1]), 0)
    part = folded[:, :128]
    for start in range(128, square.shape[1], 128):
        part += folded[:, start : start + 128]

    @pl.when((pl.program_id(0) == 0) & (pl.program_id(1) == 0))
    def _():
        square_ref[...] = jnp.zeros_like(square_ref)

    square_ref[...] += part


def weight_grad_of(columns, gathered):
    depth, batch = columns[0].shape
    width = gathered[0].shape[0]
    rows, cols = min(512, depth), min(512, width)
    left = pl.BlockSpec((rows, batch), lambda j, i: (i, 0))
    right = pl.BlockSpec((cols, batch), lambda j, i: (j, 0))
    return pl.pallas_call(
        weight_grad_kernel,
        grid=(width // cols, depth // rows),
        in_specs=[left, left, right, right],
        out_specs=[
            pl.BlockSpec((rows, cols), lambda j, i: (i, j)),
            pl.BlockSpec((8, 128), lambda j, i: (0, 0)),
        ],
        out_shape=[
            jax.ShapeDtypeStruct((depth, width), jnp.float32),
            jax.ShapeDtypeStruct((8, 128), jnp.float32),
        ],
        compiler_params=pltpu.CompilerParams(vmem_limit_bytes=48 * 1024 * 1024),
        cost_estimate=pl.CostEstimate(
            flops=4 * depth * width * batch, bytes_accessed=12 * depth * width, transcendentals=0
        ),
    )(*columns, *gathered)


def per_device(view_features, weight, velocity):
    n_dp = lax.axis_size("dp")
    n_feat = lax.axis_size("feat")
    images_dev = view_features.shape[1]
    dp_width, feat_width = weight.shape
    batch = images_dev * n_dp
    per_feat = n_dp // n_feat
    high_bits = list(range(1, bits_of("dp")))
    orders = ([0] + high_bits, [0] + high_bits[::-1])
    weight_half = weight.astype(jnp.bfloat16)
    half_width = feat_width // 2
    core = bit_value("dp", 0)

    columns, normed, half, inverse, gram = [None] * 2, [None] * 2, [None] * 2, [None] * 2, [None] * 2
    for v in (1, 0):
        pieces = view_features[v].reshape(images_dev, per_feat, dp_width).transpose(1, 0, 2)
        rows = lax.all_gather(pieces, "feat", axis=0, tiled=True)
        columns[v] = lax.all_to_all(rows, "dp", split_axis=0, concat_axis=0, tiled=True).reshape(
            batch, dp_width
        )
        local_mean = jnp.mean(columns[v].astype(jnp.float32), 0).astype(jnp.bfloat16)
        offset = jnp.einsum("kf,k->f", weight_half, local_mean, preferred_element_type=jnp.float32)
        block = jnp.einsum(
            "kf,nk->fn", weight_half, columns[v], preferred_element_type=jnp.float32
        )
        block = (block - offset[:, None]).astype(jnp.bfloat16)
        outputs = jnp.concatenate(
            [
                scatter_sum(block[path * half_width : (path + 1) * half_width], orders[path])
                for path in range(2)
            ],
            0,
        )
        centered = outputs - jnp.mean(outputs, 1, keepdims=True)
        variance = jnp.mean(centered * centered, 1, keepdims=True)
        inverse[v] = lax.rsqrt(variance + EPSILON)
        normed[v] = centered * inverse[v]
        half[v] = normed[v].astype(jnp.bfloat16)
        partial = jnp.einsum("fn,fm->nm", half[v], half[v], preferred_element_type=jnp.float32)
        partial = partial.astype(jnp.bfloat16)
        sums = [
            sum_feat(
                scatter_sum(
                    partial[path * batch // 2 : (path + 1) * batch // 2], orders[path], jnp.bfloat16
                )
            )
            for path in range(2)
        ]
        gram[v] = jnp.concatenate([gather_all(sums[path], orders[path]) for path in range(2)], 0)

    first, second = half[0].astype(jnp.float32), half[1].astype(jnp.float32)
    diagonal = jnp.sum(first * second, 1, keepdims=True) / batch
    extra = (-2.0 * (1.0 - diagonal) - 2.0 * REDUNDANCY * diagonal) / batch
    gathered = [None] * 2
    for v in (0, 1):
        grads = jnp.einsum("nm,fm->fn", gram[1 - v], half[v], preferred_element_type=jnp.float32)
        grads = grads * (2.0 * REDUNDANCY / (batch * batch)) + extra * (second, first)[v]
        grad_mean = jnp.mean(grads, 1, keepdims=True)
        grad_cross = jnp.mean(grads * normed[v], 1, keepdims=True)
        out_grad = (inverse[v] * (grads - grad_mean - normed[v] * grad_cross)).astype(jnp.bfloat16)
        share = out_grad.shape[0] // 2
        gathered[v] = jnp.concatenate(
            [
                gather_all(out_grad[path * share : (path + 1) * share], orders[path])
                for path in range(2)
            ],
            0,
        )
    weight_grad, squares = weight_grad_of([columns[0].T, columns[1].T], gathered)
    sums = sum_everywhere(jnp.stack([jnp.sum(weight * weight), jnp.sum(squares)]))
    trust = jnp.sqrt(sums[0]) / (jnp.sqrt(sums[1]) + NORM_EPSILON)
    new_velocity = MOMENTUM * velocity + trust * weight_grad
    new_weight = weight - LEARN_RATE * new_velocity
    return (new_weight, new_velocity)


def solution(mesh):
    in_specs = (P(None, "dp", "feat"), P("dp", "feat"), P("dp", "feat"))
    out_specs = (P("dp", "feat"), P("dp", "feat"))
    return jax.shard_map(
        per_device, mesh=mesh, in_specs=in_specs, out_specs=out_specs, check_vma=False
    )
```

```python
import jax
import jax.numpy as jnp
from jax import lax
from jax.experimental import pallas as pl
from jax.experimental.pallas import tpu as pltpu
from jax.sharding import PartitionSpec as P

EPSILON = 1e-05
NORM_EPSILON = 1e-06
REDUNDANCY = 0.0051
MOMENTUM = 0.9
LEARN_RATE = 0.2


def swap(value, axis, bit):
    count = lax.axis_size(axis)
    return lax.ppermute(value, axis, [(i, i ^ (1 << bit)) for i in range(count)])


def bits_of(axis):
    return lax.axis_size(axis).bit_length() - 1


def bit_value(axis, bit):
    return (lax.axis_index(axis) >> bit) & 1


def pick(stack, index):
    return lax.dynamic_index_in_dim(stack, index, 0, keepdims=False)


def join(mine, other, bit):
    return jnp.where(
        bit == 0, jnp.concatenate([mine, other], 0), jnp.concatenate([other, mine], 0)
    )


def add_up(mine, other):
    return mine.astype(jnp.float32) + other.astype(jnp.float32)


def scatter_sum(block, order, last=jnp.float32):
    for place, bit in enumerate(order):
        mine = bit_value("dp", bit)
        halves = block.reshape((2, block.shape[0] // 2) + block.shape[1:])
        other = swap(pick(halves, 1 - mine), "dp", bit)
        kind = last if place == len(order) - 1 else jnp.bfloat16
        block = add_up(pick(halves, mine), other).astype(kind)
    return block


def gather_all(piece, order):
    for bit in reversed(order):
        piece = join(piece, swap(piece, "dp", bit), bit_value("dp", bit))
    return piece


def sum_feat(value):
    for bit in range(bits_of("feat")):
        value = add_up(value, swap(value, "feat", bit)).astype(value.dtype)
    return value


def spread_features(rows, width):
    n_feat = lax.axis_size("feat")
    n_chip = lax.axis_size("dp") // 2
    assert n_chip == n_feat and rows.shape[1] == 2 * width
    core, chip = bit_value("dp", 0), lax.axis_index("dp") >> 1
    mine = lax.dynamic_slice_in_dim(rows, core * width, width, 1)
    other = swap(lax.dynamic_slice_in_dim(rows, (1 - core) * width, width, 1), "dp", 0)
    shares = [join(mine, other, core)]
    for _ in range(1, n_feat):
        ring = [(i, (i + 1) % n_feat) for i in range(n_feat)]
        shares.append(lax.ppermute(shares[-1], "feat", ring))
    count = shares[0].shape[0]
    columns = jnp.zeros((n_chip * count, width), rows.dtype)
    for mask in range(n_chip):
        peer = chip ^ mask
        part = lax.select_n(lax.rem(lax.axis_index("feat") - peer + n_feat, n_feat), *shares)
        if mask:
            part = lax.ppermute(part, "dp", [(i, i ^ (2 * mask)) for i in range(2 * n_chip)])
        columns = lax.dynamic_update_slice_in_dim(columns, part, peer * count, 0)
    return columns


def sum_everywhere(value):
    for axis in ("dp", "feat"):
        for bit in range(bits_of(axis)):
            value = value + swap(value, axis, bit)
    return value


def weight_grad_kernel(first_ref, second_ref, grad_first_ref, grad_second_ref, out_ref, square_ref):
    contract = (((1,), (1,)), ((), ()))
    total = lax.dot_general(
        first_ref[...], grad_first_ref[...], contract, preferred_element_type=jnp.float32
    )
    total += lax.dot_general(
        second_ref[...], grad_second_ref[...], contract, preferred_element_type=jnp.float32
    )
    out_ref[...] = total
    square = total * total
    folded = jnp.sum(square.reshape(-1, 8, square.shape[1]), 0)
    part = folded[:, :128]
    for start in range(128, square.shape[1], 128):
        part += folded[:, start : start + 128]

    @pl.when((pl.program_id(0) == 0) & (pl.program_id(1) == 0))
    def _():
        square_ref[...] = jnp.zeros_like(square_ref)

    square_ref[...] += part


def weight_grad_of(columns, gathered):
    depth, batch = columns[0].shape
    width = gathered[0].shape[0]
    rows, cols = min(512, depth), min(512, width)
    left = pl.BlockSpec((rows, batch), lambda j, i: (i, 0))
    right = pl.BlockSpec((cols, batch), lambda j, i: (j, 0))
    return pl.pallas_call(
        weight_grad_kernel,
        grid=(width // cols, depth // rows),
        in_specs=[left, left, right, right],
        out_specs=[
            pl.BlockSpec((rows, cols), lambda j, i: (i, j)),
            pl.BlockSpec((8, 128), lambda j, i: (0, 0)),
        ],
        out_shape=[
            jax.ShapeDtypeStruct((depth, width), jnp.float32),
            jax.ShapeDtypeStruct((8, 128), jnp.float32),
        ],
        compiler_params=pltpu.CompilerParams(vmem_limit_bytes=48 * 1024 * 1024),
        cost_estimate=pl.CostEstimate(
            flops=4 * depth * width * batch, bytes_accessed=12 * depth * width, transcendentals=0
        ),
    )(*columns, *gathered)


def per_device(view_features, weight, velocity):
    n_dp = lax.axis_size("dp")
    images_dev = view_features.shape[1]
    dp_width, feat_width = weight.shape
    batch = images_dev * n_dp
    high_bits = list(range(1, bits_of("dp")))
    orders = ([0] + high_bits, [0] + high_bits[::-1])
    weight_half = weight.astype(jnp.bfloat16)
    half_width = feat_width // 2
    core = bit_value("dp", 0)

    columns, normed, half, inverse, gram = [None] * 2, [None] * 2, [None] * 2, [None] * 2, [None] * 2
    for v in (1, 0):
        columns[v] = spread_features(view_features[v], dp_width)
        local_mean = jnp.mean(columns[v].astype(jnp.float32), 0).astype(jnp.bfloat16)
        offset = jnp.einsum("kf,k->f", weight_half, local_mean, preferred_element_type=jnp.float32)
        block = jnp.einsum(
            "kf,nk->fn", weight_half, columns[v], preferred_element_type=jnp.float32
        )
        block = (block - offset[:, None]).astype(jnp.bfloat16)
        outputs = jnp.concatenate(
            [
                scatter_sum(block[path * half_width : (path + 1) * half_width], orders[path])
                for path in range(2)
            ],
            0,
        )
        centered = outputs - jnp.mean(outputs, 1, keepdims=True)
        variance = jnp.mean(centered * centered, 1, keepdims=True)
        inverse[v] = lax.rsqrt(variance + EPSILON)
        normed[v] = centered * inverse[v]
        half[v] = normed[v].astype(jnp.bfloat16)
        partial = jnp.einsum("fn,fm->nm", half[v], half[v], preferred_element_type=jnp.float32)
        partial = partial.astype(jnp.bfloat16)
        sums = [
            sum_feat(
                scatter_sum(
                    partial[path * batch // 2 : (path + 1) * batch // 2], orders[path], jnp.bfloat16
                )
            )
            for path in range(2)
        ]
        gram[v] = jnp.concatenate([gather_all(sums[path], orders[path]) for path in range(2)], 0)

    first, second = half[0].astype(jnp.float32), half[1].astype(jnp.float32)
    diagonal = jnp.sum(first * second, 1, keepdims=True) / batch
    extra = (-2.0 * (1.0 - diagonal) - 2.0 * REDUNDANCY * diagonal) / batch
    gathered = [None] * 2
    for v in (0, 1):
        grads = jnp.einsum("nm,fm->fn", gram[1 - v], half[v], preferred_element_type=jnp.float32)
        grads = grads * (2.0 * REDUNDANCY / (batch * batch)) + extra * (second, first)[v]
        grad_mean = jnp.mean(grads, 1, keepdims=True)
        grad_cross = jnp.mean(grads * normed[v], 1, keepdims=True)
        out_grad = (inverse[v] * (grads - grad_mean - normed[v] * grad_cross)).astype(jnp.bfloat16)
        share = out_grad.shape[0] // 2
        gathered[v] = jnp.concatenate(
            [
                gather_all(out_grad[path * share : (path + 1) * share], orders[path])
                for path in range(2)
            ],
            0,
        )
    weight_grad, squares = weight_grad_of([columns[0].T, columns[1].T], gathered)
    sums = sum_everywhere(jnp.stack([jnp.sum(weight * weight), jnp.sum(squares)]))
    trust = jnp.sqrt(sums[0]) / (jnp.sqrt(sums[1]) + NORM_EPSILON)
    new_velocity = MOMENTUM * velocity + trust * weight_grad
    new_weight = weight - LEARN_RATE * new_velocity
    return (new_weight, new_velocity)


def solution(mesh):
    in_specs = (P(None, "dp", "feat"), P("dp", "feat"), P("dp", "feat"))
    out_specs = (P("dp", "feat"), P("dp", "feat"))
    return jax.shard_map(
        per_device, mesh=mesh, in_specs=in_specs, out_specs=out_specs, check_vma=False
    )
```

```python
import jax
import jax.numpy as jnp
from jax import lax
from jax.experimental import pallas as pl
from jax.experimental.pallas import tpu as pltpu
from jax.sharding import PartitionSpec as P

EPSILON = 1e-05
NORM_EPSILON = 1e-06
REDUNDANCY = 0.0051
MOMENTUM = 0.9
LEARN_RATE = 0.2
ROWS_BY_ROWS = (((1,), (1,)), ((), ()))


def swap(value, axis, mask):
    return lax.ppermute(value, axis, [(i, i ^ mask) for i in range(lax.axis_size(axis))])


def bits_of(axis):
    return lax.axis_size(axis).bit_length() - 1


def bit_value(axis, bit):
    return (lax.axis_index(axis) >> bit) & 1


def pick(stack, index):
    return lax.dynamic_index_in_dim(stack, index, 0, keepdims=False)


def join(mine, other, bit):
    return jnp.where(
        bit == 0, jnp.concatenate([mine, other], 0), jnp.concatenate([other, mine], 0)
    )


def add_up(mine, other):
    return mine.astype(jnp.float32) + other.astype(jnp.float32)


def scatter_sum(block, bits, last=jnp.float32):
    for place, bit in enumerate(bits):
        mine = bit_value("dp", bit)
        halves = block.reshape((2, block.shape[0] // 2) + block.shape[1:])
        other = swap(pick(halves, 1 - mine), "dp", 1 << bit)
        kind = last if place == len(bits) - 1 else jnp.bfloat16
        block = add_up(pick(halves, mine), other).astype(kind)
    return block


def gather_all(piece, bits):
    for bit in reversed(bits):
        piece = join(piece, swap(piece, "dp", 1 << bit), bit_value("dp", bit))
    return piece


def sum_feat(value):
    for bit in range(bits_of("feat")):
        value = add_up(value, swap(value, "feat", 1 << bit)).astype(value.dtype)
    return value


def sum_everywhere(value):
    for axis in ("dp", "feat"):
        others = [swap(value, axis, mask) for mask in range(1, lax.axis_size(axis))]
        for other in others:
            value = value + other
    return value


def fold(square):
    part = jnp.sum(square.reshape(-1, 8, square.shape[1]), 0)
    return sum(part[:, start : start + 128] for start in range(0, part.shape[1], 128))


def weight_kernel(weight_ref, turned_ref, square_ref):
    block = weight_ref[...]
    turned_ref[...] = block.T.astype(jnp.bfloat16)

    @pl.when(pl.program_id(0) == 0)
    def _():
        square_ref[...] = jnp.zeros_like(square_ref)

    square_ref[...] += fold(block * block)


def turn_weight(weight):
    depth, width = weight.shape
    step = min(256, width)
    return pl.pallas_call(
        weight_kernel,
        grid=(width // step,),
        in_specs=[pl.BlockSpec((depth, step), lambda j: (0, j))],
        out_specs=[
            pl.BlockSpec((step, depth), lambda j: (j, 0)),
            pl.BlockSpec((8, 128), lambda j: (0, 0)),
        ],
        out_shape=[
            jax.ShapeDtypeStruct((width, depth), jnp.bfloat16),
            jax.ShapeDtypeStruct((8, 128), jnp.float32),
        ],
        compiler_params=pltpu.CompilerParams(vmem_limit_bytes=16 * 1024 * 1024),
        cost_estimate=pl.CostEstimate(
            flops=2 * depth * width, bytes_accessed=6 * depth * width, transcendentals=0
        ),
    )(weight)


def forward_kernel(half_ref, turned_ref, columns_ref, out_ref):
    block = lax.dot_general(
        turned_ref[...], columns_ref[...], ROWS_BY_ROWS, preferred_element_type=jnp.float32
    )
    out_ref[...] = (block - jnp.mean(block, 1, keepdims=True)).astype(jnp.bfloat16)


def forward_half(half, turned, columns):
    width, depth = turned.shape
    batch = columns.shape[0]
    quarter = width // 4
    step = min(256, quarter)
    steps = quarter // step
    return pl.pallas_call(
        forward_kernel,
        grid_spec=pltpu.PrefetchScalarGridSpec(
            num_scalar_prefetch=1,
            grid=(2, steps),
            in_specs=[
                pl.BlockSpec((step, depth), lambda p, i, h: ((2 * p + h[0]) * steps + i, 0)),
                pl.BlockSpec((batch, depth), lambda p, i, h: (0, 0)),
            ],
            out_specs=pl.BlockSpec((step, batch), lambda p, i, h: (p * steps + i, 0)),
        ),
        out_shape=jax.ShapeDtypeStruct((2 * quarter, batch), jnp.bfloat16),
        compiler_params=pltpu.CompilerParams(vmem_limit_bytes=20 * 1024 * 1024),
        cost_estimate=pl.CostEstimate(
            flops=4 * quarter * depth * batch,
            bytes_accessed=4 * quarter * (depth + batch) + 2 * batch * depth,
            transcendentals=0,
        ),
    )(half.reshape(1), turned, columns)


def grad_kernel(has_base, core_ref, *refs):
    turned_ref, pieces = refs[0], refs[1:5]
    if has_base:
        base_ref, out_ref, square_ref = refs[5:]
    else:
        (out_ref,) = refs[5:]
    place = pl.program_id(0)
    for index, piece_ref in enumerate(pieces):

        @pl.when(place == index)
        def _():
            total = lax.dot_general(
                turned_ref[...], piece_ref[...], ROWS_BY_ROWS, preferred_element_type=jnp.float32
            )
            if has_base:
                total += base_ref[...]
            out_ref[...] = total

    if has_base:

        @pl.when((place == 0) & (pl.program_id(1) == 0))
        def _():
            square_ref[...] = jnp.zeros_like(square_ref)

        total = out_ref[...]
        square_ref[...] += fold(total * total)


def weight_grad_of(core, turned, pieces, base=None):
    depth, batch = turned.shape
    cols = pieces[0].shape[0]
    width = 4 * cols
    rows = min(512, depth)
    whole = pl.BlockSpec((cols, batch), lambda j, i, c: (0, 0))
    tile = pl.BlockSpec((rows, cols), lambda j, i, c: (i, (j >> 1) * 2 + ((j & 1) ^ c[0])))
    square = pl.BlockSpec((8, 128), lambda j, i, c: (0, 0))
    out_shape = [jax.ShapeDtypeStruct((depth, width), jnp.float32)]
    if base is not None:
        out_shape.append(jax.ShapeDtypeStruct((8, 128), jnp.float32))

    def kernel(core_ref, *refs):
        grad_kernel(base is not None, core_ref, *refs)

    return pl.pallas_call(
        kernel,
        grid_spec=pltpu.PrefetchScalarGridSpec(
            num_scalar_prefetch=1,
            grid=(4, depth // rows),
            in_specs=[pl.BlockSpec((rows, batch), lambda j, i, c: (i, 0))]
            + [whole] * 4
            + ([tile] if base is not None else []),
            out_specs=[tile, square] if base is not None else [tile],
        ),
        out_shape=out_shape,
        compiler_params=pltpu.CompilerParams(vmem_limit_bytes=28 * 1024 * 1024),
        cost_estimate=pl.CostEstimate(
            flops=2 * depth * width * batch, bytes_accessed=8 * depth * width, transcendentals=0
        ),
    )(core.reshape(1), turned, *pieces, *([base] if base is not None else []))


def core_shares(rows, width):
    core = bit_value("dp", 0)
    mine = lax.dynamic_slice_in_dim(rows, core * width, width, 1)
    other = swap(lax.dynamic_slice_in_dim(rows, (1 - core) * width, width, 1), "dp", 1)
    return join(mine, other, core)


def go_round(shares):
    n_feat = lax.axis_size("feat")
    ring = [(i, (i + 1) % n_feat) for i in range(n_feat)]
    rounds = [shares]
    for _ in range(1, n_feat):
        rounds.append([lax.ppermute(share, "feat", ring) for share in rounds[-1]])
    return rounds


def spread_plane(rounds):
    n_feat = lax.axis_size("feat")
    n_chip = lax.axis_size("dp") // 2
    chip = lax.axis_index("dp") >> 1
    n_share = len(rounds[0])
    count, width = rounds[0][0].shape
    columns = jnp.zeros((n_chip * n_share * count, width), rounds[0][0].dtype)
    for mask in range(n_chip):
        peer = chip ^ mask
        back = lax.rem(lax.axis_index("feat") - peer + n_feat, n_feat)
        for place in range(n_share):
            part = lax.select_n(back, *[shares[place] for shares in rounds])
            if mask:
                part = swap(part, "dp", 2 * mask)
            columns = lax.dynamic_update_slice_in_dim(
                columns, part, (peer * n_share + place) * count, 0
            )
    return columns


def per_device(view_features, weight, velocity):
    n_dp = lax.axis_size("dp")
    dp_width, feat_width = weight.shape
    batch = view_features.shape[1] * n_dp
    assert n_dp == 2 * lax.axis_size("feat") and view_features.shape[2] == 2 * dp_width
    high = list(range(1, bits_of("dp")))
    orders = (high, high[::-1])
    core = bit_value("dp", 0)
    turned, weight_squares = turn_weight(weight)
    half_width = feat_width // 4

    columns, normed, half, inverse, gram = [None] * 2, [None] * 2, [None] * 2, [None] * 2, [None] * 2
    shares = [core_shares(view_features[v], dp_width) for v in (0, 1)]
    parts = [[s[: s.shape[0] // 2], s[s.shape[0] // 2 :]] for s in shares]
    rounds = [None] * 2
    rounds[1] = go_round(parts[1])
    parts[0], rounds[1][-2] = lax.optimization_barrier((parts[0], rounds[1][-2]))
    rounds[0] = go_round(parts[0])
    for v in (1, 0):
        columns[v] = spread_plane(rounds[v])
        sent = forward_half(1 - core, turned, columns[v])
        other = swap(sent, "dp", 1)
        kept = forward_half(core, turned, columns[v])
        block = add_up(kept, other).astype(jnp.bfloat16)
        outputs = jnp.concatenate(
            [
                scatter_sum(block[path * half_width : (path + 1) * half_width], orders[path])
                for path in range(2)
            ],
            0,
        )
        centered = outputs - jnp.mean(outputs, 1, keepdims=True)
        variance = jnp.mean(centered * centered, 1, keepdims=True)
        inverse[v] = lax.rsqrt(variance + EPSILON)
        normed[v] = centered * inverse[v]
        half[v] = normed[v].astype(jnp.bfloat16)
        partial = jnp.einsum("fn,fm->nm", half[v], half[v], preferred_element_type=jnp.float32)
        partial = partial.astype(jnp.bfloat16)
        sums = [
            sum_feat(
                scatter_sum(
                    partial[path * batch // 2 : (path + 1) * batch // 2],
                    [0] + orders[path],
                    jnp.bfloat16,
                )
            )
            for path in range(2)
        ]
        gram[v] = jnp.concatenate(
            [gather_all(sums[path], [0] + orders[path]) for path in range(2)], 0
        )

    first, second = half[0].astype(jnp.float32), half[1].astype(jnp.float32)
    diagonal = jnp.sum(first * second, 1, keepdims=True) / batch
    extra = (-2.0 * (1.0 - diagonal) - 2.0 * REDUNDANCY * diagonal) / batch
    result = []
    for v in (0, 1):
        grads = jnp.einsum("nm,fm->fn", gram[1 - v], half[v], preferred_element_type=jnp.float32)
        grads = grads * (2.0 * REDUNDANCY / (batch * batch)) + extra * (second, first)[v]
        grad_mean = jnp.mean(grads, 1, keepdims=True)
        grad_cross = jnp.mean(grads * normed[v], 1, keepdims=True)
        out_grad = (inverse[v] * (grads - grad_mean - normed[v] * grad_cross)).astype(jnp.bfloat16)
        share = out_grad.shape[0] // 2
        pieces = []
        for path in range(2):
            own = gather_all(out_grad[path * share : (path + 1) * share], orders[path])
            pieces += [own, swap(own, "dp", 1)]
        result = weight_grad_of(core, columns[v].T, pieces, *result)
    weight_grad, squares = result
    sums = sum_everywhere(jnp.stack([jnp.sum(weight_squares), jnp.sum(squares)]))
    trust = jnp.sqrt(sums[0]) / (jnp.sqrt(sums[1]) + NORM_EPSILON)
    new_velocity = MOMENTUM * velocity + trust * weight_grad
    new_weight = weight - LEARN_RATE * new_velocity
    return (new_weight, new_velocity)


def solution(mesh):
    in_specs = (P(None, "dp", "feat"), P("dp", "feat"), P("dp", "feat"))
    out_specs = (P("dp", "feat"), P("dp", "feat"))
    return jax.shard_map(
        per_device, mesh=mesh, in_specs=in_specs, out_specs=out_specs, check_vma=False
    )
```

```python
import jax
import jax.numpy as jnp
from jax import lax
from jax.experimental import pallas as pl
from jax.experimental.pallas import tpu as pltpu
from jax.sharding import PartitionSpec as P

EPSILON = 1e-05
NORM_EPSILON = 1e-06
REDUNDANCY = 0.0051
MOMENTUM = 0.9
LEARN_RATE = 0.2
ROWS_BY_ROWS = (((1,), (1,)), ((), ()))
MIB = 1024 * 1024
F32, BF16 = jnp.float32, jnp.bfloat16


def swap(value, axis, mask):
    return lax.ppermute(value, axis, [(i, i ^ mask) for i in range(lax.axis_size(axis))])


def bit_value(axis, bit):
    return (lax.axis_index(axis) >> bit) & 1


def join(mine, other, bit):
    return jnp.where(
        bit == 0, jnp.concatenate([mine, other], 0), jnp.concatenate([other, mine], 0)
    )


def sum_everywhere(value):
    for axis in ("dp", "feat"):
        others = [swap(value, axis, mask) for mask in range(1, lax.axis_size(axis))]
        for other in others:
            value = value + other
    return value


def whole(array):
    zeros = (0,) * array.ndim
    return pl.BlockSpec(array.shape, lambda *_: zeros, pipeline_mode=pl.Buffered(1))


def like(shape, kind):
    return jax.ShapeDtypeStruct(shape, kind)


def run(body, scalars, operands, in_specs, outs, out_specs, grid=(1,), scratch=(), after=(),
        flops=0, moved=0, limit=32):
    n_in, n_after = len(operands), len(after)

    def kernel(scalars_ref, *refs):
        body(scalars_ref, *refs[:n_in], *refs[n_in + n_after :])

    return pl.pallas_call(
        kernel,
        grid_spec=pltpu.PrefetchScalarGridSpec(
            num_scalar_prefetch=1,
            grid=grid,
            in_specs=list(in_specs) + [pl.BlockSpec(memory_space=pl.ANY)] * n_after,
            out_specs=list(out_specs),
            scratch_shapes=list(scratch),
        ),
        out_shape=list(outs),
        compiler_params=pltpu.CompilerParams(vmem_limit_bytes=limit * MIB),
        cost_estimate=pl.CostEstimate(flops=flops, bytes_accessed=moved, transcendentals=0),
    )(scalars, *operands, *after)


def fold(square):
    part = jnp.sum(square.reshape(-1, 8, square.shape[1]), 0)
    return sum(part[:, start : start + 128] for start in range(0, part.shape[1], 128))


def turn_weight(weight, half):
    depth, width = weight.shape
    quarter = width // 4
    step = min(256, quarter)
    steps = quarter // step

    def body(half_ref, weight_ref, turned_ref, square_ref):
        block = weight_ref[...]
        turned_ref[...] = block.T.astype(BF16)

        @pl.when((pl.program_id(0) == 0) & (pl.program_id(1) == 0))
        def _():
            square_ref[...] = jnp.zeros_like(square_ref)

        square_ref[...] += fold(block * block)

    return run(
        body, half.reshape(1), [weight],
        [pl.BlockSpec((depth, step), lambda p, i, h: (0, (2 * p + h[0]) * steps + i))],
        [like((2 * quarter, depth), BF16), like((8, 128), F32)],
        [
            pl.BlockSpec((step, depth), lambda p, i, h: (p * steps + i, 0)),
            pl.BlockSpec((8, 128), lambda p, i, h: (0, 0)),
        ],
        grid=(2, steps), flops=depth * width, moved=3 * depth * width, limit=16,
    )


def share_of(view_features, view, after=()):
    _, count, width = view_features.shape

    def body(_, rows_ref, out_ref):
        out_ref[...] = rows_ref[...]

    (out,) = run(
        body, jnp.zeros((1,), jnp.int32), [view_features],
        [pl.BlockSpec((None, count, width), lambda i, s: (view, 0, 0))],
        [like((count, width), BF16)], [pl.BlockSpec((count, width), lambda i, s: (0, 0))],
        after=after, moved=4 * count * width, limit=8,
    )
    return out


def go_round(share):
    n_feat = lax.axis_size("feat")
    shares = [share]
    for _ in range(1, n_feat):
        ring = [(i, (i + 1) % n_feat) for i in range(n_feat)]
        shares.append(lax.ppermute(shares[-1], "feat", ring))
    return shares


def choose(shares, n_chip, after=()):
    n_feat = len(shares)
    chip = lax.axis_index("dp") >> 1
    back = [lax.rem(lax.axis_index("feat") - (chip ^ mask) + n_feat, n_feat) for mask in range(n_chip)]

    def body(back_ref, *refs):
        for mask in range(n_chip):
            for place in range(n_feat):

                @pl.when(back_ref[mask] == place)
                def _():
                    refs[n_feat + mask][...] = refs[place][...]

    shape = shares[0].shape
    return run(
        body, jnp.stack(back), shares, [whole(share) for share in shares],
        [like(shape, BF16)] * n_chip, [whole(shares[0])] * n_chip,
        after=after, moved=4 * n_chip * shape[0] * shape[1], limit=16,
    )


def assemble(place, own, other, after=()):
    n_chip = len(own)
    count, width = own[0].shape
    half = width // 2

    def body(place_ref, *refs):
        chip, core = place_ref[0], place_ref[1]
        out_ref = refs[-1]
        for mask in range(n_chip):
            for flip in range(2):
                piece_ref = refs[flip * n_chip + mask]
                row = pl.multiple_of(((chip ^ mask) * 2 + (core ^ flip)) * count, count)
                for side in range(2):
                    lane = pl.multiple_of((core ^ side) * half, half)
                    out_ref[pl.ds(row, count), side * half : (side + 1) * half] = piece_ref[
                        :, pl.ds(lane, half)
                    ]

    out = like((2 * n_chip * count, width), BF16)
    (columns,) = run(
        body, place, [*own, *other], [whole(piece) for piece in [*own, *other]],
        [out], [whole(out)], after=after, moved=8 * n_chip * count * width, limit=24,
    )
    return columns


def turn_columns(columns):
    batch, width = columns.shape
    depth = width // 2
    step = 256

    def body(_, columns_ref, out_ref):
        out_ref[...] = columns_ref[...].astype(F32).T.astype(BF16)

    (turned,) = run(
        body, jnp.zeros((1,), jnp.int32), [columns],
        [pl.BlockSpec((step, depth), lambda i, s: (i, 0))],
        [like((depth, batch), BF16)], [pl.BlockSpec((depth, step), lambda i, s: (0, i))],
        grid=(batch // step,), moved=4 * batch * depth, limit=8,
    )
    return turned


def forward(bits, turned_own, turned_other, columns, after=()):
    rows, depth = turned_own.shape
    batch = columns.shape[0]
    out_rows = rows // 4
    step = min(256, out_rows)
    steps = out_rows // step

    def body(bits_ref, own_a, other_a, own_b, other_b, columns_ref, out_a, out_b):
        for own_ref, other_ref, out_ref in ((own_a, other_a, out_a), (own_b, other_b, out_b)):
            block = lax.dot_general(
                own_ref[...], columns_ref[:, :depth], ROWS_BY_ROWS, preferred_element_type=F32
            )
            block += lax.dot_general(
                other_ref[...], columns_ref[:, depth:], ROWS_BY_ROWS, preferred_element_type=F32
            )
            out_ref[...] = (block - jnp.mean(block, 1, keepdims=True)).astype(BF16)

    def of_path(path):
        return pl.BlockSpec((step, depth), lambda i, b: ((2 * path + b[path]) * steps + i, 0))

    out_spec = pl.BlockSpec((step, batch), lambda i, b: (i, 0))
    return run(
        body, bits, [turned_own, turned_other, turned_own, turned_other, columns],
        [of_path(0), of_path(0), of_path(1), of_path(1), whole(columns)],
        [like((out_rows, batch), BF16)] * 2, [out_spec] * 2, grid=(steps,), after=after,
        flops=8 * out_rows * depth * batch, moved=8 * out_rows * depth + 4 * batch * depth,
    )


def add_halves(bits, kept, got, after=()):
    rows, batch = kept[0].shape
    half = rows // 2

    def body(bits_ref, kept_a, got_a, kept_b, got_b, send_a, send_b, keep_a, keep_b):
        for path, (kept_ref, got_ref, send_ref, keep_ref) in enumerate(
            ((kept_a, got_a, send_a, keep_a), (kept_b, got_b, send_b, keep_b))
        ):
            for flip, out_ref in ((1, send_ref), (0, keep_ref)):
                rows_of = pl.ds(pl.multiple_of((bits_ref[path] ^ flip) * half, half), half)
                total = kept_ref[rows_of, :].astype(F32) + got_ref[rows_of, :].astype(F32)
                out_ref[...] = total.astype(BF16)

    operands = [kept[0], got[0], kept[1], got[1]]
    out = like((half, batch), BF16)
    outs = run(
        body, bits, operands, [whole(one) for one in operands],
        [out] * 4, [whole(out)] * 4, after=after, moved=12 * rows * batch, limit=16,
    )
    return outs[:2], outs[2:]


def normalise(kept, got, after=()):
    rows, batch = kept[0].shape

    def body(_, kept_a, got_a, kept_b, got_b, normed_ref, half_ref, inverse_ref):
        for path, (kept_ref, got_ref) in enumerate(((kept_a, got_a), (kept_b, got_b))):
            total = kept_ref[...].astype(F32) + got_ref[...].astype(F32)
            total -= jnp.mean(total, 1, keepdims=True)
            inverse = lax.rsqrt(jnp.mean(total * total, 1, keepdims=True) + EPSILON)
            normed = total * inverse
            place = slice(path * rows, (path + 1) * rows)
            normed_ref[place, :] = normed
            half_ref[place, :] = normed.astype(BF16)
            inverse_ref[place, :] = jnp.broadcast_to(inverse, (rows, 128))

    operands = [kept[0], got[0], kept[1], got[1]]
    outs = [like((2 * rows, width), kind) for width, kind in ((batch, F32), (batch, BF16), (128, F32))]
    return run(
        body, jnp.zeros((1,), jnp.int32), operands, [whole(one) for one in operands],
        outs, [whole(out) for out in outs], after=after, moved=20 * rows * batch, limit=16,
    )


def gram_rows(place, own, other, n_chip, after=()):
    rows, batch = own.shape
    blocks = 2 * n_chip
    size = batch // blocks
    width = (blocks // 2 + 1) * size

    def body(place_ref, own_ref, other_ref, *refs):
        twice_ref = refs[-1]
        for start, ref in ((0, own_ref), (rows, other_ref)):
            twice_ref[start : start + rows, :batch] = ref[...]
            twice_ref[start : start + rows, batch:] = ref[...]
        for mask in range(n_chip):
            row = pl.multiple_of(((place_ref[0] ^ mask) * 2 + place_ref[1]) * size, size)
            left = twice_ref[:, pl.ds(row, size)].astype(F32).T.astype(BF16)
            right = twice_ref[:, pl.ds(row, width)]
            refs[mask][...] = jnp.dot(left, right, preferred_element_type=F32).astype(BF16)

    out = like((size, width), BF16)
    return run(
        body, place, [own, other], [whole(own), whole(other)],
        [out] * n_chip, [whole(out)] * n_chip,
        scratch=[pltpu.VMEM((2 * rows, 2 * batch), BF16)], after=after,
        flops=4 * rows * width * batch // 2, moved=8 * rows * batch, limit=24,
    )


def out_grad_of(place, gram_own, gram_other, normed, half, half_other, inverse, after=()):
    rows, batch = half.shape
    n_chip = gram_own.shape[0]
    blocks = 2 * n_chip
    size = batch // blocks

    def body(place_ref, own_ref, other_ref, normed_ref, half_ref, half_other_ref, inverse_ref,
             out_ref, gram_ref):
        for flip, ref in ((0, own_ref), (1, other_ref)):
            for mask in range(n_chip):
                row = (place_ref[0] ^ mask) * 2 + (place_ref[1] ^ flip)
                down = pl.ds(pl.multiple_of(row * size, size), size)
                for ahead in range(blocks // 2 + 1):
                    col = lax.rem(row + ahead, blocks)
                    along = pl.ds(pl.multiple_of(col * size, size), size)
                    tile = ref[mask, :, ahead * size : (ahead + 1) * size]
                    gram_ref[down, along] = tile
                    if 0 < ahead < blocks // 2:
                        gram_ref[along, down] = tile.astype(F32).T.astype(BF16)
        normed = normed_ref[...]
        other = half_other_ref[...].astype(F32)
        diagonal = jnp.mean(half_ref[...].astype(F32) * other, 1, keepdims=True)
        extra = (-2.0 * (1.0 - diagonal) - 2.0 * REDUNDANCY * diagonal) / batch
        grads = lax.dot_general(
            half_ref[...], gram_ref[...], ROWS_BY_ROWS, preferred_element_type=F32
        )
        grads = grads * (2.0 * REDUNDANCY / (batch * batch)) + extra * other
        grad_mean = jnp.mean(grads, 1, keepdims=True)
        grad_cross = jnp.mean(grads * normed, 1, keepdims=True)
        out_ref[...] = (
            inverse_ref[:, :1] * (grads - grad_mean - normed * grad_cross)
        ).astype(BF16)

    operands = [gram_own, gram_other, normed, half, half_other, inverse]
    out = like((rows, batch), BF16)
    (out_grad,) = run(
        body, place, operands, [whole(one) for one in operands], [out], [whole(out)],
        scratch=[pltpu.VMEM((batch, batch), BF16)], after=after,
        flops=2 * rows * batch * batch, moved=12 * rows * batch + 2 * batch * batch, limit=24,
    )
    return out_grad


def weight_grad_of(place, turned, pieces, base=None, after=()):
    depth, batch = turned.shape
    cols = pieces[0].shape[0]
    last = base is not None

    def body(place_ref, turned_ref, *refs):
        if last:
            base_ref, out_ref, square_ref = refs[4:]
        else:
            (out_ref,) = refs[4:]
        for index in range(4):

            @pl.when(pl.program_id(0) == index)
            def _():
                total = lax.dot_general(
                    turned_ref[...], refs[index][...], ROWS_BY_ROWS, preferred_element_type=F32
                )
                if last:
                    total += base_ref[...]
                    square = fold(total * total)
                    square_ref[...] = square if index == 0 else square_ref[...] + square
                out_ref[...] = total

    tile = pl.BlockSpec((depth, cols), lambda j, s: (0, (j >> 1) * 2 + ((j & 1) ^ s[1])))
    square = pl.BlockSpec((8, 128), lambda j, s: (0, 0))
    operands = [turned, *pieces]
    return run(
        body, place, operands + ([base] if last else []),
        [whole(one) for one in operands] + ([tile] if last else []),
        [like((depth, 4 * cols), F32)] + ([like((8, 128), F32)] if last else []),
        [tile] + ([square] if last else []), grid=(4,), after=after,
        flops=8 * cols * batch * depth, moved=16 * depth * cols * (2 if last else 1), limit=32,
    )


def per_device(view_features, weight, velocity):
    n_dp, n_feat = lax.axis_size("dp"), lax.axis_size("feat")
    n_chip = n_dp // 2
    assert n_chip == n_feat and view_features.shape[2] == 2 * weight.shape[0]
    high = list(range(1, n_dp.bit_length() - 1))
    orders = (high, high[::-1])
    chip, core = lax.axis_index("dp") >> 1, bit_value("dp", 0)
    place = jnp.stack([chip, core])

    def bits_at(level):
        return jnp.stack([bit_value("dp", order[level]) for order in orders])

    shares = [None] * 2
    shares[1] = go_round(share_of(view_features, 1))
    shares[0] = go_round(share_of(view_features, 0, after=[shares[1][-2]]))
    sent, sent_squares = turn_weight(weight, 1 - core)
    turned_other = swap(sent, "dp", 1)
    turned_own, own_squares = turn_weight(weight, core)
    weight_squares = sent_squares + own_squares

    turned, gram, normed, half, inverse = ([None] * 2 for _ in range(5))
    ahead = ()
    for v in (1, 0):
        own = list(choose(shares[v], n_chip, after=ahead[:1]))
        for mask in range(1, n_chip):
            own[mask] = swap(own[mask], "dp", 2 * mask)
        other = [swap(piece, "dp", 1) for piece in own]
        columns = assemble(place, own, other, after=ahead)
        turned[v] = turn_columns(columns)
        bits = bits_at(0)
        send = forward(1 - bits, turned_own, turned_other, columns)
        ahead = [send[0]]
        got = [swap(send[p], "dp", 1 << orders[p][0]) for p in range(2)]
        keep = forward(bits, turned_own, turned_other, columns)
        for level in range(1, len(high)):
            send, keep = add_halves(bits_at(level), keep, got)
            got = [swap(send[p], "dp", 1 << orders[p][level]) for p in range(2)]
        normed[v], half[v], inverse[v] = normalise(keep, got)
        rows = list(gram_rows(place, half[v], swap(half[v], "dp", 1), n_chip))
        ahead.append(rows[0])
        total = rows[0].astype(F32)
        for mask in range(1, n_chip):
            total += swap(rows[mask], "dp", 2 * mask).astype(F32)
        total = total.astype(BF16)
        for bit in range(n_feat.bit_length() - 1):
            total = (total.astype(F32) + swap(total, "feat", 1 << bit).astype(F32)).astype(BF16)
        gram_own = jnp.stack(
            [total] + [swap(total, "dp", 2 * mask) for mask in range(1, n_chip)]
        )
        gram[v] = (gram_own, swap(gram_own, "dp", 1))

    result = []
    for v in (0, 1):
        out_grad = out_grad_of(place, *gram[1 - v], normed[v], half[v], half[1 - v], inverse[v])
        share = out_grad.shape[0] // 2
        pieces = []
        for path in range(2):
            own = out_grad[path * share : (path + 1) * share]
            for bit in reversed(orders[path]):
                own = join(own, swap(own, "dp", 1 << bit), bit_value("dp", bit))
            pieces += [own, swap(own, "dp", 1)]
        result = weight_grad_of(place, turned[v], pieces, *result)
    weight_grad, squares = result
    sums = sum_everywhere(jnp.stack([jnp.sum(weight_squares), jnp.sum(squares)]))
    trust = jnp.sqrt(sums[0]) / (jnp.sqrt(sums[1]) + NORM_EPSILON)
    new_velocity = MOMENTUM * velocity + trust * weight_grad
    new_weight = weight - LEARN_RATE * new_velocity
    return (new_weight, new_velocity)


def solution(mesh):
    in_specs = (P(None, "dp", "feat"), P("dp", "feat"), P("dp", "feat"))
    out_specs = (P("dp", "feat"), P("dp", "feat"))
    return jax.shard_map(
        per_device, mesh=mesh, in_specs=in_specs, out_specs=out_specs, check_vma=False
    )
```

```python
import jax
import jax.numpy as jnp
from jax import lax
from jax.experimental import pallas as pl
from jax.experimental.pallas import tpu as pltpu
from jax.sharding import PartitionSpec as P

EPSILON = 1e-05
NORM_EPSILON = 1e-06
REDUNDANCY = 0.0051
MOMENTUM = 0.9
LEARN_RATE = 0.2
ROWS_BY_ROWS = (((1,), (1,)), ((), ()))
MIB = 1024 * 1024
F32, BF16 = jnp.float32, jnp.bfloat16


def swap(value, axis, mask):
    return lax.ppermute(value, axis, [(i, i ^ mask) for i in range(lax.axis_size(axis))])


def bit_value(axis, bit):
    return (lax.axis_index(axis) >> bit) & 1


def join(mine, other, bit):
    return jnp.where(
        bit == 0, jnp.concatenate([mine, other], 0), jnp.concatenate([other, mine], 0)
    )


def sum_everywhere(value):
    axes = ("dp", "feat")
    count = lax.axis_size(axes)
    parts = [value]
    for low in range(0, count.bit_length() - 1, 2):
        masks = [mask << low for mask in range(1, 4) if mask << low < count]
        value = sum(parts[1:], parts[0])
        parts = [value] + [
            lax.ppermute(value, axes, [(i, i ^ mask) for i in range(count)]) for mask in masks
        ]
    return parts


def whole(array):
    zeros = (0,) * array.ndim
    return pl.BlockSpec(array.shape, lambda *_: zeros, pipeline_mode=pl.Buffered(1))


def like(shape, kind):
    return jax.ShapeDtypeStruct(shape, kind)


def run(body, scalars, operands, in_specs, outs, out_specs, grid=(1,), scratch=(), after=(),
        flops=0, moved=0, limit=32):
    n_in, n_after = len(operands), len(after)

    def kernel(scalars_ref, *refs):
        body(scalars_ref, *refs[:n_in], *refs[n_in + n_after :])

    return pl.pallas_call(
        kernel,
        grid_spec=pltpu.PrefetchScalarGridSpec(
            num_scalar_prefetch=1,
            grid=grid,
            in_specs=list(in_specs) + [pl.BlockSpec(memory_space=pl.ANY)] * n_after,
            out_specs=list(out_specs),
            scratch_shapes=list(scratch),
        ),
        out_shape=list(outs),
        compiler_params=pltpu.CompilerParams(vmem_limit_bytes=limit * MIB),
        cost_estimate=pl.CostEstimate(flops=flops, bytes_accessed=moved, transcendentals=0),
    )(scalars, *operands, *after)


def fold(square):
    part = jnp.sum(square.reshape(-1, 8, square.shape[1]), 0)
    return sum(part[:, start : start + 128] for start in range(0, part.shape[1], 128))


def turn_weight(weight, core, after=()):
    depth, width = weight.shape
    quarter = width // 4
    step = min(256, quarter)
    steps = quarter // step

    def body(core_ref, weight_ref, sent_ref, kept_ref, square_ref):
        block = weight_ref[...]
        block_turned = block.T.astype(BF16)
        square = fold(block * block)
        first = (pl.program_id(0) == 0) & (pl.program_id(1) == 0)

        @pl.when(pl.program_id(0) == 0)
        def _():
            sent_ref[...] = block_turned

        @pl.when(pl.program_id(0) == 1)
        def _():
            kept_ref[...] = block_turned

        @pl.when(first)
        def _():
            square_ref[...] = square

        @pl.when(jnp.logical_not(first))
        def _():
            square_ref[...] += square

    out = like((2 * quarter, depth), BF16)
    return run(
        body, core.reshape(1), [weight],
        [
            pl.BlockSpec(
                (depth, step),
                lambda k, j, c: (0, (2 * (j // steps) + (c[0] ^ (1 - k))) * steps + j % steps),
            )
        ],
        [out, out, like((8, 128), F32)],
        [
            pl.BlockSpec((step, depth), lambda k, j, c: (jnp.where(k == 0, j, 2 * steps - 1), 0)),
            pl.BlockSpec((step, depth), lambda k, j, c: (jnp.where(k == 1, j, 0), 0)),
            pl.BlockSpec((8, 128), lambda k, j, c: (0, 0)),
        ],
        grid=(2, 2 * steps), after=after, flops=2 * depth * width, moved=6 * depth * width, limit=16,
    )


def shares_of(view_features, view, after=()):
    _, count, width = view_features.shape
    half = count // 2

    def body(_, rows_ref, low_ref, high_ref):
        low_ref[...] = rows_ref[:half, :]
        high_ref[...] = rows_ref[half:, :]

    out = like((half, width), BF16)
    return run(
        body, jnp.zeros((1,), jnp.int32), [view_features],
        [pl.BlockSpec((None, count, width), lambda i, s: (view, 0, 0))],
        [out, out], [whole(out), whole(out)], after=after, moved=4 * count * width, limit=8,
    )


def go_round(parts):
    n_feat = lax.axis_size("feat")
    ring = [(i, (i + 1) % n_feat) for i in range(n_feat)]
    lists = [[part] for part in parts]
    for _ in range(1, n_feat):
        for shares in lists:
            shares.append(lax.ppermute(shares[-1], "feat", ring))
    return lists


def choose(shares, n_chip, after=()):
    n_feat = len(shares)
    chip = lax.axis_index("dp") >> 1
    back = [lax.rem(lax.axis_index("feat") - (chip ^ mask) + n_feat, n_feat) for mask in range(n_chip)]

    def body(back_ref, *refs):
        for mask in range(n_chip):
            for place in range(n_feat):

                @pl.when(back_ref[mask] == place)
                def _():
                    refs[n_feat + mask][...] = refs[place][...]

    shape = shares[0].shape
    return run(
        body, jnp.stack(back), shares, [whole(share) for share in shares],
        [like(shape, BF16)] * n_chip, [whole(shares[0])] * n_chip,
        after=after, moved=4 * n_chip * shape[0] * shape[1], limit=16,
    )


def assemble(place, own, other, after=()):
    n_part, n_chip = len(own), len(own[0])
    count, width = own[0][0].shape
    half = width // 2
    operands = [piece for pieces in (*own, *other) for piece in pieces]

    def body(place_ref, *refs):
        chip, core = place_ref[0], place_ref[1]
        out_ref = refs[-1]
        for flip in range(2):
            for part in range(n_part):
                for mask in range(n_chip):
                    piece_ref = refs[(flip * n_part + part) * n_chip + mask]
                    row = (((chip ^ mask) * 2 + (core ^ flip)) * n_part + part) * count
                    rows = pl.ds(pl.multiple_of(row, count), count)
                    for side in range(2):
                        lane = pl.multiple_of((core ^ side) * half, half)
                        out_ref[rows, side * half : (side + 1) * half] = piece_ref[
                            :, pl.ds(lane, half)
                        ]

    out = like((len(operands) * count, width), BF16)
    (columns,) = run(
        body, place, operands, [whole(piece) for piece in operands],
        [out], [whole(out)], after=after, moved=4 * len(operands) * count * width, limit=24,
    )
    return columns


def turn_columns(columns):
    batch, width = columns.shape
    depth = width // 2
    step = 256

    def body(_, columns_ref, out_ref):
        out_ref[...] = columns_ref[...].astype(F32).T.astype(BF16)

    (turned,) = run(
        body, jnp.zeros((1,), jnp.int32), [columns],
        [pl.BlockSpec((step, depth), lambda i, s: (i, 0))],
        [like((depth, batch), BF16)], [pl.BlockSpec((depth, step), lambda i, s: (0, i))],
        grid=(batch // step,), moved=4 * batch * depth, limit=8,
    )
    return turned


def forward(bits, turned_own, turned_other, columns, after=()):
    rows, depth = turned_own.shape
    batch = columns.shape[0]
    out_rows = rows // 4
    step = min(256, out_rows)
    steps = out_rows // step

    def body(bits_ref, own_a, other_a, own_b, other_b, columns_ref, out_a, out_b):
        for own_ref, other_ref, out_ref in ((own_a, other_a, out_a), (own_b, other_b, out_b)):
            block = lax.dot_general(
                own_ref[...], columns_ref[:, :depth], ROWS_BY_ROWS, preferred_element_type=F32
            )
            block += lax.dot_general(
                other_ref[...], columns_ref[:, depth:], ROWS_BY_ROWS, preferred_element_type=F32
            )
            out_ref[...] = (block - jnp.mean(block, 1, keepdims=True)).astype(BF16)

    def of_path(path):
        return pl.BlockSpec((step, depth), lambda i, b: ((2 * path + b[path]) * steps + i, 0))

    out_spec = pl.BlockSpec((step, batch), lambda i, b: (i, 0))
    return run(
        body, bits, [turned_own, turned_other, turned_own, turned_other, columns],
        [of_path(0), of_path(0), of_path(1), of_path(1), whole(columns)],
        [like((out_rows, batch), BF16)] * 2, [out_spec] * 2, grid=(steps,), after=after,
        flops=8 * out_rows * depth * batch, moved=8 * out_rows * depth + 4 * batch * depth,
    )


def add_halves(bits, kept, got, after=()):
    rows, batch = kept[0].shape
    half = rows // 2

    def body(bits_ref, kept_a, got_a, kept_b, got_b, send_a, send_b, keep_a, keep_b):
        for path, (kept_ref, got_ref, send_ref, keep_ref) in enumerate(
            ((kept_a, got_a, send_a, keep_a), (kept_b, got_b, send_b, keep_b))
        ):
            for flip, out_ref in ((1, send_ref), (0, keep_ref)):
                rows_of = pl.ds(pl.multiple_of((bits_ref[path] ^ flip) * half, half), half)
                total = kept_ref[rows_of, :].astype(F32) + got_ref[rows_of, :].astype(F32)
                out_ref[...] = total.astype(BF16)

    operands = [kept[0], got[0], kept[1], got[1]]
    out = like((half, batch), BF16)
    outs = run(
        body, bits, operands, [whole(one) for one in operands],
        [out] * 4, [whole(out)] * 4, after=after, moved=12 * rows * batch, limit=16,
    )
    return outs[:2], outs[2:]


def normalise(kept, got, after=()):
    rows, batch = kept[0].shape

    def body(_, kept_a, got_a, kept_b, got_b, normed_ref, half_ref, inverse_ref):
        for path, (kept_ref, got_ref) in enumerate(((kept_a, got_a), (kept_b, got_b))):
            total = kept_ref[...].astype(F32) + got_ref[...].astype(F32)
            total -= jnp.mean(total, 1, keepdims=True)
            inverse = lax.rsqrt(jnp.mean(total * total, 1, keepdims=True) + EPSILON)
            normed = total * inverse
            place = slice(path * rows, (path + 1) * rows)
            normed_ref[place, :] = normed
            half_ref[place, :] = normed.astype(BF16)
            inverse_ref[place, :] = jnp.broadcast_to(inverse, (rows, 128))

    operands = [kept[0], got[0], kept[1], got[1]]
    outs = [like((2 * rows, width), kind) for width, kind in ((batch, F32), (batch, BF16), (128, F32))]
    return run(
        body, jnp.zeros((1,), jnp.int32), operands, [whole(one) for one in operands],
        outs, [whole(out) for out in outs], after=after, moved=20 * rows * batch, limit=16,
    )


def gram_rows(place, own, other, n_chip, after=()):
    rows, batch = own.shape
    blocks = 2 * n_chip
    size = batch // blocks
    width = (blocks // 2 + 1) * size

    def body(place_ref, own_ref, other_ref, *refs):
        twice_ref = refs[-1]
        for start, ref in ((0, own_ref), (rows, other_ref)):
            twice_ref[start : start + rows, :batch] = ref[...]
            twice_ref[start : start + rows, batch:] = ref[...]
        for mask in range(n_chip):
            row = pl.multiple_of(((place_ref[0] ^ mask) * 2 + place_ref[1]) * size, size)
            left = twice_ref[:, pl.ds(row, size)].astype(F32).T.astype(BF16)
            right = twice_ref[:, pl.ds(row, width)]
            refs[mask][...] = jnp.dot(left, right, preferred_element_type=F32).astype(BF16)

    out = like((size, width), BF16)
    return run(
        body, place, [own, other], [whole(own), whole(other)],
        [out] * n_chip, [whole(out)] * n_chip,
        scratch=[pltpu.VMEM((2 * rows, 2 * batch), BF16)], after=after,
        flops=4 * rows * width * batch // 2, moved=8 * rows * batch, limit=24,
    )


def out_grad_of(place, gram_own, gram_other, normed, half, half_other, inverse, after=()):
    rows, batch = half.shape
    n_chip = gram_own.shape[0]
    blocks = 2 * n_chip
    size = batch // blocks

    def body(place_ref, own_ref, other_ref, normed_ref, half_ref, half_other_ref, inverse_ref,
             out_ref, gram_ref):
        for flip, ref in ((0, own_ref), (1, other_ref)):
            for mask in range(n_chip):
                row = (place_ref[0] ^ mask) * 2 + (place_ref[1] ^ flip)
                down = pl.ds(pl.multiple_of(row * size, size), size)
                for ahead in range(blocks // 2 + 1):
                    col = lax.rem(row + ahead, blocks)
                    along = pl.ds(pl.multiple_of(col * size, size), size)
                    tile = ref[mask, :, ahead * size : (ahead + 1) * size]
                    gram_ref[down, along] = tile
                    if 0 < ahead < blocks // 2:
                        gram_ref[along, down] = tile.astype(F32).T.astype(BF16)
        normed = normed_ref[...]
        other = half_other_ref[...].astype(F32)
        diagonal = jnp.mean(half_ref[...].astype(F32) * other, 1, keepdims=True)
        extra = (-2.0 * (1.0 - diagonal) - 2.0 * REDUNDANCY * diagonal) / batch
        grads = lax.dot_general(
            half_ref[...], gram_ref[...], ROWS_BY_ROWS, preferred_element_type=F32
        )
        grads = grads * (2.0 * REDUNDANCY / (batch * batch)) + extra * other
        grad_mean = jnp.mean(grads, 1, keepdims=True)
        grad_cross = jnp.mean(grads * normed, 1, keepdims=True)
        out_ref[...] = (
            inverse_ref[:, :1] * (grads - grad_mean - normed * grad_cross)
        ).astype(BF16)

    operands = [gram_own, gram_other, normed, half, half_other, inverse]
    out = like((rows, batch), BF16)
    (out_grad,) = run(
        body, place, operands, [whole(one) for one in operands], [out], [whole(out)],
        scratch=[pltpu.VMEM((batch, batch), BF16)], after=after,
        flops=2 * rows * batch * batch, moved=12 * rows * batch + 2 * batch * batch, limit=24,
    )
    return out_grad


def weight_grad_of(place, turned, pieces, base=None, weight_squares=None, after=()):
    depth, batch = turned.shape
    cols = pieces[0].shape[0]
    last = base is not None

    def body(place_ref, turned_ref, *refs):
        if last:
            base_ref, weight_squares_ref, out_ref, square_ref = refs[4:]
        else:
            (out_ref,) = refs[4:]
        for index in range(4):

            @pl.when(pl.program_id(0) == index)
            def _():
                total = lax.dot_general(
                    turned_ref[...], refs[index][...], ROWS_BY_ROWS, preferred_element_type=F32
                )
                if last:
                    total += base_ref[...]
                    square = fold(total * total)
                    if index == 0:
                        square_ref[:8, :] = square
                        square_ref[8:, :] = weight_squares_ref[...]
                    else:
                        square_ref[:8, :] += square
                out_ref[...] = total

    tile = pl.BlockSpec((depth, cols), lambda j, s: (0, (j >> 1) * 2 + ((j & 1) ^ s[1])))
    square = pl.BlockSpec((16, 128), lambda j, s: (0, 0))
    operands = [turned, *pieces]
    return run(
        body, place, operands + ([base, weight_squares] if last else []),
        [whole(one) for one in operands] + ([tile, whole(weight_squares)] if last else []),
        [like((depth, 4 * cols), F32)] + ([like((16, 128), F32)] if last else []),
        [tile] + ([square] if last else []), grid=(4,), after=after,
        flops=8 * cols * batch * depth, moved=16 * depth * cols * (2 if last else 1), limit=32,
    )


def update(sums, weight, velocity, weight_grad):
    depth, width = weight.shape
    step = min(128, depth)
    n_sum = len(sums)

    def body(_, *refs):
        weight_ref, velocity_ref, grad_ref, new_weight_ref, new_velocity_ref = refs[n_sum:]
        total = refs[0][...]
        for ref in refs[1:n_sum]:
            total += ref[...]
        grad_norm = jnp.sqrt(jnp.sum(total[:8], keepdims=True))
        weight_norm = jnp.sqrt(jnp.sum(total[8:], keepdims=True))
        trust = weight_norm / (grad_norm + NORM_EPSILON)
        new_velocity = MOMENTUM * velocity_ref[...] + trust * grad_ref[...]
        new_velocity_ref[...] = new_velocity
        new_weight_ref[...] = weight_ref[...] - LEARN_RATE * new_velocity

    tile = pl.BlockSpec((step, width), lambda i, s: (i, 0))
    out = like((depth, width), F32)
    return run(
        body, jnp.zeros((1,), jnp.int32), [*sums, weight, velocity, weight_grad],
        [whole(one) for one in sums] + [tile] * 3, [out, out], [tile, tile],
        grid=(depth // step,), flops=4 * depth * width, moved=20 * depth * width, limit=16,
    )


def per_device(view_features, weight, velocity):
    n_dp, n_feat = lax.axis_size("dp"), lax.axis_size("feat")
    n_chip = n_dp // 2
    assert n_chip == n_feat and view_features.shape[2] == 2 * weight.shape[0]
    high = list(range(1, n_dp.bit_length() - 1))
    orders = (high, high[::-1])
    chip, core = lax.axis_index("dp") >> 1, bit_value("dp", 0)
    place = jnp.stack([chip, core])

    def bits_at(level):
        return jnp.stack([bit_value("dp", order[level]) for order in orders])

    shares = [None] * 2
    shares[1] = go_round(shares_of(view_features, 1))
    sent, turned_own, weight_squares = turn_weight(weight, core, after=[shares[1][-1][-2]])
    turned_other = swap(sent, "dp", 1)
    shares[0] = go_round(shares_of(view_features, 0, after=[turned_own]))

    turned, gram, normed, half, inverse = ([None] * 2 for _ in range(5))
    ahead = ()
    for v in (1, 0):
        own = [list(choose(part, n_chip, after=ahead[:1])) for part in shares[v]]
        for pieces in own:
            for mask in range(1, n_chip):
                pieces[mask] = swap(pieces[mask], "dp", 2 * mask)
        other = [[swap(piece, "dp", 1) for piece in pieces] for pieces in own]
        columns = assemble(place, own, other, after=ahead)
        turned[v] = turn_columns(columns)
        bits = bits_at(0)
        send = forward(1 - bits, turned_own, turned_other, columns)
        ahead = [send[0]]
        got = [swap(send[p], "dp", 1 << orders[p][0]) for p in range(2)]
        keep = forward(bits, turned_own, turned_other, columns)
        for level in range(1, len(high)):
            send, keep = add_halves(bits_at(level), keep, got)
            got = [swap(send[p], "dp", 1 << orders[p][level]) for p in range(2)]
        normed[v], half[v], inverse[v] = normalise(keep, got)
        rows = list(gram_rows(place, half[v], swap(half[v], "dp", 1), n_chip))
        ahead.append(rows[0])
        total = rows[0].astype(F32)
        for mask in range(1, n_chip):
            total += swap(rows[mask], "dp", 2 * mask).astype(F32)
        total = total.astype(BF16)
        for bit in range(n_feat.bit_length() - 1):
            total = (total.astype(F32) + swap(total, "feat", 1 << bit).astype(F32)).astype(BF16)
        gram_own = jnp.stack(
            [total] + [swap(total, "dp", 2 * mask) for mask in range(1, n_chip)]
        )
        gram[v] = (gram_own, swap(gram_own, "dp", 1))

    for v in (0, 1):
        out_grad = out_grad_of(place, *gram[1 - v], normed[v], half[v], half[1 - v], inverse[v])
        share = out_grad.shape[0] // 2
        pieces = []
        for path in range(2):
            own = out_grad[path * share : (path + 1) * share]
            for bit in reversed(orders[path]):
                own = join(own, swap(own, "dp", 1 << bit), bit_value("dp", bit))
            pieces += [own, swap(own, "dp", 1)]
        if v == 0:
            (base,) = weight_grad_of(place, turned[v], pieces)
    weight_grad, squares = weight_grad_of(place, turned[1], pieces, base, weight_squares)
    return update(sum_everywhere(squares), weight, velocity, weight_grad)


def solution(mesh):
    in_specs = (P(None, "dp", "feat"), P("dp", "feat"), P("dp", "feat"))
    out_specs = (P("dp", "feat"), P("dp", "feat"))
    return jax.shard_map(
        per_device, mesh=mesh, in_specs=in_specs, out_specs=out_specs, check_vma=False
    )
```

```python
import jax
import jax.numpy as jnp
from jax import lax
from jax.experimental import pallas as pl
from jax.experimental.pallas import tpu as pltpu
from jax.sharding import PartitionSpec as P

EPSILON = 1e-05
NORM_EPSILON = 1e-06
REDUNDANCY = 0.0051
MOMENTUM = 0.9
LEARN_RATE = 0.2
ROWS_BY_ROWS = (((1,), (1,)), ((), ()))
MIB = 1024 * 1024
F32, BF16 = jnp.float32, jnp.bfloat16


def swap(value, axis, mask):
    return lax.ppermute(value, axis, [(i, i ^ mask) for i in range(lax.axis_size(axis))])


def bit_value(axis, bit):
    return (lax.axis_index(axis) >> bit) & 1


def join(mine, other, bit):
    return jnp.where(
        bit == 0, jnp.concatenate([mine, other], 0), jnp.concatenate([other, mine], 0)
    )


def sum_everywhere(value):
    axes = ("dp", "feat")
    count = lax.axis_size(axes)
    parts = [value]
    for low in range(0, count.bit_length() - 1, 2):
        masks = [mask << low for mask in range(1, 4) if mask << low < count]
        value = sum(parts[1:], parts[0])
        parts = [value] + [
            lax.ppermute(value, axes, [(i, i ^ mask) for i in range(count)]) for mask in masks
        ]
    return parts


def whole(array):
    zeros = (0,) * array.ndim
    return pl.BlockSpec(array.shape, lambda *_: zeros, pipeline_mode=pl.Buffered(1))


def like(shape, kind):
    return jax.ShapeDtypeStruct(shape, kind)


def run(body, scalars, operands, in_specs, outs, out_specs, grid=(1,), scratch=(), after=(),
        flops=0, moved=0, limit=32):
    n_in, n_after = len(operands), len(after)

    def kernel(scalars_ref, *refs):
        body(scalars_ref, *refs[:n_in], *refs[n_in + n_after :])

    return pl.pallas_call(
        kernel,
        grid_spec=pltpu.PrefetchScalarGridSpec(
            num_scalar_prefetch=1,
            grid=grid,
            in_specs=list(in_specs) + [pl.BlockSpec(memory_space=pl.ANY)] * n_after,
            out_specs=list(out_specs),
            scratch_shapes=list(scratch),
        ),
        out_shape=list(outs),
        compiler_params=pltpu.CompilerParams(vmem_limit_bytes=limit * MIB),
        cost_estimate=pl.CostEstimate(flops=flops, bytes_accessed=moved, transcendentals=0),
    )(scalars, *operands, *after)


def fold(square):
    part = jnp.sum(square.reshape(-1, 8, square.shape[1]), 0)
    return sum(part[:, start : start + 128] for start in range(0, part.shape[1], 128))


def turn_weight(weight, core, after=()):
    depth, width = weight.shape
    quarter = width // 4
    step = min(256, quarter)
    steps = quarter // step

    def body(core_ref, weight_ref, sent_ref, kept_ref, square_ref):
        block = weight_ref[...]
        block_turned = block.T.astype(BF16)
        square = fold(block * block)
        first = (pl.program_id(0) == 0) & (pl.program_id(1) == 0)

        @pl.when(pl.program_id(0) == 0)
        def _():
            sent_ref[...] = block_turned

        @pl.when(pl.program_id(0) == 1)
        def _():
            kept_ref[...] = block_turned

        @pl.when(first)
        def _():
            square_ref[...] = square

        @pl.when(jnp.logical_not(first))
        def _():
            square_ref[...] += square

    out = like((2 * quarter, depth), BF16)
    return run(
        body, core.reshape(1), [weight],
        [
            pl.BlockSpec(
                (depth, step),
                lambda k, j, c: (0, (2 * (j // steps) + (c[0] ^ (1 - k))) * steps + j % steps),
            )
        ],
        [out, out, like((8, 128), F32)],
        [
            pl.BlockSpec((step, depth), lambda k, j, c: (jnp.where(k == 0, j, 2 * steps - 1), 0)),
            pl.BlockSpec((step, depth), lambda k, j, c: (jnp.where(k == 1, j, 0), 0)),
            pl.BlockSpec((8, 128), lambda k, j, c: (0, 0)),
        ],
        grid=(2, 2 * steps), after=after, flops=2 * depth * width, moved=6 * depth * width, limit=16,
    )


def share_of(view_features, view):
    _, count, width = view_features.shape

    def body(_, rows_ref, out_ref):
        out_ref[...] = rows_ref[...]

    out = like((count, width), BF16)
    return run(
        body, jnp.zeros((1,), jnp.int32), [view_features],
        [pl.BlockSpec((None, count, width), lambda i, s: (view, 0, 0))],
        [out], [whole(out)], moved=4 * count * width, limit=8,
    )


def go_round(parts):
    n_feat = lax.axis_size("feat")
    ring = [(i, (i + 1) % n_feat) for i in range(n_feat)]
    lists = [[part] for part in parts]
    for _ in range(1, n_feat):
        for shares in lists:
            shares.append(lax.ppermute(shares[-1], "feat", ring))
    return lists


def choose(shares, n_chip, after=()):
    n_feat = len(shares)
    chip = lax.axis_index("dp") >> 1
    back = [lax.rem(lax.axis_index("feat") - (chip ^ mask) + n_feat, n_feat) for mask in range(n_chip)]

    def body(back_ref, *refs):
        for mask in range(n_chip):
            for place in range(n_feat):

                @pl.when(back_ref[mask] == place)
                def _():
                    refs[n_feat + mask][...] = refs[place][...]

    shape = shares[0].shape
    return run(
        body, jnp.stack(back), shares, [whole(share) for share in shares],
        [like(shape, BF16)] * n_chip, [whole(shares[0])] * n_chip,
        after=after, moved=4 * n_chip * shape[0] * shape[1], limit=16,
    )


def assemble(place, own, other, after=()):
    n_part, n_chip = len(own), len(own[0])
    count, width = own[0][0].shape
    half = width // 2
    operands = [piece for pieces in (*own, *other) for piece in pieces]

    def body(place_ref, *refs):
        chip, core = place_ref[0], place_ref[1]
        out_ref = refs[-1]
        for flip in range(2):
            for part in range(n_part):
                for mask in range(n_chip):
                    piece_ref = refs[(flip * n_part + part) * n_chip + mask]
                    row = (((chip ^ mask) * 2 + (core ^ flip)) * n_part + part) * count
                    rows = pl.ds(pl.multiple_of(row, count), count)
                    for side in range(2):
                        lane = pl.multiple_of((core ^ side) * half, half)
                        out_ref[rows, side * half : (side + 1) * half] = piece_ref[
                            :, pl.ds(lane, half)
                        ]

    out = like((len(operands) * count, width), BF16)
    (columns,) = run(
        body, place, operands, [whole(piece) for piece in operands],
        [out], [whole(out)], after=after, moved=4 * len(operands) * count * width, limit=24,
    )
    return columns


def turn_columns(columns):
    batch, width = columns.shape
    depth = width // 2
    step = 256

    def body(_, columns_ref, out_ref):
        out_ref[...] = columns_ref[...].astype(F32).T.astype(BF16)

    (turned,) = run(
        body, jnp.zeros((1,), jnp.int32), [columns],
        [pl.BlockSpec((step, depth), lambda i, s: (i, 0))],
        [like((depth, batch), BF16)], [pl.BlockSpec((depth, step), lambda i, s: (0, i))],
        grid=(batch // step,), moved=4 * batch * depth, limit=8,
    )
    return turned


def forward(bits, turned_own, turned_other, columns, after=()):
    rows, depth = turned_own.shape
    batch = columns.shape[0]
    out_rows = rows // 4
    step = min(256, out_rows)
    steps = out_rows // step

    def body(bits_ref, own_a, other_a, own_b, other_b, columns_ref, out_a, out_b):
        for own_ref, other_ref, out_ref in ((own_a, other_a, out_a), (own_b, other_b, out_b)):
            block = lax.dot_general(
                own_ref[...], columns_ref[:, :depth], ROWS_BY_ROWS, preferred_element_type=F32
            )
            block += lax.dot_general(
                other_ref[...], columns_ref[:, depth:], ROWS_BY_ROWS, preferred_element_type=F32
            )
            out_ref[...] = (block - jnp.mean(block, 1, keepdims=True)).astype(BF16)

    def of_path(path):
        return pl.BlockSpec((step, depth), lambda i, b: ((2 * path + b[path]) * steps + i, 0))

    out_spec = pl.BlockSpec((step, batch), lambda i, b: (i, 0))
    return run(
        body, bits, [turned_own, turned_other, turned_own, turned_other, columns],
        [of_path(0), of_path(0), of_path(1), of_path(1), whole(columns)],
        [like((out_rows, batch), BF16)] * 2, [out_spec] * 2, grid=(steps,), after=after,
        flops=8 * out_rows * depth * batch, moved=8 * out_rows * depth + 4 * batch * depth,
    )


def add_halves(bits, kept, got, after=()):
    rows, batch = kept[0].shape
    half = rows // 2

    def body(bits_ref, kept_a, got_a, kept_b, got_b, send_a, send_b, keep_a, keep_b):
        for path, (kept_ref, got_ref, send_ref, keep_ref) in enumerate(
            ((kept_a, got_a, send_a, keep_a), (kept_b, got_b, send_b, keep_b))
        ):
            for flip, out_ref in ((1, send_ref), (0, keep_ref)):
                rows_of = pl.ds(pl.multiple_of((bits_ref[path] ^ flip) * half, half), half)
                total = kept_ref[rows_of, :].astype(F32) + got_ref[rows_of, :].astype(F32)
                out_ref[...] = total.astype(BF16)

    operands = [kept[0], got[0], kept[1], got[1]]
    out = like((half, batch), BF16)
    outs = run(
        body, bits, operands, [whole(one) for one in operands],
        [out] * 4, [whole(out)] * 4, after=after, moved=12 * rows * batch, limit=16,
    )
    return outs[:2], outs[2:]


def normalise(kept, got, after=()):
    rows, batch = kept[0].shape

    def body(_, kept_a, got_a, kept_b, got_b, normed_ref, half_ref, inverse_ref):
        for path, (kept_ref, got_ref) in enumerate(((kept_a, got_a), (kept_b, got_b))):
            total = kept_ref[...].astype(F32) + got_ref[...].astype(F32)
            total -= jnp.mean(total, 1, keepdims=True)
            inverse = lax.rsqrt(jnp.mean(total * total, 1, keepdims=True) + EPSILON)
            normed = total * inverse
            place = slice(path * rows, (path + 1) * rows)
            normed_ref[place, :] = normed
            half_ref[place, :] = normed.astype(BF16)
            inverse_ref[place, :] = jnp.broadcast_to(inverse, (rows, 128))

    operands = [kept[0], got[0], kept[1], got[1]]
    outs = [like((2 * rows, width), kind) for width, kind in ((batch, F32), (batch, BF16), (128, F32))]
    return run(
        body, jnp.zeros((1,), jnp.int32), operands, [whole(one) for one in operands],
        outs, [whole(out) for out in outs], after=after, moved=20 * rows * batch, limit=16,
    )


def gram_rows(place, own, other, n_chip, after=()):
    rows, batch = own.shape
    blocks = 2 * n_chip
    size = batch // blocks
    width = (blocks // 2 + 1) * size

    def body(place_ref, own_ref, other_ref, *refs):
        twice_ref = refs[-1]
        for start, ref in ((0, own_ref), (rows, other_ref)):
            twice_ref[start : start + rows, :batch] = ref[...]
            twice_ref[start : start + rows, batch:] = ref[...]
        for mask in range(n_chip):
            row = pl.multiple_of(((place_ref[0] ^ mask) * 2 + place_ref[1]) * size, size)
            left = twice_ref[:, pl.ds(row, size)].astype(F32).T.astype(BF16)
            right = twice_ref[:, pl.ds(row, width)]
            refs[mask][...] = jnp.dot(left, right, preferred_element_type=F32).astype(BF16)

    out = like((size, width), BF16)
    return run(
        body, place, [own, other], [whole(own), whole(other)],
        [out] * n_chip, [whole(out)] * n_chip,
        scratch=[pltpu.VMEM((2 * rows, 2 * batch), BF16)], after=after,
        flops=4 * rows * width * batch // 2, moved=8 * rows * batch, limit=24,
    )


def out_grad_of(place, gram_own, gram_other, normed, half, half_other, inverse, after=()):
    rows, batch = half.shape
    n_chip = gram_own.shape[0]
    blocks = 2 * n_chip
    size = batch // blocks

    def body(place_ref, own_ref, other_ref, normed_ref, half_ref, half_other_ref, inverse_ref,
             out_ref, gram_ref):
        for flip, ref in ((0, own_ref), (1, other_ref)):
            for mask in range(n_chip):
                row = (place_ref[0] ^ mask) * 2 + (place_ref[1] ^ flip)
                down = pl.ds(pl.multiple_of(row * size, size), size)
                for ahead in range(blocks // 2 + 1):
                    col = lax.rem(row + ahead, blocks)
                    along = pl.ds(pl.multiple_of(col * size, size), size)
                    tile = ref[mask, :, ahead * size : (ahead + 1) * size]
                    gram_ref[down, along] = tile
                    if 0 < ahead < blocks // 2:
                        gram_ref[along, down] = tile.astype(F32).T.astype(BF16)
        normed = normed_ref[...]
        other = half_other_ref[...].astype(F32)
        diagonal = jnp.mean(half_ref[...].astype(F32) * other, 1, keepdims=True)
        extra = (-2.0 * (1.0 - diagonal) - 2.0 * REDUNDANCY * diagonal) / batch
        grads = lax.dot_general(
            half_ref[...], gram_ref[...], ROWS_BY_ROWS, preferred_element_type=F32
        )
        grads = grads * (2.0 * REDUNDANCY / (batch * batch)) + extra * other
        grad_mean = jnp.mean(grads, 1, keepdims=True)
        grad_cross = jnp.mean(grads * normed, 1, keepdims=True)
        out_ref[...] = (
            inverse_ref[:, :1] * (grads - grad_mean - normed * grad_cross)
        ).astype(BF16)

    operands = [gram_own, gram_other, normed, half, half_other, inverse]
    out = like((rows, batch), BF16)
    (out_grad,) = run(
        body, place, operands, [whole(one) for one in operands], [out], [whole(out)],
        scratch=[pltpu.VMEM((batch, batch), BF16)], after=after,
        flops=2 * rows * batch * batch, moved=12 * rows * batch + 2 * batch * batch, limit=24,
    )
    return out_grad


def weight_grad_of(place, turned, pieces, base=None, weight_squares=None, after=()):
    depth, batch = turned.shape
    cols = pieces[0].shape[0]
    last = base is not None

    def body(place_ref, turned_ref, *refs):
        if last:
            base_ref, weight_squares_ref, out_ref, square_ref = refs[4:]
        else:
            (out_ref,) = refs[4:]
        for index in range(4):

            @pl.when(pl.program_id(0) == index)
            def _():
                total = lax.dot_general(
                    turned_ref[...], refs[index][...], ROWS_BY_ROWS, preferred_element_type=F32
                )
                if last:
                    total += base_ref[...]
                    square = fold(total * total)
                    if index == 0:
                        square_ref[:8, :] = square
                        square_ref[8:, :] = weight_squares_ref[...]
                    else:
                        square_ref[:8, :] += square
                out_ref[...] = total

    tile = pl.BlockSpec((depth, cols), lambda j, s: (0, (j >> 1) * 2 + ((j & 1) ^ s[1])))
    square = pl.BlockSpec((16, 128), lambda j, s: (0, 0))
    operands = [turned, *pieces]
    return run(
        body, place, operands + ([base, weight_squares] if last else []),
        [whole(one) for one in operands] + ([tile, whole(weight_squares)] if last else []),
        [like((depth, 4 * cols), F32)] + ([like((16, 128), F32)] if last else []),
        [tile] + ([square] if last else []), grid=(4,), after=after,
        flops=8 * cols * batch * depth, moved=16 * depth * cols * (2 if last else 1), limit=20,
    )


def update(sums, weight, velocity, weight_grad):
    depth, width = weight.shape
    step = min(128, depth)
    n_sum = len(sums)

    def body(_, *refs):
        weight_ref, velocity_ref, grad_ref, new_weight_ref, new_velocity_ref = refs[n_sum:]
        total = refs[0][...]
        for ref in refs[1:n_sum]:
            total += ref[...]
        grad_norm = jnp.sqrt(jnp.sum(total[:8], keepdims=True))
        weight_norm = jnp.sqrt(jnp.sum(total[8:], keepdims=True))
        trust = weight_norm / (grad_norm + NORM_EPSILON)
        new_velocity = MOMENTUM * velocity_ref[...] + trust * grad_ref[...]
        new_velocity_ref[...] = new_velocity
        new_weight_ref[...] = weight_ref[...] - LEARN_RATE * new_velocity

    tile = pl.BlockSpec((step, width), lambda i, s: (i, 0))
    out = like((depth, width), F32)
    return run(
        body, jnp.zeros((1,), jnp.int32), [*sums, weight, velocity, weight_grad],
        [whole(one) for one in sums] + [tile] * 3, [out, out], [tile, tile],
        grid=(depth // step,), flops=4 * depth * width, moved=20 * depth * width, limit=16,
    )


def per_device(view_features, weight, velocity):
    n_dp, n_feat = lax.axis_size("dp"), lax.axis_size("feat")
    n_chip = n_dp // 2
    assert n_chip == n_feat and view_features.shape[2] == 2 * weight.shape[0]
    high = list(range(1, n_dp.bit_length() - 1))
    orders = (high, high[::-1])
    chip, core = lax.axis_index("dp") >> 1, bit_value("dp", 0)
    place = jnp.stack([chip, core])

    def bits_at(level):
        return jnp.stack([bit_value("dp", order[level]) for order in orders])

    shares = [go_round(share_of(view_features, v)) for v in (0, 1)]
    sent, turned_own, weight_squares = turn_weight(weight, core)
    turned_other = swap(sent, "dp", 1)

    turned, gram, normed, half, inverse = ([None] * 2 for _ in range(5))
    ahead = ()
    for v in (1, 0):
        own = [list(choose(part, n_chip)) for part in shares[v]]
        for pieces in own:
            for mask in range(1, n_chip):
                pieces[mask] = swap(pieces[mask], "dp", 2 * mask)
        other = [[swap(piece, "dp", 1) for piece in pieces] for pieces in own]
        columns = assemble(place, own, other, after=ahead[:1])
        turned[v] = turn_columns(columns)
        bits = bits_at(0)
        send = forward(1 - bits, turned_own, turned_other, columns)
        got = [swap(send[p], "dp", 1 << orders[p][0]) for p in range(2)]
        keep = forward(bits, turned_own, turned_other, columns, after=[turned[v]])
        for level in range(1, len(high)):
            send, keep = add_halves(bits_at(level), keep, got, after=ahead[1:])
            ahead = [send[0]]
            got = [swap(send[p], "dp", 1 << orders[p][level]) for p in range(2)]
        normed[v], half[v], inverse[v] = normalise(keep, got)
        rows = list(gram_rows(place, half[v], swap(half[v], "dp", 1), n_chip))
        ahead.append(rows[0])
        total = rows[0].astype(F32)
        for mask in range(1, n_chip):
            total += swap(rows[mask], "dp", 2 * mask).astype(F32)
        total = total.astype(BF16)
        for bit in range(n_feat.bit_length() - 1):
            total = (total.astype(F32) + swap(total, "feat", 1 << bit).astype(F32)).astype(BF16)
        gram_own = jnp.stack(
            [total] + [swap(total, "dp", 2 * mask) for mask in range(1, n_chip)]
        )
        gram[v] = (gram_own, swap(gram_own, "dp", 1))

    for v in (0, 1):
        out_grad = out_grad_of(place, *gram[1 - v], normed[v], half[v], half[1 - v], inverse[v])
        share = out_grad.shape[0] // 2
        pieces = []
        for path in range(2):
            own = out_grad[path * share : (path + 1) * share]
            for bit in reversed(orders[path]):
                own = join(own, swap(own, "dp", 1 << bit), bit_value("dp", bit))
            pieces += [own, swap(own, "dp", 1)]
        if v == 0:
            (base,) = weight_grad_of(place, turned[v], pieces)
    weight_grad, squares = weight_grad_of(place, turned[1], pieces, base, weight_squares)
    return update(sum_everywhere(squares), weight, velocity, weight_grad)


def solution(mesh):
    in_specs = (P(None, "dp", "feat"), P("dp", "feat"), P("dp", "feat"))
    out_specs = (P("dp", "feat"), P("dp", "feat"))
    return jax.shard_map(
        per_device, mesh=mesh, in_specs=in_specs, out_specs=out_specs, check_vma=False
    )
```

```python
import jax
import jax.numpy as jnp
from jax import lax
from jax.experimental import pallas as pl
from jax.experimental.pallas import tpu as pltpu
from jax.sharding import PartitionSpec as P

EPSILON = 1e-05
NORM_EPSILON = 1e-06
REDUNDANCY = 0.0051
MOMENTUM = 0.9
LEARN_RATE = 0.2
ROWS_BY_ROWS = (((1,), (1,)), ((), ()))
MIB = 1024 * 1024
F32, BF16 = jnp.float32, jnp.bfloat16


def swap(value, axis, mask):
    return lax.ppermute(value, axis, [(i, i ^ mask) for i in range(lax.axis_size(axis))])


def bit_value(axis, bit):
    return (lax.axis_index(axis) >> bit) & 1


def join(mine, other, bit):
    return jnp.where(
        bit == 0, jnp.concatenate([mine, other], 0), jnp.concatenate([other, mine], 0)
    )


def sum_everywhere(value):
    axes = ("dp", "feat")
    count = lax.axis_size(axes)
    parts = [value]
    for low in range(0, count.bit_length() - 1, 2):
        masks = [mask << low for mask in range(1, 4) if mask << low < count]
        value = sum(parts[1:], parts[0])
        parts = [value] + [
            lax.ppermute(value, axes, [(i, i ^ mask) for i in range(count)]) for mask in masks
        ]
    return parts


def whole(array):
    zeros = (0,) * array.ndim
    return pl.BlockSpec(array.shape, lambda *_: zeros, pipeline_mode=pl.Buffered(1))


def like(shape, kind):
    return jax.ShapeDtypeStruct(shape, kind)


def run(body, scalars, operands, in_specs, outs, out_specs, grid=(1,), scratch=(), after=(),
        flops=0, moved=0, limit=32, name=None):
    n_in, n_after = len(operands), len(after)

    def kernel(scalars_ref, *refs):
        body(scalars_ref, *refs[:n_in], *refs[n_in + n_after :])

    return pl.pallas_call(
        kernel,
        grid_spec=pltpu.PrefetchScalarGridSpec(
            num_scalar_prefetch=1,
            grid=grid,
            in_specs=list(in_specs) + [pl.BlockSpec(memory_space=pl.ANY)] * n_after,
            out_specs=list(out_specs),
            scratch_shapes=list(scratch),
        ),
        out_shape=list(outs),
        compiler_params=pltpu.CompilerParams(vmem_limit_bytes=limit * MIB),
        cost_estimate=pl.CostEstimate(flops=flops, bytes_accessed=moved, transcendentals=0),
        name=name,
    )(scalars, *operands, *after)


def fold(square):
    part = jnp.sum(square.reshape(-1, 8, square.shape[1]), 0)
    return sum(part[:, start : start + 128] for start in range(0, part.shape[1], 128))


def turn_weight(weight, core, after=()):
    depth, width = weight.shape
    quarter = width // 4
    step = min(256, quarter)
    steps = quarter // step

    def body(core_ref, weight_ref, sent_ref, kept_ref, square_ref):
        block = weight_ref[...]
        block_turned = block.T.astype(BF16)
        square = fold(block * block)
        first = (pl.program_id(0) == 0) & (pl.program_id(1) == 0)

        @pl.when(pl.program_id(0) == 0)
        def _():
            sent_ref[...] = block_turned

        @pl.when(pl.program_id(0) == 1)
        def _():
            kept_ref[...] = block_turned

        @pl.when(first)
        def _():
            square_ref[...] = square

        @pl.when(jnp.logical_not(first))
        def _():
            square_ref[...] += square

    out = like((2 * quarter, depth), BF16)
    return run(
        body, core.reshape(1), [weight],
        [
            pl.BlockSpec(
                (depth, step),
                lambda k, j, c: (0, (2 * (j // steps) + (c[0] ^ (1 - k))) * steps + j % steps),
            )
        ],
        [out, out, like((8, 128), F32)],
        [
            pl.BlockSpec((step, depth), lambda k, j, c: (jnp.where(k == 0, j, 2 * steps - 1), 0)),
            pl.BlockSpec((step, depth), lambda k, j, c: (jnp.where(k == 1, j, 0), 0)),
            pl.BlockSpec((8, 128), lambda k, j, c: (0, 0)),
        ],
        grid=(2, 2 * steps), after=after, flops=2 * depth * width, moved=6 * depth * width, limit=16, name="turn_weight",
    )


def shares_of(view_features):
    _, count, width = view_features.shape
    half = count // 2

    def body(_, rows_ref, first_ref, low_ref, high_ref):
        low_ref[...] = rows_ref[1, :half, :]
        high_ref[...] = rows_ref[1, half:, :]
        first_ref[...] = rows_ref[0]

    outs = [like((rows, width), BF16) for rows in (count, half, half)]
    first, low, high = run(
        body, jnp.zeros((1,), jnp.int32), [view_features], [whole(view_features)],
        outs, [whole(out) for out in outs], moved=8 * count * width, limit=8, name="shares_of",
    )
    return [first], [low, high]


def go_round(parts):
    n_feat = lax.axis_size("feat")
    ring = [(i, (i + 1) % n_feat) for i in range(n_feat)]
    lists = [[part] for part in parts]
    for _ in range(1, n_feat):
        for shares in lists:
            shares.append(lax.ppermute(shares[-1], "feat", ring))
    return lists


def choose(shares, n_chip, after=()):
    n_feat = len(shares)
    chip = lax.axis_index("dp") >> 1
    back = [lax.rem(lax.axis_index("feat") - (chip ^ mask) + n_feat, n_feat) for mask in range(n_chip)]

    def body(back_ref, *refs):
        for mask in range(n_chip):
            for place in range(n_feat):

                @pl.when(back_ref[mask] == place)
                def _():
                    refs[n_feat + mask][...] = refs[place][...]

    shape = shares[0].shape
    return run(
        body, jnp.stack(back), shares, [whole(share) for share in shares],
        [like(shape, BF16)] * n_chip, [whole(shares[0])] * n_chip,
        after=after, moved=4 * n_chip * shape[0] * shape[1], limit=16, name="choose",
    )


def collect(place, own, after=()):
    n_part, n_chip = len(own), len(own[0])
    count, width = own[0][0].shape
    operands = [piece for pieces in own for piece in pieces]

    def body(place_ref, *refs):
        for part in range(n_part):
            for mask in range(n_chip):
                row = ((place_ref[0] ^ mask) * n_part + part) * count
                rows = pl.ds(pl.multiple_of(row, count), count)
                refs[-1][rows, :] = refs[part * n_chip + mask][...]

    out = like((len(operands) * count, width), BF16)
    (images,) = run(
        body, place, operands, [whole(piece) for piece in operands], [out], [whole(out)],
        after=after, moved=4 * len(operands) * count * width, limit=16, name="collect",
    )
    return images


def assemble(place, own, other, count, after=()):
    n_chip = own.shape[0] // count
    width = own.shape[1]
    half = width // 2

    def body(place_ref, own_ref, other_ref, out_ref):
        core = place_ref[1]
        for flip, ref in ((0, own_ref), (1, other_ref)):
            for chip in range(n_chip):
                rows = pl.ds(pl.multiple_of((chip * 2 + (core ^ flip)) * count, count), count)
                for side in range(2):
                    lane = pl.multiple_of((core ^ side) * half, half)
                    out_ref[rows, side * half : (side + 1) * half] = ref[
                        chip * count : (chip + 1) * count, pl.ds(lane, half)
                    ]

    out = like((2 * n_chip * count, width), BF16)
    (columns,) = run(
        body, place, [own, other], [whole(own), whole(other)], [out], [whole(out)], after=after,
        moved=8 * n_chip * count * width, limit=24, name="assemble",
    )
    return columns


def turn_columns(columns):
    batch, width = columns.shape
    depth = width // 2
    step = 256

    def body(_, columns_ref, out_ref):
        out_ref[...] = columns_ref[...].astype(F32).T.astype(BF16)

    (turned,) = run(
        body, jnp.zeros((1,), jnp.int32), [columns],
        [pl.BlockSpec((step, depth), lambda i, s: (i, 0))],
        [like((depth, batch), BF16)], [pl.BlockSpec((depth, step), lambda i, s: (0, i))],
        grid=(batch // step,), moved=4 * batch * depth, limit=8, name="turn_columns",
    )
    return turned


def forward(bits, turned_own, turned_other, columns, after=()):
    rows, depth = turned_own.shape
    batch = columns.shape[0]
    out_rows = rows // 4
    step = min(256, out_rows)
    steps = out_rows // step

    def body(bits_ref, own_a, other_a, own_b, other_b, columns_ref, out_a, out_b):
        for own_ref, other_ref, out_ref in ((own_a, other_a, out_a), (own_b, other_b, out_b)):
            block = lax.dot_general(
                own_ref[...], columns_ref[:, :depth], ROWS_BY_ROWS, preferred_element_type=F32
            )
            block += lax.dot_general(
                other_ref[...], columns_ref[:, depth:], ROWS_BY_ROWS, preferred_element_type=F32
            )
            out_ref[...] = (block - jnp.mean(block, 1, keepdims=True)).astype(BF16)

    def of_path(path):
        return pl.BlockSpec((step, depth), lambda i, b: ((2 * path + b[path]) * steps + i, 0))

    out_spec = pl.BlockSpec((step, batch), lambda i, b: (i, 0))
    return run(
        body, bits, [turned_own, turned_other, turned_own, turned_other, columns],
        [of_path(0), of_path(0), of_path(1), of_path(1), whole(columns)],
        [like((out_rows, batch), BF16)] * 2, [out_spec] * 2, grid=(steps,), after=after,
        flops=8 * out_rows * depth * batch, moved=8 * out_rows * depth + 4 * batch * depth, name="forward",
    )


def add_halves(bits, kept, got, after=()):
    rows, batch = kept[0].shape
    half = rows // 2

    def body(bits_ref, kept_a, got_a, kept_b, got_b, send_a, send_b, keep_a, keep_b):
        for path, (kept_ref, got_ref, send_ref, keep_ref) in enumerate(
            ((kept_a, got_a, send_a, keep_a), (kept_b, got_b, send_b, keep_b))
        ):
            for flip, out_ref in ((1, send_ref), (0, keep_ref)):
                rows_of = pl.ds(pl.multiple_of((bits_ref[path] ^ flip) * half, half), half)
                total = kept_ref[rows_of, :].astype(F32) + got_ref[rows_of, :].astype(F32)
                out_ref[...] = total.astype(BF16)

    operands = [kept[0], got[0], kept[1], got[1]]
    out = like((half, batch), BF16)
    outs = run(
        body, bits, operands, [whole(one) for one in operands],
        [out] * 4, [whole(out)] * 4, after=after, moved=12 * rows * batch, limit=16, name="add_halves",
    )
    return outs[:2], outs[2:]


def normalise(kept, got, after=()):
    rows, batch = kept[0].shape

    def body(_, kept_a, got_a, kept_b, got_b, normed_ref, half_ref, inverse_ref):
        for path, (kept_ref, got_ref) in enumerate(((kept_a, got_a), (kept_b, got_b))):
            total = kept_ref[...].astype(F32) + got_ref[...].astype(F32)
            total -= jnp.mean(total, 1, keepdims=True)
            inverse = lax.rsqrt(jnp.mean(total * total, 1, keepdims=True) + EPSILON)
            normed = total * inverse
            place = slice(path * rows, (path + 1) * rows)
            normed_ref[place, :] = normed
            half_ref[place, :] = normed.astype(BF16)
            inverse_ref[place, :] = jnp.broadcast_to(inverse, (rows, 128))

    operands = [kept[0], got[0], kept[1], got[1]]
    outs = [like((2 * rows, width), kind) for width, kind in ((batch, F32), (batch, BF16), (128, F32))]
    return run(
        body, jnp.zeros((1,), jnp.int32), operands, [whole(one) for one in operands],
        outs, [whole(out) for out in outs], after=after, moved=20 * rows * batch, limit=16, name="normalise",
    )


def gram_rows(place, own, other, n_chip, after=()):
    rows, batch = own.shape
    blocks = 2 * n_chip
    size = batch // blocks
    width = (blocks // 2 + 1) * size

    def body(place_ref, own_ref, other_ref, *refs):
        twice_ref = refs[-1]
        for start, ref in ((0, own_ref), (rows, other_ref)):
            twice_ref[start : start + rows, :batch] = ref[...]
            twice_ref[start : start + rows, batch:] = ref[...]
        for mask in range(n_chip):
            row = pl.multiple_of(((place_ref[0] ^ mask) * 2 + place_ref[1]) * size, size)
            left = twice_ref[:, pl.ds(row, size)].astype(F32).T.astype(BF16)
            right = twice_ref[:, pl.ds(row, width)]
            refs[mask][...] = jnp.dot(left, right, preferred_element_type=F32).astype(BF16)

    out = like((size, width), BF16)
    return run(
        body, place, [own, other], [whole(own), whole(other)],
        [out] * n_chip, [whole(out)] * n_chip,
        scratch=[pltpu.VMEM((2 * rows, 2 * batch), BF16)], after=after,
        flops=4 * rows * width * batch // 2, moved=8 * rows * batch, limit=24, name="gram_rows",
    )


def pile(parts, after=()):
    rows, width = parts[0].shape

    def body(_, *refs):
        for index in range(len(parts)):
            refs[-1][index] = refs[index][...]

    out = like((len(parts), rows, width), BF16)
    (stack,) = run(
        body, jnp.zeros((1,), jnp.int32), parts, [whole(part) for part in parts],
        [out], [whole(out)], after=after, moved=4 * len(parts) * rows * width, limit=8, name="pile",
    )
    return stack


def out_grad_of(place, gram_own, gram_other, normed, half, half_other, inverse, after=()):
    rows, batch = half.shape
    n_chip = gram_own.shape[0]
    blocks = 2 * n_chip
    size = batch // blocks

    def body(place_ref, own_ref, other_ref, normed_ref, half_ref, half_other_ref, inverse_ref,
             out_ref, gram_ref):
        for flip, ref in ((0, own_ref), (1, other_ref)):
            for mask in range(n_chip):
                row = (place_ref[0] ^ mask) * 2 + (place_ref[1] ^ flip)
                down = pl.ds(pl.multiple_of(row * size, size), size)
                for ahead in range(blocks // 2 + 1):
                    col = lax.rem(row + ahead, blocks)
                    along = pl.ds(pl.multiple_of(col * size, size), size)
                    tile = ref[mask, :, ahead * size : (ahead + 1) * size]
                    gram_ref[down, along] = tile
                    if 0 < ahead < blocks // 2:
                        gram_ref[along, down] = tile.astype(F32).T.astype(BF16)
        normed = normed_ref[...]
        other = half_other_ref[...].astype(F32)
        diagonal = jnp.mean(half_ref[...].astype(F32) * other, 1, keepdims=True)
        extra = (-2.0 * (1.0 - diagonal) - 2.0 * REDUNDANCY * diagonal) / batch
        grads = lax.dot_general(
            half_ref[...], gram_ref[...], ROWS_BY_ROWS, preferred_element_type=F32
        )
        grads = grads * (2.0 * REDUNDANCY / (batch * batch)) + extra * other
        grad_mean = jnp.mean(grads, 1, keepdims=True)
        grad_cross = jnp.mean(grads * normed, 1, keepdims=True)
        out_ref[...] = (
            inverse_ref[:, :1] * (grads - grad_mean - normed * grad_cross)
        ).astype(BF16)

    operands = [gram_own, gram_other, normed, half, half_other, inverse]
    out = like((rows, batch), BF16)
    (out_grad,) = run(
        body, place, operands, [whole(one) for one in operands], [out], [whole(out)],
        scratch=[pltpu.VMEM((batch, batch), BF16)], after=after,
        flops=2 * rows * batch * batch, moved=12 * rows * batch + 2 * batch * batch, limit=24, name="out_grad_of",
    )
    return out_grad


def weight_grad_of(place, turned, pieces, base=None, weight_squares=None, after=()):
    depth, batch = turned.shape
    cols = pieces[0].shape[0]
    last = base is not None

    def body(place_ref, turned_ref, *refs):
        if last:
            base_ref, weight_squares_ref, out_ref, square_ref = refs[4:]
        else:
            (out_ref,) = refs[4:]
        for index in range(4):

            @pl.when(pl.program_id(0) == index)
            def _():
                total = lax.dot_general(
                    turned_ref[...], refs[index][...], ROWS_BY_ROWS, preferred_element_type=F32
                )
                if last:
                    total += base_ref[...]
                    square = fold(total * total)
                    if index == 0:
                        square_ref[:8, :] = square
                        square_ref[8:, :] = weight_squares_ref[...]
                    else:
                        square_ref[:8, :] += square
                out_ref[...] = total

    tile = pl.BlockSpec((depth, cols), lambda j, s: (0, (j >> 1) * 2 + ((j & 1) ^ s[1])))
    square = pl.BlockSpec((16, 128), lambda j, s: (0, 0))
    operands = [turned, *pieces]
    return run(
        body, place, operands + ([base, weight_squares] if last else []),
        [whole(one) for one in operands] + ([tile, whole(weight_squares)] if last else []),
        [like((depth, 4 * cols), F32)] + ([like((16, 128), F32)] if last else []),
        [tile] + ([square] if last else []), grid=(4,), after=after,
        flops=8 * cols * batch * depth, moved=16 * depth * cols * (2 if last else 1), limit=20, name="weight_grad_of",
    )


def update(sums, weight, velocity, weight_grad):
    depth, width = weight.shape
    step = min(128, depth)
    n_sum = len(sums)

    def body(_, *refs):
        weight_ref, velocity_ref, grad_ref, new_weight_ref, new_velocity_ref = refs[n_sum:]
        total = refs[0][...]
        for ref in refs[1:n_sum]:
            total += ref[...]
        grad_norm = jnp.sqrt(jnp.sum(total[:8], keepdims=True))
        weight_norm = jnp.sqrt(jnp.sum(total[8:], keepdims=True))
        trust = weight_norm / (grad_norm + NORM_EPSILON)
        new_velocity = MOMENTUM * velocity_ref[...] + trust * grad_ref[...]
        new_velocity_ref[...] = new_velocity
        new_weight_ref[...] = weight_ref[...] - LEARN_RATE * new_velocity

    tile = pl.BlockSpec((step, width), lambda i, s: (i, 0))
    out = like((depth, width), F32)
    return run(
        body, jnp.zeros((1,), jnp.int32), [*sums, weight, velocity, weight_grad],
        [whole(one) for one in sums] + [tile] * 3, [out, out], [tile, tile],
        grid=(depth // step,), flops=4 * depth * width, moved=20 * depth * width, limit=16, name="update",
    )


def per_device(view_features, weight, velocity):
    n_dp, n_feat = lax.axis_size("dp"), lax.axis_size("feat")
    n_chip = n_dp // 2
    assert n_chip == n_feat and view_features.shape[2] == 2 * weight.shape[0]
    high = list(range(1, n_dp.bit_length() - 1))
    orders = (high, high[::-1])
    chip, core = lax.axis_index("dp") >> 1, bit_value("dp", 0)
    place = jnp.stack([chip, core])

    def bits_at(level):
        return jnp.stack([bit_value("dp", order[level]) for order in orders])

    shares = [go_round(parts) for parts in shares_of(view_features)]
    def cross_plane(part, after=()):
        own = list(choose(part, n_chip, after=after))
        for mask in range(1, n_chip):
            own[mask] = swap(own[mask], "dp", 2 * mask)
        return own

    def both_cores(own, collect_after=(), after=()):
        images = collect(place, own, after=collect_after)
        other = swap(images, "dp", 1)
        return assemble(place, images, other, view_features.shape[1], after=after)

    def send_on(v, level, send):
        return [swap(send[p], "dp", 1 << orders[p][level]) for p in range(2)]

    def sum_plane(rows):
        total = rows[0].astype(F32)
        for mask in range(1, n_chip):
            total += swap(rows[mask], "dp", 2 * mask).astype(F32)
        return total.astype(BF16)

    def sum_line(total, bit):
        return (total.astype(F32) + swap(total, "feat", 1 << bit).astype(F32)).astype(BF16)

    def spread_gram(total, after=()):
        parts = [total] + [swap(total, "dp", 2 * mask) for mask in range(1, n_chip)]
        own = pile(parts, after=after)
        return own, swap(own, "dp", 1)

    def gather_step(parts, step):
        bits_of = [order[len(order) - 1 - step] for order in orders]
        return [
            join(part, swap(part, "dp", 1 << bit), bit_value("dp", bit))
            for part, bit in zip(parts, bits_of)
        ]

    columns, turned, send, keep, got, gram, normed, half, inverse, rows = (
        [None] * 2 for _ in range(10)
    )
    bits = bits_at(0)
    line_bits = range(n_feat.bit_length() - 1)
    pieces = [cross_plane(part) for part in shares[1]]
    sent, turned_own, weight_squares = turn_weight(weight, core, after=[pieces[1][0]])
    turned_other = swap(sent, "dp", 1)
    columns[1] = both_cores(pieces, collect_after=[turned_own, shares[0][0][-2]])
    turned[1] = turn_columns(columns[1])
    send[1] = forward(1 - bits, turned_own, turned_other, columns[1])
    got[1] = send_on(1, 0, send[1])
    pieces = [cross_plane(part, [send[1][0]]) for part in shares[0]]
    keep[1] = forward(bits, turned_own, turned_other, columns[1], after=[turned[1], send[1][0]])
    for level in range(1, len(high)):
        send[1], keep[1] = add_halves(bits_at(level), keep[1], got[1])
        got[1] = send_on(1, level, send[1])
    columns[0] = both_cores(pieces, [send[1][0]])
    turned[0] = turn_columns(columns[0])
    send[0] = forward(1 - bits, turned_own, turned_other, columns[0])
    ahead = [send[0][0]]
    got[0] = send_on(0, 0, send[0])
    normed[1], half[1], inverse[1] = normalise(keep[1], got[1], after=ahead)
    rows[1] = list(gram_rows(place, half[1], swap(half[1], "dp", 1), n_chip))
    gram[1] = sum_plane(rows[1])
    keep[0] = forward(bits, turned_own, turned_other, columns[0], after=[turned[0], send[1][0]])
    for level in range(1, len(high)):
        send[0], keep[0] = add_halves(bits_at(level), keep[0], got[0], after=[rows[1][0]])
        got[0] = send_on(0, level, send[0])
    normed[0], half[0], inverse[0] = normalise(keep[0], got[0], after=[gram[1]])
    rows[0] = list(gram_rows(place, half[0], swap(half[0], "dp", 1), n_chip))
    for bit in line_bits:
        gram[1] = sum_line(gram[1], bit)
    gram[1] = spread_gram(gram[1])
    out_grad = [None] * 2
    out_grad[0] = out_grad_of(place, *gram[1], normed[0], half[0], half[1], inverse[0])
    gram[0] = sum_plane(rows[0])
    for bit in line_bits:
        gram[0] = sum_line(gram[0], bit)
    gram[0] = spread_gram(gram[0], after=[out_grad[0]])
    share = out_grad[0].shape[0] // 2
    parts = [None] * 2
    parts[0] = gather_step([out_grad[0][:share], out_grad[0][share:]], 0)
    out_grad[1] = out_grad_of(
        place, *gram[0], normed[1], half[1], half[0], inverse[1], after=[parts[0][0]]
    )
    parts[1] = gather_step([out_grad[1][:share], out_grad[1][share:]], 0)
    for step in range(1, len(high)):
        parts = [gather_step(part, step) for part in parts]
    gathered = [[one for own in part for one in (own, swap(own, "dp", 1))] for part in parts]
    (base,) = weight_grad_of(place, turned[0], gathered[0])
    weight_grad, squares = weight_grad_of(
        place, turned[1], gathered[1], base, weight_squares
    )
    return update(sum_everywhere(squares), weight, velocity, weight_grad)


def solution(mesh):
    in_specs = (P(None, "dp", "feat"), P("dp", "feat"), P("dp", "feat"))
    out_specs = (P("dp", "feat"), P("dp", "feat"))
    return jax.shard_map(
        per_device, mesh=mesh, in_specs=in_specs, out_specs=out_specs, check_vma=False
    )
```

```python
import jax
import jax.numpy as jnp
from jax import lax
from jax.experimental import pallas as pl
from jax.experimental.pallas import tpu as pltpu
from jax.sharding import PartitionSpec as P

EPSILON = 1e-05
NORM_EPSILON = 1e-06
REDUNDANCY = 0.0051
MOMENTUM = 0.9
LEARN_RATE = 0.2
ROWS_BY_ROWS = (((1,), (1,)), ((), ()))
MIB = 1024 * 1024
F32, BF16 = jnp.float32, jnp.bfloat16


def swap(value, axis, mask):
    return lax.ppermute(value, axis, [(i, i ^ mask) for i in range(lax.axis_size(axis))])


def bit_value(axis, bit):
    return (lax.axis_index(axis) >> bit) & 1


def join(mine, other, bit):
    return jnp.where(
        bit == 0, jnp.concatenate([mine, other], 0), jnp.concatenate([other, mine], 0)
    )


def sum_everywhere(value):
    axes = ("dp", "feat")
    count = lax.axis_size(axes)
    parts = [value]
    for low in range(0, count.bit_length() - 1, 2):
        masks = [mask << low for mask in range(1, 4) if mask << low < count]
        value = sum(parts[1:], parts[0])
        parts = [value] + [
            lax.ppermute(value, axes, [(i, i ^ mask) for i in range(count)]) for mask in masks
        ]
    return parts


def whole(array):
    zeros = (0,) * array.ndim
    return pl.BlockSpec(array.shape, lambda *_: zeros, pipeline_mode=pl.Buffered(1))


def like(shape, kind):
    return jax.ShapeDtypeStruct(shape, kind)


def run(body, scalars, operands, in_specs, outs, out_specs, grid=(1,), scratch=(), after=(),
        flops=0, moved=0, limit=32, name=None):
    n_in, n_after = len(operands), len(after)

    def kernel(scalars_ref, *refs):
        body(scalars_ref, *refs[:n_in], *refs[n_in + n_after :])

    return pl.pallas_call(
        kernel,
        grid_spec=pltpu.PrefetchScalarGridSpec(
            num_scalar_prefetch=1,
            grid=grid,
            in_specs=list(in_specs) + [pl.BlockSpec(memory_space=pl.ANY)] * n_after,
            out_specs=list(out_specs),
            scratch_shapes=list(scratch),
        ),
        out_shape=list(outs),
        compiler_params=pltpu.CompilerParams(vmem_limit_bytes=limit * MIB),
        cost_estimate=pl.CostEstimate(flops=flops, bytes_accessed=moved, transcendentals=0),
        name=name,
    )(scalars, *operands, *after)


def fold(square):
    part = jnp.sum(square.reshape(-1, 8, square.shape[1]), 0)
    return sum(part[:, start : start + 128] for start in range(0, part.shape[1], 128))


def turn_weight(weight, core, after=()):
    depth, width = weight.shape
    quarter = width // 4
    step = min(256, quarter)
    steps = quarter // step

    def body(core_ref, weight_ref, sent_ref, kept_ref, square_ref):
        block = weight_ref[...]
        block_turned = block.T.astype(BF16)
        square = fold(block * block)
        first = (pl.program_id(0) == 0) & (pl.program_id(1) == 0)

        @pl.when(pl.program_id(0) == 0)
        def _():
            sent_ref[...] = block_turned

        @pl.when(pl.program_id(0) == 1)
        def _():
            kept_ref[...] = block_turned

        @pl.when(first)
        def _():
            square_ref[...] = square

        @pl.when(jnp.logical_not(first))
        def _():
            square_ref[...] += square

    out = like((2 * quarter, depth), BF16)
    return run(
        body, core.reshape(1), [weight],
        [
            pl.BlockSpec(
                (depth, step),
                lambda k, j, c: (0, (2 * (j // steps) + (c[0] ^ (1 - k))) * steps + j % steps),
            )
        ],
        [out, out, like((8, 128), F32)],
        [
            pl.BlockSpec((step, depth), lambda k, j, c: (jnp.where(k == 0, j, 2 * steps - 1), 0)),
            pl.BlockSpec((step, depth), lambda k, j, c: (jnp.where(k == 1, j, 0), 0)),
            pl.BlockSpec((8, 128), lambda k, j, c: (0, 0)),
        ],
        grid=(2, 2 * steps), after=after, flops=2 * depth * width, moved=6 * depth * width, limit=54, name="turn_weight",
    )


def shares_of(view_features):
    _, count, width = view_features.shape
    half = count // 2

    def body(_, rows_ref, first_ref, low_ref, high_ref):
        low_ref[...] = rows_ref[1, :half, :]
        high_ref[...] = rows_ref[1, half:, :]
        first_ref[...] = rows_ref[0]

    outs = [like((rows, width), BF16) for rows in (count, half, half)]
    first, low, high = run(
        body, jnp.zeros((1,), jnp.int32), [view_features], [whole(view_features)],
        outs, [whole(out) for out in outs], moved=8 * count * width, limit=8, name="shares_of",
    )
    return [first], [low, high]


def go_round(parts):
    n_feat = lax.axis_size("feat")
    ring = [(i, (i + 1) % n_feat) for i in range(n_feat)]
    lists = [[part] for part in parts]
    for _ in range(1, n_feat):
        for shares in lists:
            shares.append(lax.ppermute(shares[-1], "feat", ring))
    return lists


def choose(shares, n_chip, after=()):
    n_feat = len(shares)
    chip = lax.axis_index("dp") >> 1
    back = [lax.rem(lax.axis_index("feat") - (chip ^ mask) + n_feat, n_feat) for mask in range(n_chip)]

    def body(back_ref, *refs):
        for mask in range(n_chip):
            for place in range(n_feat):

                @pl.when(back_ref[mask] == place)
                def _():
                    refs[n_feat + mask][...] = refs[place][...]

    shape = shares[0].shape
    return run(
        body, jnp.stack(back), shares, [whole(share) for share in shares],
        [like(shape, BF16)] * n_chip, [whole(shares[0])] * n_chip,
        after=after, moved=4 * n_chip * shape[0] * shape[1], limit=10, name="choose",
    )


def collect(place, own, after=()):
    n_part, n_chip = len(own), len(own[0])
    count, width = own[0][0].shape
    operands = [piece for pieces in own for piece in pieces]

    def body(place_ref, *refs):
        for part in range(n_part):
            for mask in range(n_chip):
                row = ((place_ref[0] ^ mask) * n_part + part) * count
                rows = pl.ds(pl.multiple_of(row, count), count)
                refs[-1][rows, :] = refs[part * n_chip + mask][...]

    out = like((len(operands) * count, width), BF16)
    (images,) = run(
        body, place, operands, [whole(piece) for piece in operands], [out], [whole(out)],
        after=after, moved=4 * len(operands) * count * width, limit=10, name="collect",
    )
    return images


def assemble(place, own, other, count, after=()):
    n_chip = own.shape[0] // count
    width = own.shape[1]
    half = width // 2

    def body(place_ref, own_ref, other_ref, out_ref):
        core = place_ref[1]
        for flip, ref in ((0, own_ref), (1, other_ref)):
            for chip in range(n_chip):
                rows = pl.ds(pl.multiple_of((chip * 2 + (core ^ flip)) * count, count), count)
                for side in range(2):
                    lane = pl.multiple_of((core ^ side) * half, half)
                    out_ref[rows, side * half : (side + 1) * half] = ref[
                        chip * count : (chip + 1) * count, pl.ds(lane, half)
                    ]

    out = like((2 * n_chip * count, width), BF16)
    (columns,) = run(
        body, place, [own, other], [whole(own), whole(other)], [out], [whole(out)], after=after,
        moved=8 * n_chip * count * width, limit=12, name="assemble",
    )
    return columns


def turn_columns(columns):
    batch, width = columns.shape
    depth = width // 2
    step = 256

    def body(_, columns_ref, out_ref):
        out_ref[...] = columns_ref[...].astype(F32).T.astype(BF16)

    (turned,) = run(
        body, jnp.zeros((1,), jnp.int32), [columns],
        [pl.BlockSpec((step, depth), lambda i, s: (i, 0))],
        [like((depth, batch), BF16)], [pl.BlockSpec((depth, step), lambda i, s: (0, i))],
        grid=(batch // step,), moved=4 * batch * depth, limit=8, name="turn_columns",
    )
    return turned


def forward(bits, turned_own, turned_other, columns, after=()):
    rows, depth = turned_own.shape
    batch = columns.shape[0]
    out_rows = rows // 4
    step = min(256, out_rows)
    steps = out_rows // step

    def body(bits_ref, own_a, other_a, own_b, other_b, columns_ref, out_a, out_b):
        own = jnp.concatenate([own_a[...], own_b[...]], 0)
        other = jnp.concatenate([other_a[...], other_b[...]], 0)
        block = lax.dot_general(
            own, columns_ref[:, :depth], ROWS_BY_ROWS, preferred_element_type=F32
        )
        block += lax.dot_general(
            other, columns_ref[:, depth:], ROWS_BY_ROWS, preferred_element_type=F32
        )
        block = (block - jnp.mean(block, 1, keepdims=True)).astype(BF16)
        out_a[...] = block[:step]
        out_b[...] = block[step:]

    def of_path(path):
        return pl.BlockSpec((step, depth), lambda i, b: ((2 * path + b[path]) * steps + i, 0))

    out_spec = pl.BlockSpec((step, batch), lambda i, b: (i, 0))
    return run(
        body, bits, [turned_own, turned_other, turned_own, turned_other, columns],
        [of_path(0), of_path(0), of_path(1), of_path(1), whole(columns)],
        [like((out_rows, batch), BF16)] * 2, [out_spec] * 2, grid=(steps,), after=after,
        flops=8 * out_rows * depth * batch, moved=8 * out_rows * depth + 4 * batch * depth, name="forward",
    )


def add_halves(bits, kept, got, after=()):
    rows, batch = kept[0].shape
    half = rows // 2

    def body(bits_ref, kept_a, got_a, kept_b, got_b, send_a, send_b, keep_a, keep_b):
        for path, (kept_ref, got_ref, send_ref, keep_ref) in enumerate(
            ((kept_a, got_a, send_a, keep_a), (kept_b, got_b, send_b, keep_b))
        ):
            for flip, out_ref in ((1, send_ref), (0, keep_ref)):
                rows_of = pl.ds(pl.multiple_of((bits_ref[path] ^ flip) * half, half), half)
                total = kept_ref[rows_of, :].astype(F32) + got_ref[rows_of, :].astype(F32)
                out_ref[...] = total.astype(BF16)

    operands = [kept[0], got[0], kept[1], got[1]]
    out = like((half, batch), BF16)
    outs = run(
        body, bits, operands, [whole(one) for one in operands],
        [out] * 4, [whole(out)] * 4, after=after, moved=12 * rows * batch, limit=16, name="add_halves",
    )
    return outs[:2], outs[2:]


def normalise(kept, got, after=()):
    rows, batch = kept[0].shape

    def body(_, kept_a, got_a, kept_b, got_b, normed_ref, half_ref, inverse_ref):
        for path, (kept_ref, got_ref) in enumerate(((kept_a, got_a), (kept_b, got_b))):
            total = kept_ref[...].astype(F32) + got_ref[...].astype(F32)
            total -= jnp.mean(total, 1, keepdims=True)
            inverse = lax.rsqrt(jnp.mean(total * total, 1, keepdims=True) + EPSILON)
            normed = total * inverse
            place = slice(path * rows, (path + 1) * rows)
            normed_ref[place, :] = normed
            half_ref[place, :] = normed.astype(BF16)
            inverse_ref[place, :] = jnp.broadcast_to(inverse, (rows, 128))

    operands = [kept[0], got[0], kept[1], got[1]]
    outs = [like((2 * rows, width), kind) for width, kind in ((batch, F32), (batch, BF16), (128, F32))]
    return run(
        body, jnp.zeros((1,), jnp.int32), operands, [whole(one) for one in operands],
        outs, [whole(out) for out in outs], after=after, moved=20 * rows * batch, limit=16, name="normalise",
    )


def gram_rows(place, own, other, n_chip, after=()):
    rows, batch = own.shape
    blocks = 2 * n_chip
    size = batch // blocks
    width = (blocks // 2 + 1) * size

    def body(place_ref, own_ref, other_ref, *refs):
        twice_ref = refs[-1]
        for start, ref in ((0, own_ref), (rows, other_ref)):
            twice_ref[start : start + rows, :batch] = ref[...]
            twice_ref[start : start + rows, batch:] = ref[...]
        for mask in range(n_chip):
            row = pl.multiple_of(((place_ref[0] ^ mask) * 2 + place_ref[1]) * size, size)
            left = twice_ref[:, pl.ds(row, size)].astype(F32).T.astype(BF16)
            right = twice_ref[:, pl.ds(row, width)]
            refs[mask][...] = jnp.dot(left, right, preferred_element_type=F32).astype(BF16)

    out = like((size, width), BF16)
    return run(
        body, place, [own, other], [whole(own), whole(other)],
        [out] * n_chip, [whole(out)] * n_chip,
        scratch=[pltpu.VMEM((2 * rows, 2 * batch), BF16)], after=after,
        flops=4 * rows * width * batch // 2, moved=8 * rows * batch, limit=24, name="gram_rows",
    )


def join_after(mine, other, bit, after):
    rows, width = mine.shape

    def body(bit_ref, mine_ref, other_ref, out_ref):
        first = pl.multiple_of(bit_ref[0] * rows, rows)
        second = pl.multiple_of((1 - bit_ref[0]) * rows, rows)
        out_ref[pl.ds(first, rows), :] = mine_ref[...]
        out_ref[pl.ds(second, rows), :] = other_ref[...]

    out = like((2 * rows, width), BF16)
    (joined,) = run(
        body, bit.reshape(1), [mine, other], [whole(mine), whole(other)], [out], [whole(out)],
        after=after, moved=8 * rows * width, limit=8, name="join_after",
    )
    return joined


def add_up(parts, after=()):
    def body(_, *refs):
        total = refs[0][...].astype(F32)
        for ref in refs[1:-1]:
            total += ref[...].astype(F32)
        refs[-1][...] = total.astype(BF16)

    (out,) = run(
        body, jnp.zeros((1,), jnp.int32), parts, [whole(part) for part in parts],
        [like(parts[0].shape, BF16)], [whole(parts[0])], after=after,
        moved=4 * len(parts) * parts[0].size, limit=8, name="add_up",
    )
    return out


def pile(parts, after=()):
    rows, width = parts[0].shape

    def body(_, *refs):
        for index in range(len(parts)):
            refs[-1][index] = refs[index][...]

    out = like((len(parts), rows, width), BF16)
    (stack,) = run(
        body, jnp.zeros((1,), jnp.int32), parts, [whole(part) for part in parts],
        [out], [whole(out)], after=after, moved=4 * len(parts) * rows * width, limit=8, name="pile",
    )
    return stack


def out_grad_of(place, gram_own, gram_other, normed, half, half_other, inverse, after=()):
    rows, batch = half.shape
    n_chip = gram_own.shape[0]
    blocks = 2 * n_chip
    size = batch // blocks

    def body(place_ref, own_ref, other_ref, normed_ref, half_ref, half_other_ref, inverse_ref,
             out_ref, gram_ref):
        for flip, ref in ((0, own_ref), (1, other_ref)):
            for mask in range(n_chip):
                row = (place_ref[0] ^ mask) * 2 + (place_ref[1] ^ flip)
                down = pl.ds(pl.multiple_of(row * size, size), size)
                for ahead in range(blocks // 2 + 1):
                    col = lax.rem(row + ahead, blocks)
                    along = pl.ds(pl.multiple_of(col * size, size), size)
                    tile = ref[mask, :, ahead * size : (ahead + 1) * size]
                    gram_ref[down, along] = tile
                    if 0 < ahead < blocks // 2:
                        gram_ref[along, down] = tile.astype(F32).T.astype(BF16)
        normed = normed_ref[...]
        other = half_other_ref[...].astype(F32)
        diagonal = jnp.mean(half_ref[...].astype(F32) * other, 1, keepdims=True)
        extra = (-2.0 * (1.0 - diagonal) - 2.0 * REDUNDANCY * diagonal) / batch
        grads = lax.dot_general(
            half_ref[...], gram_ref[...], ROWS_BY_ROWS, preferred_element_type=F32
        )
        grads = grads * (2.0 * REDUNDANCY / (batch * batch)) + extra * other
        grad_mean = jnp.mean(grads, 1, keepdims=True)
        grad_cross = jnp.mean(grads * normed, 1, keepdims=True)
        out_ref[...] = (
            inverse_ref[:, :1] * (grads - grad_mean - normed * grad_cross)
        ).astype(BF16)

    operands = [gram_own, gram_other, normed, half, half_other, inverse]
    out = like((rows, batch), BF16)
    (out_grad,) = run(
        body, place, operands, [whole(one) for one in operands], [out], [whole(out)],
        scratch=[pltpu.VMEM((batch, batch), BF16)], after=after,
        flops=2 * rows * batch * batch, moved=12 * rows * batch + 2 * batch * batch, limit=24, name="out_grad_of",
    )
    return out_grad


def weight_grad_of(place, turned, pieces, base=None, weight_squares=None, after=()):
    depth, batch = turned.shape
    cols = pieces[0].shape[0]
    last = base is not None

    def body(place_ref, turned_ref, *refs):
        if last:
            base_ref, weight_squares_ref, out_ref, square_ref = refs[4:]
        else:
            (out_ref,) = refs[4:]
        for index in range(4):

            @pl.when(pl.program_id(0) == index)
            def _():
                total = lax.dot_general(
                    turned_ref[...], refs[index][...], ROWS_BY_ROWS, preferred_element_type=F32
                )
                if last:
                    total += base_ref[...]
                    square = fold(total * total)
                    if index == 0:
                        square_ref[:8, :] = square
                        square_ref[8:, :] = weight_squares_ref[...]
                    else:
                        square_ref[:8, :] += square
                out_ref[...] = total

    tile = pl.BlockSpec((depth, cols), lambda j, s: (0, (j >> 1) * 2 + ((j & 1) ^ s[1])))
    square = pl.BlockSpec((16, 128), lambda j, s: (0, 0))
    operands = [turned, *pieces]
    return run(
        body, place, operands + ([base, weight_squares] if last else []),
        [whole(one) for one in operands] + ([tile, whole(weight_squares)] if last else []),
        [like((depth, 4 * cols), F32)] + ([like((16, 128), F32)] if last else []),
        [tile] + ([square] if last else []), grid=(4,), after=after,
        flops=8 * cols * batch * depth, moved=16 * depth * cols * (2 if last else 1), limit=20, name="weight_grad_of",
    )


def update(sums, weight, velocity, weight_grad):
    depth, width = weight.shape
    step = min(128, depth)
    n_sum = len(sums)

    def body(_, *refs):
        weight_ref, velocity_ref, grad_ref, new_weight_ref, new_velocity_ref = refs[n_sum:]
        total = refs[0][...]
        for ref in refs[1:n_sum]:
            total += ref[...]
        grad_norm = jnp.sqrt(jnp.sum(total[:8], keepdims=True))
        weight_norm = jnp.sqrt(jnp.sum(total[8:], keepdims=True))
        trust = weight_norm / (grad_norm + NORM_EPSILON)
        new_velocity = MOMENTUM * velocity_ref[...] + trust * grad_ref[...]
        new_velocity_ref[...] = new_velocity
        new_weight_ref[...] = weight_ref[...] - LEARN_RATE * new_velocity

    tile = pl.BlockSpec((step, width), lambda i, s: (i, 0))
    out = like((depth, width), F32)
    return run(
        body, jnp.zeros((1,), jnp.int32), [*sums, weight, velocity, weight_grad],
        [whole(one) for one in sums] + [tile] * 3, [out, out], [tile, tile],
        grid=(depth // step,), flops=4 * depth * width, moved=20 * depth * width, limit=16, name="update",
    )


def per_device(view_features, weight, velocity):
    n_dp, n_feat = lax.axis_size("dp"), lax.axis_size("feat")
    n_chip = n_dp // 2
    assert n_chip == n_feat and view_features.shape[2] == 2 * weight.shape[0]
    high = list(range(1, n_dp.bit_length() - 1))
    orders = (high, high[::-1])
    chip, core = lax.axis_index("dp") >> 1, bit_value("dp", 0)
    place = jnp.stack([chip, core])

    def bits_at(level):
        return jnp.stack([bit_value("dp", order[level]) for order in orders])

    shares = [go_round(parts) for parts in shares_of(view_features)]
    def cross_plane(part, after=()):
        own = list(choose(part, n_chip, after=after))
        for mask in range(1, n_chip):
            own[mask] = swap(own[mask], "dp", 2 * mask)
        return own

    def both_cores(own, collect_after=(), after=()):
        images = collect(place, own, after=collect_after)
        other = swap(images, "dp", 1)
        return assemble(place, images, other, view_features.shape[1], after=after)

    def send_on(v, level, send):
        return [swap(send[p], "dp", 1 << orders[p][level]) for p in range(2)]

    def sum_plane(rows, after=()):
        parts = [rows[0]] + [swap(rows[mask], "dp", 2 * mask) for mask in range(1, n_chip)]
        return add_up(parts, after=after)

    def sum_line(total, bit, after=()):
        return add_up([total, swap(total, "feat", 1 << bit)], after=after)

    def spread_gram(total, after=()):
        parts = [total] + [swap(total, "dp", 2 * mask) for mask in range(1, n_chip)]
        own = pile(parts, after=after)
        return own, swap(own, "dp", 1)

    def gather_step(parts, step, after=None):
        out = []
        for part, order in zip(parts, orders):
            bit = order[len(order) - 1 - step]
            other = swap(part, "dp", 1 << bit)
            if after is None:
                out.append(join(part, other, bit_value("dp", bit)))
            else:
                out.append(join_after(part, other, bit_value("dp", bit), after))
        return out

    def with_swapped(parts):
        return [one for own in parts for one in (own, swap(own, "dp", 1))]

    columns, turned, send, keep, got, gram, normed, half, inverse, rows = (
        [None] * 2 for _ in range(10)
    )
    bits = bits_at(0)
    line_bits = range(n_feat.bit_length() - 1)
    pieces = [cross_plane(part) for part in shares[1]]
    sent, turned_own, weight_squares = turn_weight(weight, core, after=[pieces[1][0]])
    turned_other = swap(sent, "dp", 1)
    columns[1] = both_cores(pieces, collect_after=[turned_own, shares[0][0][-2]])
    turned[1] = turn_columns(columns[1])
    send[1] = forward(1 - bits, turned_own, turned_other, columns[1])
    got[1] = send_on(1, 0, send[1])
    pieces = [cross_plane(part, [send[1][0]]) for part in shares[0]]
    keep[1] = forward(bits, turned_own, turned_other, columns[1], after=[turned[1], send[1][0]])
    for level in range(1, len(high)):
        send[1], keep[1] = add_halves(bits_at(level), keep[1], got[1])
        got[1] = send_on(1, level, send[1])
    columns[0] = both_cores(pieces, [send[1][0]])
    turned[0] = turn_columns(columns[0])
    send[0] = forward(1 - bits, turned_own, turned_other, columns[0])
    ahead = [send[0][0]]
    got[0] = send_on(0, 0, send[0])
    normed[1], half[1], inverse[1] = normalise(keep[1], got[1], after=ahead)
    rows[1] = list(gram_rows(place, half[1], swap(half[1], "dp", 1), n_chip))
    keep[0] = forward(bits, turned_own, turned_other, columns[0], after=[turned[0], send[1][0]])
    for level in range(1, len(high)):
        send[0], keep[0] = add_halves(bits_at(level), keep[0], got[0], after=[rows[1][0]])
        got[0] = send_on(0, level, send[0])
    gram[1] = sum_plane(rows[1], after=[send[0][0]])
    normed[0], half[0], inverse[0] = normalise(keep[0], got[0], after=[gram[1]])
    rows[0] = list(gram_rows(place, half[0], swap(half[0], "dp", 1), n_chip))
    last = line_bits[-1]
    for bit in line_bits[:-1]:
        gram[1] = sum_line(gram[1], bit, after=[rows[0][0]])
    gram[0] = sum_plane(rows[0])
    gram[1] = sum_line(gram[1], last, after=[gram[0]])
    for bit in line_bits[:-1]:
        gram[0] = sum_line(gram[0], bit)
    gram[1] = spread_gram(gram[1], after=[gram[0]])
    gram[0] = sum_line(gram[0], last)
    out_grad = [None] * 2
    out_grad[0] = out_grad_of(
        place, *gram[1], normed[0], half[0], half[1], inverse[0], after=[gram[0]]
    )
    gram[0] = spread_gram(gram[0])
    share = out_grad[0].shape[0] // 2
    parts = gather_step([out_grad[0][:share], out_grad[0][share:]], 0, after=[gram[0][0]])
    out_grad[1] = out_grad_of(place, *gram[0], normed[1], half[1], half[0], inverse[1])
    last_parts = gather_step([out_grad[1][:share], out_grad[1][share:]], 0)
    for step in range(1, len(high)):
        parts = gather_step(parts, step, after=last_parts)
    (base,) = weight_grad_of(place, turned[0], with_swapped(parts))
    for step in range(1, len(high)):
        last_parts = gather_step(last_parts, step, after=[base] if step == len(high) - 1 else None)
    weight_grad, squares = weight_grad_of(
        place, turned[1], with_swapped(last_parts), base, weight_squares
    )
    return update(sum_everywhere(squares), weight, velocity, weight_grad)


def solution(mesh):
    in_specs = (P(None, "dp", "feat"), P("dp", "feat"), P("dp", "feat"))
    out_specs = (P("dp", "feat"), P("dp", "feat"))
    return jax.shard_map(
        per_device, mesh=mesh, in_specs=in_specs, out_specs=out_specs, check_vma=False
    )
```

```python
import jax
import jax.numpy as jnp
from jax import lax
from jax.experimental import pallas as pl
from jax.experimental.pallas import tpu as pltpu
from jax.sharding import PartitionSpec as P

EPSILON = 1e-05
NORM_EPSILON = 1e-06
REDUNDANCY = 0.0051
MOMENTUM = 0.9
LEARN_RATE = 0.2
ROWS_BY_ROWS = (((1,), (1,)), ((), ()))
MIB = 1024 * 1024
F32, BF16 = jnp.float32, jnp.bfloat16


def swap(value, axis, mask):
    return lax.ppermute(value, axis, [(i, i ^ mask) for i in range(lax.axis_size(axis))])


def bit_value(axis, bit):
    return (lax.axis_index(axis) >> bit) & 1


def join(mine, other, bit):
    return jnp.where(
        bit == 0, jnp.concatenate([mine, other], 0), jnp.concatenate([other, mine], 0)
    )


def sum_everywhere(value):
    axes = ("dp", "feat")
    count = lax.axis_size(axes)
    parts = [value]
    for low in range(0, count.bit_length() - 1, 2):
        masks = [mask << low for mask in range(1, 4) if mask << low < count]
        value = sum(parts[1:], parts[0])
        parts = [value] + [
            lax.ppermute(value, axes, [(i, i ^ mask) for i in range(count)]) for mask in masks
        ]
    return parts


def whole(array):
    zeros = (0,) * array.ndim
    return pl.BlockSpec(array.shape, lambda *_: zeros, pipeline_mode=pl.Buffered(1))


def like(shape, kind):
    return jax.ShapeDtypeStruct(shape, kind)


def run(body, scalars, operands, in_specs, outs, out_specs, grid=(1,), scratch=(), after=(),
        flops=0, moved=0, limit=32, name=None, aliases=None):
    n_in, n_after = len(operands), len(after)

    def kernel(scalars_ref, *refs):
        body(scalars_ref, *refs[:n_in], *refs[n_in + n_after :])

    return pl.pallas_call(
        kernel,
        grid_spec=pltpu.PrefetchScalarGridSpec(
            num_scalar_prefetch=1,
            grid=grid,
            in_specs=list(in_specs) + [pl.BlockSpec(memory_space=pl.ANY)] * n_after,
            out_specs=list(out_specs),
            scratch_shapes=list(scratch),
        ),
        out_shape=list(outs),
        compiler_params=pltpu.CompilerParams(vmem_limit_bytes=limit * MIB),
        cost_estimate=pl.CostEstimate(flops=flops, bytes_accessed=moved, transcendentals=0),
        name=name,
        input_output_aliases=aliases or {},
    )(scalars, *operands, *after)


def fold(square):
    part = jnp.sum(square.reshape(-1, 8, square.shape[1]), 0)
    return sum(part[:, start : start + 128] for start in range(0, part.shape[1], 128))


def turn_weight(weight, core, after=()):
    depth, width = weight.shape
    quarter = width // 4
    step = min(256, quarter)
    steps = quarter // step

    def body(core_ref, weight_ref, sent_ref, kept_ref, square_ref):
        block = weight_ref[...]
        block_turned = block.T.astype(BF16)
        square = fold(block * block)
        first = (pl.program_id(0) == 0) & (pl.program_id(1) == 0)

        @pl.when(pl.program_id(0) == 0)
        def _():
            sent_ref[...] = block_turned

        @pl.when(pl.program_id(0) == 1)
        def _():
            kept_ref[...] = block_turned

        @pl.when(first)
        def _():
            square_ref[:8, :] = jnp.zeros_like(square)
            square_ref[8:, :] = square

        @pl.when(jnp.logical_not(first))
        def _():
            square_ref[8:, :] += square

    out = like((2 * quarter, depth), BF16)
    return run(
        body, core.reshape(1), [weight],
        [
            pl.BlockSpec(
                (depth, step),
                lambda k, j, c: (0, (2 * (j // steps) + (c[0] ^ (1 - k))) * steps + j % steps),
            )
        ],
        [out, out, like((16, 128), F32)],
        [
            pl.BlockSpec((step, depth), lambda k, j, c: (jnp.where(k == 0, j, 2 * steps - 1), 0)),
            pl.BlockSpec((step, depth), lambda k, j, c: (jnp.where(k == 1, j, 0), 0)),
            pl.BlockSpec((16, 128), lambda k, j, c: (0, 0)),
        ],
        grid=(2, 2 * steps), after=after, flops=2 * depth * width, moved=6 * depth * width, limit=16, name="turn_weight",
    )


def shares_of(view_features):
    _, count, width = view_features.shape
    half = count // 2

    def body(_, rows_ref, first_ref, low_ref, high_ref):
        low_ref[...] = rows_ref[1, :half, :]
        high_ref[...] = rows_ref[1, half:, :]
        first_ref[...] = rows_ref[0]

    outs = [like((rows, width), BF16) for rows in (count, half, half)]
    first, low, high = run(
        body, jnp.zeros((1,), jnp.int32), [view_features], [whole(view_features)],
        outs, [whole(out) for out in outs], moved=8 * count * width, limit=8, name="shares_of",
    )
    return [first], [low, high]


def go_round(parts):
    n_feat = lax.axis_size("feat")
    ring = [(i, (i + 1) % n_feat) for i in range(n_feat)]
    lists = [[part] for part in parts]
    for _ in range(1, n_feat):
        for shares in lists:
            shares.append(lax.ppermute(shares[-1], "feat", ring))
    return lists


def choose(shares, n_chip, after=()):
    n_feat = len(shares)
    chip = lax.axis_index("dp") >> 1
    back = [lax.rem(lax.axis_index("feat") - (chip ^ mask) + n_feat, n_feat) for mask in range(n_chip)]

    def body(back_ref, *refs):
        for mask in range(n_chip):
            for place in range(n_feat):

                @pl.when(back_ref[mask] == place)
                def _():
                    refs[n_feat + mask][...] = refs[place][...]

    shape = shares[0].shape
    return run(
        body, jnp.stack(back), shares, [whole(share) for share in shares],
        [like(shape, BF16)] * n_chip, [whole(shares[0])] * n_chip,
        after=after, moved=4 * n_chip * shape[0] * shape[1], limit=10, name="choose",
    )


def collect(place, own, after=()):
    n_part, n_chip = len(own), len(own[0])
    count, width = own[0][0].shape
    operands = [piece for pieces in own for piece in pieces]

    def body(place_ref, *refs):
        for part in range(n_part):
            for mask in range(n_chip):
                row = ((place_ref[0] ^ mask) * n_part + part) * count
                rows = pl.ds(pl.multiple_of(row, count), count)
                refs[-1][rows, :] = refs[part * n_chip + mask][...]

    out = like((len(operands) * count, width), BF16)
    (images,) = run(
        body, place, operands, [whole(piece) for piece in operands], [out], [whole(out)],
        after=after, moved=4 * len(operands) * count * width, limit=10, name="collect",
    )
    return images


def assemble(place, own, other, count, after=()):
    n_chip = own.shape[0] // count
    width = own.shape[1]
    half = width // 2

    def body(place_ref, own_ref, other_ref, out_ref):
        core = place_ref[1]
        for flip, ref in ((0, own_ref), (1, other_ref)):
            for chip in range(n_chip):
                rows = pl.ds(pl.multiple_of((chip * 2 + (core ^ flip)) * count, count), count)
                for side in range(2):
                    lane = pl.multiple_of((core ^ side) * half, half)
                    out_ref[rows, side * half : (side + 1) * half] = ref[
                        chip * count : (chip + 1) * count, pl.ds(lane, half)
                    ]

    out = like((2 * n_chip * count, width), BF16)
    (columns,) = run(
        body, place, [own, other], [whole(own), whole(other)], [out], [whole(out)], after=after,
        moved=8 * n_chip * count * width, limit=12, name="assemble",
    )
    return columns


def turn_columns(columns):
    batch, width = columns.shape
    depth = width // 2
    step = 256

    def body(_, columns_ref, out_ref):
        out_ref[...] = columns_ref[...].astype(F32).T.astype(BF16)

    (turned,) = run(
        body, jnp.zeros((1,), jnp.int32), [columns],
        [pl.BlockSpec((step, depth), lambda i, s: (i, 0))],
        [like((depth, batch), BF16)], [pl.BlockSpec((depth, step), lambda i, s: (0, i))],
        grid=(batch // step,), moved=4 * batch * depth, limit=8, name="turn_columns",
    )
    return turned


def forward(bits, turned_own, turned_other, columns, after=()):
    rows, depth = turned_own.shape
    batch = columns.shape[0]
    out_rows = rows // 4
    step = min(256, out_rows)
    steps = out_rows // step

    def body(bits_ref, own_a, other_a, own_b, other_b, columns_ref, out_a, out_b):
        own = jnp.concatenate([own_a[...], own_b[...]], 0)
        other = jnp.concatenate([other_a[...], other_b[...]], 0)
        block = lax.dot_general(
            own, columns_ref[:, :depth], ROWS_BY_ROWS, preferred_element_type=F32
        )
        block += lax.dot_general(
            other, columns_ref[:, depth:], ROWS_BY_ROWS, preferred_element_type=F32
        )
        block = (block - jnp.mean(block, 1, keepdims=True)).astype(BF16)
        out_a[...] = block[:step]
        out_b[...] = block[step:]

    def of_path(path):
        return pl.BlockSpec((step, depth), lambda i, b: ((2 * path + b[path]) * steps + i, 0))

    out_spec = pl.BlockSpec((step, batch), lambda i, b: (i, 0))
    return run(
        body, bits, [turned_own, turned_other, turned_own, turned_other, columns],
        [of_path(0), of_path(0), of_path(1), of_path(1), whole(columns)],
        [like((out_rows, batch), BF16)] * 2, [out_spec] * 2, grid=(steps,), after=after,
        flops=8 * out_rows * depth * batch, moved=8 * out_rows * depth + 4 * batch * depth, name="forward",
    )


def add_halves(bits, kept, got, after=()):
    rows, batch = kept[0].shape
    half = rows // 2

    def body(bits_ref, kept_a, got_a, kept_b, got_b, send_a, send_b, keep_a, keep_b):
        for path, (kept_ref, got_ref, send_ref, keep_ref) in enumerate(
            ((kept_a, got_a, send_a, keep_a), (kept_b, got_b, send_b, keep_b))
        ):
            for flip, out_ref in ((1, send_ref), (0, keep_ref)):
                rows_of = pl.ds(pl.multiple_of((bits_ref[path] ^ flip) * half, half), half)
                total = kept_ref[rows_of, :].astype(F32) + got_ref[rows_of, :].astype(F32)
                out_ref[...] = total.astype(BF16)

    operands = [kept[0], got[0], kept[1], got[1]]
    out = like((half, batch), BF16)
    outs = run(
        body, bits, operands, [whole(one) for one in operands],
        [out] * 4, [whole(out)] * 4, after=after, moved=12 * rows * batch, limit=16, name="add_halves",
    )
    return outs[:2], outs[2:]


def normalise(kept, got, after=()):
    rows, batch = kept[0].shape

    def body(_, kept_a, got_a, kept_b, got_b, normed_ref, half_ref, inverse_ref):
        for path, (kept_ref, got_ref) in enumerate(((kept_a, got_a), (kept_b, got_b))):
            total = kept_ref[...].astype(F32) + got_ref[...].astype(F32)
            total -= jnp.mean(total, 1, keepdims=True)
            inverse = lax.rsqrt(jnp.mean(total * total, 1, keepdims=True) + EPSILON)
            normed = total * inverse
            place = slice(path * rows, (path + 1) * rows)
            normed_ref[place, :] = normed
            half_ref[place, :] = normed.astype(BF16)
            inverse_ref[place, :] = jnp.broadcast_to(inverse, (rows, 128))

    operands = [kept[0], got[0], kept[1], got[1]]
    outs = [like((2 * rows, width), kind) for width, kind in ((batch, F32), (batch, BF16), (128, F32))]
    return run(
        body, jnp.zeros((1,), jnp.int32), operands, [whole(one) for one in operands],
        outs, [whole(out) for out in outs], after=after, moved=20 * rows * batch, limit=16, name="normalise",
    )


def gram_rows(place, own, other, n_chip, after=()):
    rows, batch = own.shape
    blocks = 2 * n_chip
    size = batch // blocks
    width = (blocks // 2 + 1) * size

    def body(place_ref, own_ref, other_ref, *refs):
        twice_ref = refs[-1]
        for start, ref in ((0, own_ref), (rows, other_ref)):
            twice_ref[start : start + rows, :batch] = ref[...]
            twice_ref[start : start + rows, batch:] = ref[...]
        for mask in range(n_chip):
            row = pl.multiple_of(((place_ref[0] ^ mask) * 2 + place_ref[1]) * size, size)
            left = twice_ref[:, pl.ds(row, size)].astype(F32).T.astype(BF16)
            right = twice_ref[:, pl.ds(row, width)]
            refs[mask][...] = jnp.dot(left, right, preferred_element_type=F32).astype(BF16)

    out = like((size, width), BF16)
    return run(
        body, place, [own, other], [whole(own), whole(other)],
        [out] * n_chip, [whole(out)] * n_chip,
        scratch=[pltpu.VMEM((2 * rows, 2 * batch), BF16)], after=after,
        flops=4 * rows * width * batch // 2, moved=8 * rows * batch, limit=24, name="gram_rows",
    )


def join_after(mine, other, bit, after):
    rows, width = mine.shape

    def body(bit_ref, mine_ref, other_ref, out_ref):
        first = pl.multiple_of(bit_ref[0] * rows, rows)
        second = pl.multiple_of((1 - bit_ref[0]) * rows, rows)
        out_ref[pl.ds(first, rows), :] = mine_ref[...]
        out_ref[pl.ds(second, rows), :] = other_ref[...]

    out = like((2 * rows, width), BF16)
    (joined,) = run(
        body, bit.reshape(1), [mine, other], [whole(mine), whole(other)], [out], [whole(out)],
        after=after, moved=8 * rows * width, limit=8, name="join_after",
    )
    return joined


def add_up(parts, after=()):
    def body(_, *refs):
        total = refs[0][...].astype(F32)
        for ref in refs[1:-1]:
            total += ref[...].astype(F32)
        refs[-1][...] = total.astype(BF16)

    (out,) = run(
        body, jnp.zeros((1,), jnp.int32), parts, [whole(part) for part in parts],
        [like(parts[0].shape, BF16)], [whole(parts[0])], after=after,
        moved=4 * len(parts) * parts[0].size, limit=8, name="add_up",
    )
    return out


def pile(parts, after=()):
    rows, width = parts[0].shape

    def body(_, *refs):
        for index in range(len(parts)):
            refs[-1][index] = refs[index][...]

    out = like((len(parts), rows, width), BF16)
    (stack,) = run(
        body, jnp.zeros((1,), jnp.int32), parts, [whole(part) for part in parts],
        [out], [whole(out)], after=after, moved=4 * len(parts) * rows * width, limit=8, name="pile",
    )
    return stack


def out_grad_of(place, gram_own, gram_other, normed, half, half_other, inverse, after=()):
    rows, batch = half.shape
    n_chip = gram_own.shape[0]
    blocks = 2 * n_chip
    size = batch // blocks

    def body(place_ref, own_ref, other_ref, normed_ref, half_ref, half_other_ref, inverse_ref,
             out_ref, gram_ref):
        for flip, ref in ((0, own_ref), (1, other_ref)):
            for mask in range(n_chip):
                row = (place_ref[0] ^ mask) * 2 + (place_ref[1] ^ flip)
                down = pl.ds(pl.multiple_of(row * size, size), size)
                for ahead in range(blocks // 2 + 1):
                    col = lax.rem(row + ahead, blocks)
                    along = pl.ds(pl.multiple_of(col * size, size), size)
                    tile = ref[mask, :, ahead * size : (ahead + 1) * size]
                    gram_ref[down, along] = tile
                    if 0 < ahead < blocks // 2:
                        gram_ref[along, down] = tile.astype(F32).T.astype(BF16)
        normed = normed_ref[...]
        other = half_other_ref[...].astype(F32)
        diagonal = jnp.mean(half_ref[...].astype(F32) * other, 1, keepdims=True)
        extra = (-2.0 * (1.0 - diagonal) - 2.0 * REDUNDANCY * diagonal) / batch
        grads = lax.dot_general(
            half_ref[...], gram_ref[...], ROWS_BY_ROWS, preferred_element_type=F32
        )
        grads = grads * (2.0 * REDUNDANCY / (batch * batch)) + extra * other
        grad_mean = jnp.mean(grads, 1, keepdims=True)
        grad_cross = jnp.mean(grads * normed, 1, keepdims=True)
        out_ref[...] = (
            inverse_ref[:, :1] * (grads - grad_mean - normed * grad_cross)
        ).astype(BF16)

    operands = [gram_own, gram_other, normed, half, half_other, inverse]
    out = like((rows, batch), BF16)
    (out_grad,) = run(
        body, place, operands, [whole(one) for one in operands], [out], [whole(out)],
        scratch=[pltpu.VMEM((batch, batch), BF16)], after=after,
        flops=2 * rows * batch * batch, moved=12 * rows * batch + 2 * batch * batch, limit=24, name="out_grad_of",
    )
    return out_grad


def weight_grad_of(place, turned, pieces, flips, base=None, done=None, weight_squares=None):
    depth, batch = turned.shape
    cols, n_piece = pieces[0].shape[0], len(pieces)
    n_path = 2
    squares = weight_squares is not None
    rest = [one for one in (base, done, weight_squares) if one is not None]

    def body(place_ref, turned_ref, *refs):
        base_ref = refs[n_piece] if base is not None else None
        squares_in_ref = refs[n_piece + len(rest) - 1] if squares else None
        out_ref = refs[n_piece + len(rest)]
        for index in range(n_piece):

            @pl.when(pl.program_id(0) == index)
            def _():
                total = lax.dot_general(
                    turned_ref[...], refs[index][...], ROWS_BY_ROWS, preferred_element_type=F32
                )
                if base is not None:
                    total += base_ref[...]
                if squares:
                    square_ref = refs[-1]
                    if index == 0:
                        square_ref[...] = squares_in_ref[...]
                    square_ref[:8, :] += fold(total * total)
                out_ref[...] = total

    def column(j, s):
        if len(flips) == 1:
            return j * n_path + (s[1] ^ flips[0])
        return (j >> 1) * n_path + ((j & 1) ^ s[1])

    tile = pl.BlockSpec((depth, cols), lambda j, s: (0, column(j, s)))
    square = pl.BlockSpec((16, 128), lambda j, s: (0, 0))
    operands = [turned, *pieces]
    rest_specs = [tile] if base is not None else []
    if done is not None:
        rest_specs.append(pl.BlockSpec(memory_space=pl.ANY))
    if squares:
        rest_specs.append(whole(weight_squares))
    return run(
        body, place, operands + rest, [whole(one) for one in operands] + rest_specs,
        [like((depth, 4 * cols), F32)] + ([like((16, 128), F32)] if squares else []),
        [tile] + ([square] if squares else []), grid=(n_piece,),
        flops=2 * n_piece * cols * batch * depth, moved=4 * n_piece * depth * cols, limit=20,
        aliases={1 + len(operands) + len(rest_specs) - 1 - squares: 0} if done is not None else {},
        name="weight_grad_of",
    )


def update(sums, weight, velocity, weight_grad):
    depth, width = weight.shape
    step = min(128, depth)
    n_sum = len(sums)

    def body(_, *refs):
        weight_ref, velocity_ref, grad_ref, new_weight_ref, new_velocity_ref = refs[n_sum:]
        total = refs[0][...]
        for ref in refs[1:n_sum]:
            total += ref[...]
        grad_norm = jnp.sqrt(jnp.sum(total[:8], keepdims=True))
        weight_norm = jnp.sqrt(jnp.sum(total[8:], keepdims=True))
        trust = weight_norm / (grad_norm + NORM_EPSILON)
        new_velocity = MOMENTUM * velocity_ref[...] + trust * grad_ref[...]
        new_velocity_ref[...] = new_velocity
        new_weight_ref[...] = weight_ref[...] - LEARN_RATE * new_velocity

    tile = pl.BlockSpec((step, width), lambda i, s: (i, 0))
    out = like((depth, width), F32)
    return run(
        body, jnp.zeros((1,), jnp.int32), [*sums, weight, velocity, weight_grad],
        [whole(one) for one in sums] + [tile] * 3, [out, out], [tile, tile],
        grid=(depth // step,), flops=4 * depth * width, moved=20 * depth * width, limit=16, name="update",
    )


def per_device(view_features, weight, velocity):
    n_dp, n_feat = lax.axis_size("dp"), lax.axis_size("feat")
    n_chip = n_dp // 2
    assert n_chip == n_feat and view_features.shape[2] == 2 * weight.shape[0]
    high = list(range(1, n_dp.bit_length() - 1))
    orders = (high, high[::-1])
    chip, core = lax.axis_index("dp") >> 1, bit_value("dp", 0)
    place = jnp.stack([chip, core])

    def bits_at(level):
        return jnp.stack([bit_value("dp", order[level]) for order in orders])

    shares = [go_round(parts) for parts in shares_of(view_features)]
    def cross_plane(part, after=()):
        own = list(choose(part, n_chip, after=after))
        for mask in range(1, n_chip):
            own[mask] = swap(own[mask], "dp", 2 * mask)
        return own

    def both_cores(own, collect_after=(), after=()):
        images = collect(place, own, after=collect_after)
        other = swap(images, "dp", 1)
        return assemble(place, images, other, view_features.shape[1], after=after)

    def send_on(v, level, send):
        return [swap(send[p], "dp", 1 << orders[p][level]) for p in range(2)]

    def sum_plane(rows):
        total = rows[0].astype(F32)
        for mask in range(1, n_chip):
            total += swap(rows[mask], "dp", 2 * mask).astype(F32)
        return total.astype(BF16)

    def sum_line(total, bit):
        return (total.astype(F32) + swap(total, "feat", 1 << bit).astype(F32)).astype(BF16)

    def spread_gram(total, after=()):
        parts = [total] + [swap(total, "dp", 2 * mask) for mask in range(1, n_chip)]
        own = pile(parts, after=after)
        return own, swap(own, "dp", 1)

    def gather_step(parts, step, after=None):
        out = []
        for part, order in zip(parts, orders):
            bit = order[len(order) - 1 - step]
            other = swap(part, "dp", 1 << bit)
            if after is None:
                out.append(join(part, other, bit_value("dp", bit)))
            else:
                out.append(join_after(part, other, bit_value("dp", bit), after))
        return out

    def with_swapped(parts):
        return [one for own in parts for one in (own, swap(own, "dp", 1))]

    columns, turned, send, keep, got, gram, normed, half, inverse, rows = (
        [None] * 2 for _ in range(10)
    )
    bits = bits_at(0)
    line_bits = range(n_feat.bit_length() - 1)
    pieces = [cross_plane(part) for part in shares[1]]
    sent, turned_own, weight_squares = turn_weight(weight, core, after=[pieces[1][0]])
    turned_other = swap(sent, "dp", 1)
    columns[1] = both_cores(pieces, collect_after=[turned_own, shares[0][0][-2]])
    turned[1] = turn_columns(columns[1])
    send[1] = forward(1 - bits, turned_own, turned_other, columns[1])
    got[1] = send_on(1, 0, send[1])
    pieces = [cross_plane(part, [send[1][0]]) for part in shares[0]]
    keep[1] = forward(bits, turned_own, turned_other, columns[1], after=[turned[1], send[1][0]])
    for level in range(1, len(high)):
        send[1], keep[1] = add_halves(bits_at(level), keep[1], got[1])
        got[1] = send_on(1, level, send[1])
    columns[0] = both_cores(pieces, [send[1][0]])
    turned[0] = turn_columns(columns[0])
    send[0] = forward(1 - bits, turned_own, turned_other, columns[0])
    ahead = [send[0][0]]
    got[0] = send_on(0, 0, send[0])
    normed[1], half[1], inverse[1] = normalise(keep[1], got[1], after=ahead)
    rows[1] = list(gram_rows(place, half[1], swap(half[1], "dp", 1), n_chip))
    keep[0] = forward(bits, turned_own, turned_other, columns[0], after=[turned[0], send[1][0]])
    for level in range(1, len(high)):
        send[0], keep[0] = add_halves(bits_at(level), keep[0], got[0], after=[rows[1][0]])
        got[0] = send_on(0, level, send[0])
    gram[1] = sum_plane(rows[1])
    normed[0], half[0], inverse[0] = normalise(keep[0], got[0], after=[gram[1]])
    rows[0] = list(gram_rows(place, half[0], swap(half[0], "dp", 1), n_chip))
    for bit in line_bits:
        gram[1] = sum_line(gram[1], bit)
    gram[1] = spread_gram(gram[1])
    gram[0] = sum_plane(rows[0])
    for bit in line_bits:
        gram[0] = sum_line(gram[0], bit)
    out_grad = [None] * 2
    out_grad[0] = out_grad_of(
        place, *gram[1], normed[0], half[0], half[1], inverse[0], after=[gram[0]]
    )
    gram[0] = spread_gram(gram[0], after=[out_grad[0]])
    share = out_grad[0].shape[0] // 2
    out_grad[1] = out_grad_of(place, *gram[0], normed[1], half[1], half[0], inverse[1])
    parts = gather_step([out_grad[0][:share], out_grad[0][share:]], 0, after=[out_grad[1]])
    last_parts = gather_step([out_grad[1][:share], out_grad[1][share:]], 0)
    for step in range(1, len(high)):
        parts = gather_step(parts, step, after=last_parts)
    (base,) = weight_grad_of(place, turned[0], with_swapped(parts), (0, 1))
    for step in range(1, len(high)):
        last_parts = gather_step(last_parts, step, after=[base] if step == len(high) - 1 else None)
    swapped = [swap(part, "dp", 1) for part in last_parts]
    weight_grad, squares = weight_grad_of(
        place, turned[1], last_parts, (0,), base, None, weight_squares
    )
    weight_grad, squares = weight_grad_of(
        place, turned[1], swapped, (1,), base, weight_grad, squares
    )
    return update(sum_everywhere(squares), weight, velocity, weight_grad)


def solution(mesh):
    in_specs = (P(None, "dp", "feat"), P("dp", "feat"), P("dp", "feat"))
    out_specs = (P("dp", "feat"), P("dp", "feat"))
    return jax.shard_map(
        per_device, mesh=mesh, in_specs=in_specs, out_specs=out_specs, check_vma=False
    )
```

```python
import jax
import jax.numpy as jnp
from jax import lax
from jax.experimental import pallas as pl
from jax.experimental.pallas import tpu as pltpu
from jax.sharding import PartitionSpec as P

EPSILON = 1e-05
NORM_EPSILON = 1e-06
REDUNDANCY = 0.0051
MOMENTUM = 0.9
LEARN_RATE = 0.2
ROWS_BY_ROWS = (((1,), (1,)), ((), ()))
MIB = 1024 * 1024
F32, BF16 = jnp.float32, jnp.bfloat16


def swap(value, axis, mask):
    return lax.ppermute(value, axis, [(i, i ^ mask) for i in range(lax.axis_size(axis))])


def bit_value(axis, bit):
    return (lax.axis_index(axis) >> bit) & 1


def join(mine, other, bit):
    return jnp.where(
        bit == 0, jnp.concatenate([mine, other], 0), jnp.concatenate([other, mine], 0)
    )


def sum_everywhere(value):
    axes = ("dp", "feat")
    count = lax.axis_size(axes)
    parts = [value]
    for low in range(0, count.bit_length() - 1, 2):
        masks = [mask << low for mask in range(1, 4) if mask << low < count]
        value = sum(parts[1:], parts[0])
        parts = [value] + [
            lax.ppermute(value, axes, [(i, i ^ mask) for i in range(count)]) for mask in masks
        ]
    return parts


def whole(array):
    zeros = (0,) * array.ndim
    return pl.BlockSpec(array.shape, lambda *_: zeros, pipeline_mode=pl.Buffered(1))


def like(shape, kind):
    return jax.ShapeDtypeStruct(shape, kind)


def run(body, scalars, operands, in_specs, outs, out_specs, grid=(1,), scratch=(), after=(),
        flops=0, moved=0, limit=32, name=None, aliases=None):
    n_in, n_after = len(operands), len(after)

    def kernel(scalars_ref, *refs):
        body(scalars_ref, *refs[:n_in], *refs[n_in + n_after :])

    return pl.pallas_call(
        kernel,
        grid_spec=pltpu.PrefetchScalarGridSpec(
            num_scalar_prefetch=1,
            grid=grid,
            in_specs=list(in_specs) + [pl.BlockSpec(memory_space=pl.ANY)] * n_after,
            out_specs=list(out_specs),
            scratch_shapes=list(scratch),
        ),
        out_shape=list(outs),
        compiler_params=pltpu.CompilerParams(vmem_limit_bytes=limit * MIB),
        cost_estimate=pl.CostEstimate(flops=flops, bytes_accessed=moved, transcendentals=0),
        name=name,
        input_output_aliases=aliases or {},
    )(scalars, *operands, *after)


def fold(square):
    part = jnp.sum(square.reshape(-1, 8, square.shape[1]), 0)
    return sum(part[:, start : start + 128] for start in range(0, part.shape[1], 128))


def turn_weight(weight, core, after=()):
    depth, width = weight.shape
    quarter = width // 4
    step = min(256, quarter)
    steps = quarter // step

    def body(core_ref, weight_ref, sent_ref, kept_ref, square_ref):
        block = weight_ref[...]
        block_turned = block.T.astype(BF16)
        square = fold(block * block)
        first = (pl.program_id(0) == 0) & (pl.program_id(1) == 0)

        @pl.when(pl.program_id(0) == 0)
        def _():
            sent_ref[...] = block_turned

        @pl.when(pl.program_id(0) == 1)
        def _():
            kept_ref[...] = block_turned

        @pl.when(first)
        def _():
            square_ref[:8, :] = jnp.zeros_like(square)
            square_ref[8:, :] = square

        @pl.when(jnp.logical_not(first))
        def _():
            square_ref[8:, :] += square

    out = like((2 * quarter, depth), BF16)
    return run(
        body, core.reshape(1), [weight],
        [
            pl.BlockSpec(
                (depth, step),
                lambda k, j, c: (0, (2 * (j // steps) + (c[0] ^ (1 - k))) * steps + j % steps),
            )
        ],
        [out, out, like((16, 128), F32)],
        [
            pl.BlockSpec((step, depth), lambda k, j, c: (jnp.where(k == 0, j, 2 * steps - 1), 0)),
            pl.BlockSpec((step, depth), lambda k, j, c: (jnp.where(k == 1, j, 0), 0)),
            pl.BlockSpec((16, 128), lambda k, j, c: (0, 0)),
        ],
        grid=(2, 2 * steps), after=after, flops=2 * depth * width, moved=6 * depth * width, limit=16, name="turn_weight",
    )


def shares_of(view_features):
    _, count, width = view_features.shape
    half = count // 2

    def body(_, rows_ref, first_ref, low_ref, high_ref):
        low_ref[...] = rows_ref[1, :half, :]
        high_ref[...] = rows_ref[1, half:, :]
        first_ref[...] = rows_ref[0]

    outs = [like((rows, width), BF16) for rows in (count, half, half)]
    first, low, high = run(
        body, jnp.zeros((1,), jnp.int32), [view_features], [whole(view_features)],
        outs, [whole(out) for out in outs], moved=8 * count * width, limit=8, name="shares_of",
    )
    return [first], [low, high]


def go_round(parts):
    n_feat = lax.axis_size("feat")
    ring = [(i, (i + 1) % n_feat) for i in range(n_feat)]
    lists = [[part] for part in parts]
    for _ in range(1, n_feat):
        for shares in lists:
            shares.append(lax.ppermute(shares[-1], "feat", ring))
    return lists


def choose(shares, n_chip, after=()):
    n_feat = len(shares)
    chip = lax.axis_index("dp") >> 1
    back = [lax.rem(lax.axis_index("feat") - (chip ^ mask) + n_feat, n_feat) for mask in range(n_chip)]

    def body(back_ref, *refs):
        for mask in range(n_chip):
            for place in range(n_feat):

                @pl.when(back_ref[mask] == place)
                def _():
                    refs[n_feat + mask][...] = refs[place][...]

    shape = shares[0].shape
    return run(
        body, jnp.stack(back), shares, [whole(share) for share in shares],
        [like(shape, BF16)] * n_chip, [whole(shares[0])] * n_chip,
        after=after, moved=4 * n_chip * shape[0] * shape[1], limit=10, name="choose",
    )


def collect(place, own, after=()):
    n_part, n_chip = len(own), len(own[0])
    count, width = own[0][0].shape
    operands = [piece for pieces in own for piece in pieces]

    def body(place_ref, *refs):
        for part in range(n_part):
            for mask in range(n_chip):
                row = ((place_ref[0] ^ mask) * n_part + part) * count
                rows = pl.ds(pl.multiple_of(row, count), count)
                refs[-1][rows, :] = refs[part * n_chip + mask][...]

    out = like((len(operands) * count, width), BF16)
    (images,) = run(
        body, place, operands, [whole(piece) for piece in operands], [out], [whole(out)],
        after=after, moved=4 * len(operands) * count * width, limit=10, name="collect",
    )
    return images


def assemble(place, own, other, count, after=()):
    n_chip = own.shape[0] // count
    width = own.shape[1]
    half = width // 2

    def body(place_ref, own_ref, other_ref, out_ref):
        core = place_ref[1]
        for flip, ref in ((0, own_ref), (1, other_ref)):
            for chip in range(n_chip):
                rows = pl.ds(pl.multiple_of((chip * 2 + (core ^ flip)) * count, count), count)
                for side in range(2):
                    lane = pl.multiple_of((core ^ side) * half, half)
                    out_ref[rows, side * half : (side + 1) * half] = ref[
                        chip * count : (chip + 1) * count, pl.ds(lane, half)
                    ]

    out = like((2 * n_chip * count, width), BF16)
    (columns,) = run(
        body, place, [own, other], [whole(own), whole(other)], [out], [whole(out)], after=after,
        moved=8 * n_chip * count * width, limit=12, name="assemble",
    )
    return columns


def turn_columns(columns):
    batch, width = columns.shape
    depth = width // 2
    step = 256

    def body(_, columns_ref, out_ref):
        out_ref[...] = columns_ref[...].astype(F32).T.astype(BF16)

    (turned,) = run(
        body, jnp.zeros((1,), jnp.int32), [columns],
        [pl.BlockSpec((step, depth), lambda i, s: (i, 0))],
        [like((depth, batch), BF16)], [pl.BlockSpec((depth, step), lambda i, s: (0, i))],
        grid=(batch // step,), moved=4 * batch * depth, limit=8, name="turn_columns",
    )
    return turned


def forward(bits, turned_own, turned_other, columns, after=()):
    rows, depth = turned_own.shape
    batch = columns.shape[0]
    out_rows = rows // 4
    step = min(256, out_rows)
    steps = out_rows // step

    def body(bits_ref, own_a, other_a, own_b, other_b, columns_ref, out_a, out_b):
        own = jnp.concatenate([own_a[...], own_b[...]], 0)
        other = jnp.concatenate([other_a[...], other_b[...]], 0)
        block = lax.dot_general(
            own, columns_ref[:, :depth], ROWS_BY_ROWS, preferred_element_type=F32
        )
        block += lax.dot_general(
            other, columns_ref[:, depth:], ROWS_BY_ROWS, preferred_element_type=F32
        )
        block = (block - jnp.mean(block, 1, keepdims=True)).astype(BF16)
        out_a[...] = block[:step]
        out_b[...] = block[step:]

    def of_path(path):
        return pl.BlockSpec((step, depth), lambda i, b: ((2 * path + b[path]) * steps + i, 0))

    out_spec = pl.BlockSpec((step, batch), lambda i, b: (i, 0))
    return run(
        body, bits, [turned_own, turned_other, turned_own, turned_other, columns],
        [of_path(0), of_path(0), of_path(1), of_path(1), whole(columns)],
        [like((out_rows, batch), BF16)] * 2, [out_spec] * 2, grid=(steps,), after=after,
        flops=8 * out_rows * depth * batch, moved=8 * out_rows * depth + 4 * batch * depth, limit=22, name="forward",
    )


def add_halves(bits, kept, got, after=()):
    rows, batch = kept[0].shape
    half = rows // 2

    def body(bits_ref, kept_a, got_a, kept_b, got_b, send_a, send_b, keep_a, keep_b):
        for path, (kept_ref, got_ref, send_ref, keep_ref) in enumerate(
            ((kept_a, got_a, send_a, keep_a), (kept_b, got_b, send_b, keep_b))
        ):
            for flip, out_ref in ((1, send_ref), (0, keep_ref)):
                rows_of = pl.ds(pl.multiple_of((bits_ref[path] ^ flip) * half, half), half)
                total = kept_ref[rows_of, :].astype(F32) + got_ref[rows_of, :].astype(F32)
                out_ref[...] = total.astype(BF16)

    operands = [kept[0], got[0], kept[1], got[1]]
    out = like((half, batch), BF16)
    outs = run(
        body, bits, operands, [whole(one) for one in operands],
        [out] * 4, [whole(out)] * 4, after=after, moved=12 * rows * batch, limit=16, name="add_halves",
    )
    return outs[:2], outs[2:]


def normalise(kept, got, after=()):
    rows, batch = kept[0].shape

    def body(_, kept_a, got_a, kept_b, got_b, normed_ref, half_ref, inverse_ref):
        for path, (kept_ref, got_ref) in enumerate(((kept_a, got_a), (kept_b, got_b))):
            total = kept_ref[...].astype(F32) + got_ref[...].astype(F32)
            total -= jnp.mean(total, 1, keepdims=True)
            inverse = lax.rsqrt(jnp.mean(total * total, 1, keepdims=True) + EPSILON)
            normed = total * inverse
            place = slice(path * rows, (path + 1) * rows)
            normed_ref[place, :] = normed
            half_ref[place, :] = normed.astype(BF16)
            inverse_ref[place, :] = jnp.broadcast_to(inverse, (rows, 128))

    operands = [kept[0], got[0], kept[1], got[1]]
    outs = [like((2 * rows, width), kind) for width, kind in ((batch, F32), (batch, BF16), (128, F32))]
    return run(
        body, jnp.zeros((1,), jnp.int32), operands, [whole(one) for one in operands],
        outs, [whole(out) for out in outs], after=after, moved=20 * rows * batch, limit=16, name="normalise",
    )


def gram_rows(place, own, other, n_chip, after=()):
    rows, batch = own.shape
    blocks = 2 * n_chip
    size = batch // blocks
    width = (blocks // 2 + 1) * size

    def body(place_ref, own_ref, other_ref, *refs):
        twice_ref = refs[-1]
        for start, ref in ((0, own_ref), (rows, other_ref)):
            twice_ref[start : start + rows, :batch] = ref[...]
            twice_ref[start : start + rows, batch:] = ref[...]
        for mask in range(n_chip):
            row = pl.multiple_of(((place_ref[0] ^ mask) * 2 + place_ref[1]) * size, size)
            left = twice_ref[:, pl.ds(row, size)].astype(F32).T.astype(BF16)
            right = twice_ref[:, pl.ds(row, width)]
            refs[mask][...] = jnp.dot(left, right, preferred_element_type=F32).astype(BF16)

    out = like((size, width), BF16)
    return run(
        body, place, [own, other], [whole(own), whole(other)],
        [out] * n_chip, [whole(out)] * n_chip,
        scratch=[pltpu.VMEM((2 * rows, 2 * batch), BF16)], after=after,
        flops=4 * rows * width * batch // 2, moved=8 * rows * batch, limit=24, name="gram_rows",
    )


def join_all(mine, other, bits, after=()):
    count = len(mine)

    def body(bits_ref, *refs):
        for index in range(count):
            rows = mine[index].shape[0]
            bit = bits_ref[index]
            first = pl.multiple_of(bit * rows, rows)
            second = pl.multiple_of((1 - bit) * rows, rows)
            out_ref = refs[2 * count + index]
            out_ref[pl.ds(first, rows), :] = refs[index][...]
            out_ref[pl.ds(second, rows), :] = refs[count + index][...]

    outs = [like((2 * one.shape[0], one.shape[1]), BF16) for one in mine]
    return run(
        body, jnp.stack(bits), [*mine, *other], [whole(one) for one in [*mine, *other]],
        outs, [whole(out) for out in outs], after=after,
        moved=8 * sum(one.size for one in mine), limit=12, name="join_all",
    )


def add_up(parts, after=()):
    def body(_, *refs):
        total = refs[0][...].astype(F32)
        for ref in refs[1:-1]:
            total += ref[...].astype(F32)
        refs[-1][...] = total.astype(BF16)

    (out,) = run(
        body, jnp.zeros((1,), jnp.int32), parts, [whole(part) for part in parts],
        [like(parts[0].shape, BF16)], [whole(parts[0])], after=after,
        moved=4 * len(parts) * parts[0].size, limit=8, name="add_up",
    )
    return out


def pile(parts, after=()):
    rows, width = parts[0].shape

    def body(_, *refs):
        for index in range(len(parts)):
            refs[-1][index] = refs[index][...]

    out = like((len(parts), rows, width), BF16)
    (stack,) = run(
        body, jnp.zeros((1,), jnp.int32), parts, [whole(part) for part in parts],
        [out], [whole(out)], after=after, moved=4 * len(parts) * rows * width, limit=8, name="pile",
    )
    return stack


def out_grad_of(place, gram_own, gram_other, normed, half, half_other, inverse, after=()):
    rows, batch = half.shape
    n_chip = gram_own.shape[0]
    blocks = 2 * n_chip
    size = batch // blocks

    def body(place_ref, own_ref, other_ref, normed_ref, half_ref, half_other_ref, inverse_ref,
             out_ref, gram_ref):
        for flip, ref in ((0, own_ref), (1, other_ref)):
            for mask in range(n_chip):
                row = (place_ref[0] ^ mask) * 2 + (place_ref[1] ^ flip)
                down = pl.ds(pl.multiple_of(row * size, size), size)
                for ahead in range(blocks // 2 + 1):
                    col = lax.rem(row + ahead, blocks)
                    along = pl.ds(pl.multiple_of(col * size, size), size)
                    tile = ref[mask, :, ahead * size : (ahead + 1) * size]
                    gram_ref[down, along] = tile
                    if 0 < ahead < blocks // 2:
                        gram_ref[along, down] = tile.astype(F32).T.astype(BF16)
        normed = normed_ref[...]
        other = half_other_ref[...].astype(F32)
        diagonal = jnp.mean(half_ref[...].astype(F32) * other, 1, keepdims=True)
        extra = (-2.0 * (1.0 - diagonal) - 2.0 * REDUNDANCY * diagonal) / batch
        grads = lax.dot_general(
            half_ref[...], gram_ref[...], ROWS_BY_ROWS, preferred_element_type=F32
        )
        grads = grads * (2.0 * REDUNDANCY / (batch * batch)) + extra * other
        grad_mean = jnp.mean(grads, 1, keepdims=True)
        grad_cross = jnp.mean(grads * normed, 1, keepdims=True)
        out_ref[...] = (
            inverse_ref[:, :1] * (grads - grad_mean - normed * grad_cross)
        ).astype(BF16)

    operands = [gram_own, gram_other, normed, half, half_other, inverse]
    out = like((rows, batch), BF16)
    (out_grad,) = run(
        body, place, operands, [whole(one) for one in operands], [out], [whole(out)],
        scratch=[pltpu.VMEM((batch, batch), BF16)], after=after,
        flops=2 * rows * batch * batch, moved=12 * rows * batch + 2 * batch * batch, limit=24, name="out_grad_of",
    )
    return out_grad


def weight_grad_of(place, turned, pieces, flip, squares, done=None):
    depth, batch = turned[0].shape
    cols = pieces[0].shape[0]
    n_path = len(pieces) // 2

    def body(place_ref, first_ref, second_ref, *refs):
        square_in_ref = refs[len(pieces)]
        out_ref, square_ref = refs[-2:]
        for path in range(n_path):

            @pl.when(pl.program_id(0) == path)
            def _():
                total = lax.dot_general(
                    first_ref[...], refs[path][...], ROWS_BY_ROWS, preferred_element_type=F32
                )
                total += lax.dot_general(
                    second_ref[...], refs[n_path + path][...], ROWS_BY_ROWS,
                    preferred_element_type=F32,
                )
                if path == 0:
                    square_ref[...] = square_in_ref[...]
                square_ref[:8, :] += fold(total * total)
                out_ref[...] = total

    operands = [*turned, *pieces, squares] + ([] if done is None else [done])
    specs = [whole(one) for one in [*turned, *pieces, squares]]
    if done is not None:
        specs.append(pl.BlockSpec(memory_space=pl.ANY))
    return run(
        body, place, operands, specs,
        [like((depth, 2 * n_path * cols), F32), like(squares.shape, F32)],
        [
            pl.BlockSpec((depth, cols), lambda j, s: (0, 2 * j + (s[1] ^ flip))),
            pl.BlockSpec(squares.shape, lambda j, s: (0, 0)),
        ],
        grid=(n_path,), flops=4 * n_path * cols * batch * depth, moved=4 * n_path * depth * cols,
        limit=22, aliases={len(operands): 0} if done is not None else {}, name="weight_grad_of",
    )


def update(sums, weight, velocity, weight_grad):
    depth, width = weight.shape
    step = min(128, depth)
    n_sum = len(sums)

    def body(_, *refs):
        weight_ref, velocity_ref, grad_ref, new_weight_ref, new_velocity_ref = refs[n_sum:]
        total = refs[0][...]
        for ref in refs[1:n_sum]:
            total += ref[...]
        grad_norm = jnp.sqrt(jnp.sum(total[:8], keepdims=True))
        weight_norm = jnp.sqrt(jnp.sum(total[8:], keepdims=True))
        trust = weight_norm / (grad_norm + NORM_EPSILON)
        new_velocity = MOMENTUM * velocity_ref[...] + trust * grad_ref[...]
        new_velocity_ref[...] = new_velocity
        new_weight_ref[...] = weight_ref[...] - LEARN_RATE * new_velocity

    tile = pl.BlockSpec((step, width), lambda i, s: (i, 0))
    out = like((depth, width), F32)
    return run(
        body, jnp.zeros((1,), jnp.int32), [*sums, weight, velocity, weight_grad],
        [whole(one) for one in sums] + [tile] * 3, [out, out], [tile, tile],
        grid=(depth // step,), flops=4 * depth * width, moved=20 * depth * width, limit=16, name="update",
    )


def per_device(view_features, weight, velocity):
    n_dp, n_feat = lax.axis_size("dp"), lax.axis_size("feat")
    n_chip = n_dp // 2
    assert n_chip == n_feat and view_features.shape[2] == 2 * weight.shape[0]
    high = list(range(1, n_dp.bit_length() - 1))
    orders = (high, high[::-1])
    chip, core = lax.axis_index("dp") >> 1, bit_value("dp", 0)
    place = jnp.stack([chip, core])

    def bits_at(level):
        return jnp.stack([bit_value("dp", order[level]) for order in orders])

    shares = [go_round(parts) for parts in shares_of(view_features)]
    def cross_plane(part, after=()):
        own = list(choose(part, n_chip, after=after))
        for mask in range(1, n_chip):
            own[mask] = swap(own[mask], "dp", 2 * mask)
        return own

    def both_cores(images):
        return assemble(place, images, swap(images, "dp", 1), view_features.shape[1])

    def send_on(v, level, send):
        return [swap(send[p], "dp", 1 << orders[p][level]) for p in range(2)]

    def sum_plane(rows, after=()):
        others = [swap(rows[mask], "dp", 2 * mask) for mask in range(1, n_chip)]
        return add_up([rows[0], *others], after=after)

    def sum_line(total, bit, after=()):
        return add_up([total, swap(total, "feat", 1 << bit)], after=after)

    def spread_gram(total, after=()):
        parts = [total] + [swap(total, "dp", 2 * mask) for mask in range(1, n_chip)]
        own = pile(parts, after=after)
        return own, swap(own, "dp", 1)

    def gather_step(parts, step, after=()):
        bits = [order[len(order) - 1 - step] for order in orders] * (len(parts) // 2)
        other = [swap(part, "dp", 1 << bit) for part, bit in zip(parts, bits)]
        return join_all(parts, other, [bit_value("dp", bit) for bit in bits], after=after)

    def with_swapped(parts):
        return [one for own in parts for one in (own, swap(own, "dp", 1))]

    columns, turned, send, keep, got, gram, normed, half, inverse, rows = (
        [None] * 2 for _ in range(10)
    )
    bits = bits_at(0)
    line_bits = range(n_feat.bit_length() - 1)
    pieces = [cross_plane(part) for part in shares[1]]
    sent, turned_own, weight_squares = turn_weight(weight, core, after=[pieces[1][0]])
    turned_other = swap(sent, "dp", 1)
    images = collect(place, pieces, after=[turned_own, shares[0][0][-2]])
    columns[1] = both_cores(images)
    turned[1] = turn_columns(columns[1])
    images = collect(place, [cross_plane(part, [images]) for part in shares[0]])
    send[1] = forward(1 - bits, turned_own, turned_other, columns[1], after=[images])
    got[1] = send_on(1, 0, send[1])
    keep[1] = forward(bits, turned_own, turned_other, columns[1], after=[turned[1], send[1][0]])
    columns[0] = both_cores(images)
    turned[0] = turn_columns(columns[0])
    send[0] = forward(1 - bits, turned_own, turned_other, columns[0], after=[keep[1][0]])
    got[0] = send_on(0, 0, send[0])
    keep[0] = forward(bits, turned_own, turned_other, columns[0], after=[turned[0], send[0][0]])
    ahead = [keep[0][0]]
    for level in range(1, len(high)):
        for v in (1, 0):
            send[v], keep[v] = add_halves(bits_at(level), keep[v], got[v], after=ahead)
            got[v] = send_on(v, level, send[v])
            ahead = [send[v][0]]
    normed[1], half[1], inverse[1] = normalise(keep[1], got[1], after=ahead)
    rows[1] = list(gram_rows(place, half[1], swap(half[1], "dp", 1), n_chip))
    normed[0], half[0], inverse[0] = normalise(keep[0], got[0], after=[rows[1][0]])
    rows[0] = list(gram_rows(place, half[0], swap(half[0], "dp", 1), n_chip))
    gram[1] = sum_plane(rows[1], after=[rows[0][0]])
    gram[0] = sum_plane(rows[0], after=[gram[1]])
    for bit in line_bits:
        gram[1] = sum_line(gram[1], bit, after=[gram[0]])
        gram[0] = sum_line(gram[0], bit, after=[gram[1]])
    gram[0] = spread_gram(gram[0])
    gram[1] = spread_gram(gram[1], after=[gram[0][0]])
    out_grad = [None] * 2
    out_grad[0] = out_grad_of(place, *gram[1], normed[0], half[0], half[1], inverse[0])
    share = out_grad[0].shape[0] // 2
    out_grad[1] = out_grad_of(place, *gram[0], normed[1], half[1], half[0], inverse[1])
    parts = [one for grad in out_grad for one in (grad[:share], grad[share:])]
    for step in range(len(high)):
        parts = gather_step(parts, step)
    swapped = [swap(part, "dp", 1) for part in parts]
    weight_grad, squares = weight_grad_of(place, turned, parts, 0, weight_squares)
    weight_grad, squares = weight_grad_of(place, turned, swapped, 1, squares, weight_grad)
    return update(sum_everywhere(squares), weight, velocity, weight_grad)


def solution(mesh):
    in_specs = (P(None, "dp", "feat"), P("dp", "feat"), P("dp", "feat"))
    out_specs = (P("dp", "feat"), P("dp", "feat"))
    return jax.shard_map(
        per_device, mesh=mesh, in_specs=in_specs, out_specs=out_specs, check_vma=False
    )
```

```python
import jax
import jax.numpy as jnp
from jax import lax
from jax.experimental import pallas as pl
from jax.experimental.pallas import tpu as pltpu
from jax.sharding import PartitionSpec as P

EPSILON = 1e-05
NORM_EPSILON = 1e-06
REDUNDANCY = 0.0051
MOMENTUM = 0.9
LEARN_RATE = 0.2
ROWS_BY_ROWS = (((1,), (1,)), ((), ()))
MIB = 1024 * 1024
F32, BF16 = jnp.float32, jnp.bfloat16


def swap(value, axis, mask):
    return lax.ppermute(value, axis, [(i, i ^ mask) for i in range(lax.axis_size(axis))])


def bit_value(axis, bit):
    return (lax.axis_index(axis) >> bit) & 1


def join(mine, other, bit):
    return jnp.where(
        bit == 0, jnp.concatenate([mine, other], 0), jnp.concatenate([other, mine], 0)
    )


def sum_everywhere(value):
    axes = ("dp", "feat")
    count = lax.axis_size(axes)
    parts = [value]
    for low in range(0, count.bit_length() - 1, 2):
        masks = [mask << low for mask in range(1, 4) if mask << low < count]
        value = sum(parts[1:], parts[0])
        parts = [value] + [
            lax.ppermute(value, axes, [(i, i ^ mask) for i in range(count)]) for mask in masks
        ]
    return parts


def whole(array):
    zeros = (0,) * array.ndim
    return pl.BlockSpec(array.shape, lambda *_: zeros, pipeline_mode=pl.Buffered(1))


def like(shape, kind):
    return jax.ShapeDtypeStruct(shape, kind)


def run(body, scalars, operands, in_specs, outs, out_specs, grid=(1,), scratch=(), after=(),
        flops=0, moved=0, limit=32, name=None, aliases=None):
    n_in, n_after = len(operands), len(after)

    def kernel(scalars_ref, *refs):
        body(scalars_ref, *refs[:n_in], *refs[n_in + n_after :])

    return pl.pallas_call(
        kernel,
        grid_spec=pltpu.PrefetchScalarGridSpec(
            num_scalar_prefetch=1,
            grid=grid,
            in_specs=list(in_specs) + [pl.BlockSpec(memory_space=pl.ANY)] * n_after,
            out_specs=list(out_specs),
            scratch_shapes=list(scratch),
        ),
        out_shape=list(outs),
        compiler_params=pltpu.CompilerParams(vmem_limit_bytes=limit * MIB),
        cost_estimate=pl.CostEstimate(flops=flops, bytes_accessed=moved, transcendentals=0),
        name=name,
        input_output_aliases=aliases or {},
    )(scalars, *operands, *after)


def fold(square):
    part = jnp.sum(square.reshape(-1, 8, square.shape[1]), 0)
    return sum(part[:, start : start + 128] for start in range(0, part.shape[1], 128))


def turn_weight(weight, core, after=()):
    depth, width = weight.shape
    quarter = width // 4
    step = min(256, quarter)
    steps = quarter // step

    def body(core_ref, weight_ref, sent_ref, kept_ref, square_ref):
        block = weight_ref[...]
        block_turned = block.T.astype(BF16)
        square = fold(block * block)
        first = (pl.program_id(0) == 0) & (pl.program_id(1) == 0)

        @pl.when(pl.program_id(0) == 0)
        def _():
            sent_ref[...] = block_turned

        @pl.when(pl.program_id(0) == 1)
        def _():
            kept_ref[...] = block_turned

        @pl.when(first)
        def _():
            square_ref[:8, :] = jnp.zeros_like(square)
            square_ref[8:, :] = square

        @pl.when(jnp.logical_not(first))
        def _():
            square_ref[8:, :] += square

    out = like((2 * quarter, depth), BF16)
    return run(
        body, core.reshape(1), [weight],
        [
            pl.BlockSpec(
                (depth, step),
                lambda k, j, c: (0, (2 * (j // steps) + (c[0] ^ (1 - k))) * steps + j % steps),
            )
        ],
        [out, out, like((16, 128), F32)],
        [
            pl.BlockSpec((step, depth), lambda k, j, c: (jnp.where(k == 0, j, 2 * steps - 1), 0)),
            pl.BlockSpec((step, depth), lambda k, j, c: (jnp.where(k == 1, j, 0), 0)),
            pl.BlockSpec((16, 128), lambda k, j, c: (0, 0)),
        ],
        grid=(2, 2 * steps), after=after, flops=2 * depth * width, moved=6 * depth * width, limit=54, name="turn_weight",
    )


def shares_of(view_features):
    _, count, width = view_features.shape
    half = count // 2

    def body(_, rows_ref, first_ref, low_ref, high_ref):
        low_ref[...] = rows_ref[1, :half, :]
        high_ref[...] = rows_ref[1, half:, :]
        first_ref[...] = rows_ref[0]

    outs = [like((rows, width), BF16) for rows in (count, half, half)]
    first, low, high = run(
        body, jnp.zeros((1,), jnp.int32), [view_features], [whole(view_features)],
        outs, [whole(out) for out in outs], moved=8 * count * width, limit=8, name="shares_of",
    )
    return [first], [low, high]


def relay(value, after):
    def body(_, value_ref, out_ref):
        out_ref[...] = value_ref[...]

    (out,) = run(
        body, jnp.zeros((1,), jnp.int32), [value], [whole(value)], [like(value.shape, BF16)],
        [whole(value)], after=after, moved=4 * value.size, limit=8, name="relay",
    )
    return out


def ring_step(share):
    n_feat = lax.axis_size("feat")
    return lax.ppermute(share, "feat", [(i, (i + 1) % n_feat) for i in range(n_feat)])


def choose(shares, n_chip, after=()):
    n_feat = len(shares)
    chip = lax.axis_index("dp") >> 1
    back = [lax.rem(lax.axis_index("feat") - (chip ^ mask) + n_feat, n_feat) for mask in range(n_chip)]

    def body(back_ref, *refs):
        for mask in range(n_chip):
            for place in range(n_feat):

                @pl.when(back_ref[mask] == place)
                def _():
                    refs[n_feat + mask][...] = refs[place][...]

    shape = shares[0].shape
    return run(
        body, jnp.stack(back), shares, [whole(share) for share in shares],
        [like(shape, BF16)] * n_chip, [whole(shares[0])] * n_chip,
        after=after, moved=4 * n_chip * shape[0] * shape[1], limit=10, name="choose",
    )


def collect(place, own, after=()):
    n_part, n_chip = len(own), len(own[0])
    count, width = own[0][0].shape
    operands = [piece for pieces in own for piece in pieces]

    def body(place_ref, *refs):
        for part in range(n_part):
            for mask in range(n_chip):
                row = ((place_ref[0] ^ mask) * n_part + part) * count
                rows = pl.ds(pl.multiple_of(row, count), count)
                refs[-1][rows, :] = refs[part * n_chip + mask][...]

    out = like((len(operands) * count, width), BF16)
    (images,) = run(
        body, place, operands, [whole(piece) for piece in operands], [out], [whole(out)],
        after=after, moved=4 * len(operands) * count * width, limit=10, name="collect",
    )
    return images


def assemble(place, own, other, count, after=()):
    n_chip = own.shape[0] // count
    width = own.shape[1]
    half = width // 2

    def body(place_ref, own_ref, other_ref, out_ref):
        core = place_ref[1]
        for flip, ref in ((0, own_ref), (1, other_ref)):
            for chip in range(n_chip):
                rows = pl.ds(pl.multiple_of((chip * 2 + (core ^ flip)) * count, count), count)
                for side in range(2):
                    lane = pl.multiple_of((core ^ side) * half, half)
                    out_ref[rows, side * half : (side + 1) * half] = ref[
                        chip * count : (chip + 1) * count, pl.ds(lane, half)
                    ]

    out = like((2 * n_chip * count, width), BF16)
    (columns,) = run(
        body, place, [own, other], [whole(own), whole(other)], [out], [whole(out)], after=after,
        moved=8 * n_chip * count * width, limit=12, name="assemble",
    )
    return columns


def turn_columns(columns):
    batch, width = columns.shape
    depth = width // 2
    step = 256

    def body(_, columns_ref, out_ref):
        out_ref[...] = columns_ref[...].astype(F32).T.astype(BF16)

    (turned,) = run(
        body, jnp.zeros((1,), jnp.int32), [columns],
        [pl.BlockSpec((step, depth), lambda i, s: (i, 0))],
        [like((depth, batch), BF16)], [pl.BlockSpec((depth, step), lambda i, s: (0, i))],
        grid=(batch // step,), moved=4 * batch * depth, limit=8, name="turn_columns",
    )
    return turned


def forward(bits, turned_own, turned_other, columns, after=()):
    rows, depth = turned_own.shape
    batch = columns.shape[0]
    out_rows = rows // 4
    step = min(256, out_rows)
    steps = out_rows // step

    def body(bits_ref, own_a, other_a, own_b, other_b, columns_ref, out_a, out_b):
        own = jnp.concatenate([own_a[...], own_b[...]], 0)
        other = jnp.concatenate([other_a[...], other_b[...]], 0)
        block = lax.dot_general(
            own, columns_ref[:, :depth], ROWS_BY_ROWS, preferred_element_type=F32
        )
        block += lax.dot_general(
            other, columns_ref[:, depth:], ROWS_BY_ROWS, preferred_element_type=F32
        )
        block = (block - jnp.mean(block, 1, keepdims=True)).astype(BF16)
        out_a[...] = block[:step]
        out_b[...] = block[step:]

    def of_path(path):
        return pl.BlockSpec((step, depth), lambda i, b: ((2 * path + b[path]) * steps + i, 0))

    out_spec = pl.BlockSpec((step, batch), lambda i, b: (i, 0))
    return run(
        body, bits, [turned_own, turned_other, turned_own, turned_other, columns],
        [of_path(0), of_path(0), of_path(1), of_path(1), whole(columns)],
        [like((out_rows, batch), BF16)] * 2, [out_spec] * 2, grid=(steps,), after=after,
        flops=8 * out_rows * depth * batch, moved=8 * out_rows * depth + 4 * batch * depth, name="forward",
    )


def add_halves(bits, kept, got, after=()):
    rows, batch = kept[0].shape
    half = rows // 2

    def body(bits_ref, kept_a, got_a, kept_b, got_b, send_a, send_b, keep_a, keep_b):
        for path, (kept_ref, got_ref, send_ref, keep_ref) in enumerate(
            ((kept_a, got_a, send_a, keep_a), (kept_b, got_b, send_b, keep_b))
        ):
            for flip, out_ref in ((1, send_ref), (0, keep_ref)):
                rows_of = pl.ds(pl.multiple_of((bits_ref[path] ^ flip) * half, half), half)
                total = kept_ref[rows_of, :].astype(F32) + got_ref[rows_of, :].astype(F32)
                out_ref[...] = total.astype(BF16)

    operands = [kept[0], got[0], kept[1], got[1]]
    out = like((half, batch), BF16)
    outs = run(
        body, bits, operands, [whole(one) for one in operands],
        [out] * 4, [whole(out)] * 4, after=after, moved=12 * rows * batch, limit=16, name="add_halves",
    )
    return outs[:2], outs[2:]


def normalise(kept, got, after=()):
    rows, batch = kept[0].shape

    def body(_, kept_a, got_a, kept_b, got_b, normed_ref, half_ref, inverse_ref):
        for path, (kept_ref, got_ref) in enumerate(((kept_a, got_a), (kept_b, got_b))):
            total = kept_ref[...].astype(F32) + got_ref[...].astype(F32)
            total -= jnp.mean(total, 1, keepdims=True)
            inverse = lax.rsqrt(jnp.mean(total * total, 1, keepdims=True) + EPSILON)
            normed = total * inverse
            place = slice(path * rows, (path + 1) * rows)
            normed_ref[place, :] = normed
            half_ref[place, :] = normed.astype(BF16)
            inverse_ref[place, :] = jnp.broadcast_to(inverse, (rows, 128))

    operands = [kept[0], got[0], kept[1], got[1]]
    outs = [like((2 * rows, width), kind) for width, kind in ((batch, F32), (batch, BF16), (128, F32))]
    return run(
        body, jnp.zeros((1,), jnp.int32), operands, [whole(one) for one in operands],
        outs, [whole(out) for out in outs], after=after, moved=20 * rows * batch, limit=16, name="normalise",
    )


def gram_rows(place, own, other, n_chip, after=()):
    rows, batch = own.shape
    blocks = 2 * n_chip
    size = batch // blocks
    width = (blocks // 2 + 1) * size

    def body(place_ref, own_ref, other_ref, *refs):
        twice_ref = refs[-1]
        for start, ref in ((0, own_ref), (rows, other_ref)):
            twice_ref[start : start + rows, :batch] = ref[...]
            twice_ref[start : start + rows, batch:] = ref[...]
        for mask in range(n_chip):
            row = pl.multiple_of(((place_ref[0] ^ mask) * 2 + place_ref[1]) * size, size)
            left = twice_ref[:, pl.ds(row, size)].astype(F32).T.astype(BF16)
            right = twice_ref[:, pl.ds(row, width)]
            refs[mask][...] = jnp.dot(left, right, preferred_element_type=F32).astype(BF16)

    out = like((size, width), BF16)
    return run(
        body, place, [own, other], [whole(own), whole(other)],
        [out] * n_chip, [whole(out)] * n_chip,
        scratch=[pltpu.VMEM((2 * rows, 2 * batch), BF16)], after=after,
        flops=4 * rows * width * batch // 2, moved=8 * rows * batch, limit=24, name="gram_rows",
    )


def join_all(mine, other, bits, after=()):
    count = len(mine)

    def body(bits_ref, *refs):
        for index in range(count):
            rows = mine[index].shape[0]
            bit = bits_ref[index]
            first = pl.multiple_of(bit * rows, rows)
            second = pl.multiple_of((1 - bit) * rows, rows)
            out_ref = refs[2 * count + index]
            out_ref[pl.ds(first, rows), :] = refs[index][...]
            out_ref[pl.ds(second, rows), :] = refs[count + index][...]

    outs = [like((2 * one.shape[0], one.shape[1]), BF16) for one in mine]
    return run(
        body, jnp.stack(bits), [*mine, *other], [whole(one) for one in [*mine, *other]],
        outs, [whole(out) for out in outs], after=after,
        moved=8 * sum(one.size for one in mine), limit=12, name="join_all",
    )


def add_up(parts, after=()):
    def body(_, *refs):
        total = refs[0][...].astype(F32)
        for ref in refs[1:-1]:
            total += ref[...].astype(F32)
        refs[-1][...] = total.astype(BF16)

    (out,) = run(
        body, jnp.zeros((1,), jnp.int32), parts, [whole(part) for part in parts],
        [like(parts[0].shape, BF16)], [whole(parts[0])], after=after,
        moved=4 * len(parts) * parts[0].size, limit=8, name="add_up",
    )
    return out


def pile(parts, after=()):
    rows, width = parts[0].shape

    def body(_, *refs):
        for index in range(len(parts)):
            refs[-1][index] = refs[index][...]

    out = like((len(parts), rows, width), BF16)
    (stack,) = run(
        body, jnp.zeros((1,), jnp.int32), parts, [whole(part) for part in parts],
        [out], [whole(out)], after=after, moved=4 * len(parts) * rows * width, limit=8, name="pile",
    )
    return stack


def out_grad_of(place, gram_own, gram_other, normed, half, half_other, inverse, after=()):
    rows, batch = half.shape
    n_chip = gram_own.shape[0]
    blocks = 2 * n_chip
    size = batch // blocks

    def body(place_ref, own_ref, other_ref, normed_ref, half_ref, half_other_ref, inverse_ref,
             out_ref, gram_ref):
        for flip, ref in ((0, own_ref), (1, other_ref)):
            for mask in range(n_chip):
                row = (place_ref[0] ^ mask) * 2 + (place_ref[1] ^ flip)
                down = pl.ds(pl.multiple_of(row * size, size), size)
                for ahead in range(blocks // 2 + 1):
                    col = lax.rem(row + ahead, blocks)
                    along = pl.ds(pl.multiple_of(col * size, size), size)
                    tile = ref[mask, :, ahead * size : (ahead + 1) * size]
                    gram_ref[down, along] = tile
                    if 0 < ahead < blocks // 2:
                        gram_ref[along, down] = tile.astype(F32).T.astype(BF16)
        normed = normed_ref[...]
        other = half_other_ref[...].astype(F32)
        diagonal = jnp.mean(half_ref[...].astype(F32) * other, 1, keepdims=True)
        extra = (-2.0 * (1.0 - diagonal) - 2.0 * REDUNDANCY * diagonal) / batch
        grads = lax.dot_general(
            half_ref[...], gram_ref[...], ROWS_BY_ROWS, preferred_element_type=F32
        )
        grads = grads * (2.0 * REDUNDANCY / (batch * batch)) + extra * other
        grad_mean = jnp.mean(grads, 1, keepdims=True)
        grad_cross = jnp.mean(grads * normed, 1, keepdims=True)
        out_ref[...] = (
            inverse_ref[:, :1] * (grads - grad_mean - normed * grad_cross)
        ).astype(BF16)

    operands = [gram_own, gram_other, normed, half, half_other, inverse]
    out = like((rows, batch), BF16)
    (out_grad,) = run(
        body, place, operands, [whole(one) for one in operands], [out], [whole(out)],
        scratch=[pltpu.VMEM((batch, batch), BF16)], after=after,
        flops=2 * rows * batch * batch, moved=12 * rows * batch + 2 * batch * batch, limit=24, name="out_grad_of",
    )
    return out_grad


def weight_grad_of(place, turned, pieces, flip, squares, done=None):
    depth, batch = turned[0].shape
    cols = pieces[0].shape[0]
    n_path = len(pieces) // 2

    def body(place_ref, first_ref, second_ref, *refs):
        square_in_ref = refs[len(pieces)]
        out_ref, square_ref = refs[-2:]
        for path in range(n_path):

            @pl.when(pl.program_id(0) == path)
            def _():
                total = lax.dot_general(
                    first_ref[...], refs[path][...], ROWS_BY_ROWS, preferred_element_type=F32
                )
                total += lax.dot_general(
                    second_ref[...], refs[n_path + path][...], ROWS_BY_ROWS,
                    preferred_element_type=F32,
                )
                if path == 0:
                    square_ref[...] = square_in_ref[...]
                square_ref[:8, :] += fold(total * total)
                out_ref[...] = total

    operands = [*turned, *pieces, squares] + ([] if done is None else [done])
    specs = [whole(one) for one in [*turned, *pieces, squares]]
    if done is not None:
        specs.append(pl.BlockSpec(memory_space=pl.ANY))
    return run(
        body, place, operands, specs,
        [like((depth, 2 * n_path * cols), F32), like(squares.shape, F32)],
        [
            pl.BlockSpec((depth, cols), lambda j, s: (0, 2 * j + (s[1] ^ flip))),
            pl.BlockSpec(squares.shape, lambda j, s: (0, 0)),
        ],
        grid=(n_path,), flops=4 * n_path * cols * batch * depth, moved=4 * n_path * depth * cols,
        limit=22, aliases={len(operands): 0} if done is not None else {}, name="weight_grad_of",
    )


def update(sums, weight, velocity, weight_grad):
    depth, width = weight.shape
    step = min(128, depth)
    n_sum = len(sums)

    def body(_, *refs):
        weight_ref, velocity_ref, grad_ref, new_weight_ref, new_velocity_ref = refs[n_sum:]
        total = refs[0][...]
        for ref in refs[1:n_sum]:
            total += ref[...]
        grad_norm = jnp.sqrt(jnp.sum(total[:8], keepdims=True))
        weight_norm = jnp.sqrt(jnp.sum(total[8:], keepdims=True))
        trust = weight_norm / (grad_norm + NORM_EPSILON)
        new_velocity = MOMENTUM * velocity_ref[...] + trust * grad_ref[...]
        new_velocity_ref[...] = new_velocity
        new_weight_ref[...] = weight_ref[...] - LEARN_RATE * new_velocity

    tile = pl.BlockSpec((step, width), lambda i, s: (i, 0))
    out = like((depth, width), F32)
    return run(
        body, jnp.zeros((1,), jnp.int32), [*sums, weight, velocity, weight_grad],
        [whole(one) for one in sums] + [tile] * 3, [out, out], [tile, tile],
        grid=(depth // step,), flops=4 * depth * width, moved=20 * depth * width, limit=16, name="update",
    )


def per_device(view_features, weight, velocity):
    n_dp, n_feat = lax.axis_size("dp"), lax.axis_size("feat")
    n_chip = n_dp // 2
    assert n_chip == n_feat and view_features.shape[2] == 2 * weight.shape[0]
    high = list(range(1, n_dp.bit_length() - 1))
    orders = (high, high[::-1])
    chip, core = lax.axis_index("dp") >> 1, bit_value("dp", 0)
    place = jnp.stack([chip, core])

    def bits_at(level):
        return jnp.stack([bit_value("dp", order[level]) for order in orders])

    shares = [[[part] for part in parts] for parts in shares_of(view_features)]
    for step in range(1, n_feat):
        if step == 2:
            sent, turned_own, weight_squares = turn_weight(weight, core, after=[shares[1][0][-1]])
            shares[1][0][-1] = relay(shares[1][0][-1], [turned_own])
        for part in shares[1] + shares[0]:
            part.append(ring_step(part[-1]))
    turned_other = swap(sent, "dp", 1)

    def cross_plane(part, after=()):
        own = list(choose(part, n_chip, after=after))
        for mask in range(1, n_chip):
            own[mask] = swap(own[mask], "dp", 2 * mask)
        return own

    def both_cores(own, collect_after=(), after=()):
        images = collect(place, own, after=collect_after)
        other = swap(images, "dp", 1)
        return assemble(place, images, other, view_features.shape[1], after=after)

    def send_on(v, level, send):
        return [swap(send[p], "dp", 1 << orders[p][level]) for p in range(2)]

    def sum_plane(rows):
        total = rows[0].astype(F32)
        for mask in range(1, n_chip):
            total += swap(rows[mask], "dp", 2 * mask).astype(F32)
        return total.astype(BF16)

    def sum_line(total, bit):
        return (total.astype(F32) + swap(total, "feat", 1 << bit).astype(F32)).astype(BF16)

    def spread_gram(total, after=()):
        parts = [total] + [swap(total, "dp", 2 * mask) for mask in range(1, n_chip)]
        own = pile(parts, after=after)
        return own, swap(own, "dp", 1)

    def gather_step(parts, step, after=()):
        bits = [order[len(order) - 1 - step] for order in orders] * (len(parts) // 2)
        other = [swap(part, "dp", 1 << bit) for part, bit in zip(parts, bits)]
        return join_all(parts, other, [bit_value("dp", bit) for bit in bits], after=after)

    columns, turned, send, keep, got, gram, normed, half, inverse, rows = (
        [None] * 2 for _ in range(10)
    )
    bits = bits_at(0)
    line_bits = range(n_feat.bit_length() - 1)
    pieces = [cross_plane(part) for part in shares[1]]
    columns[1] = both_cores(pieces, collect_after=[turned_own, shares[0][0][-2]])
    turned[1] = turn_columns(columns[1])
    send[1] = forward(1 - bits, turned_own, turned_other, columns[1])
    got[1] = send_on(1, 0, send[1])
    pieces = [cross_plane(part, [send[1][0]]) for part in shares[0]]
    keep[1] = forward(bits, turned_own, turned_other, columns[1], after=[turned[1], send[1][0]])
    for level in range(1, len(high)):
        send[1], keep[1] = add_halves(bits_at(level), keep[1], got[1])
        got[1] = send_on(1, level, send[1])
    columns[0] = both_cores(pieces, [send[1][0]])
    turned[0] = turn_columns(columns[0])
    send[0] = forward(1 - bits, turned_own, turned_other, columns[0])
    ahead = [send[0][0]]
    got[0] = send_on(0, 0, send[0])
    normed[1], half[1], inverse[1] = normalise(keep[1], got[1], after=ahead)
    rows[1] = list(gram_rows(place, half[1], swap(half[1], "dp", 1), n_chip))
    keep[0] = forward(bits, turned_own, turned_other, columns[0], after=[turned[0], send[1][0]])
    for level in range(1, len(high)):
        send[0], keep[0] = add_halves(bits_at(level), keep[0], got[0], after=[rows[1][0]])
        got[0] = send_on(0, level, send[0])
    gram[1] = sum_plane(rows[1])
    normed[0], half[0], inverse[0] = normalise(keep[0], got[0], after=[gram[1]])
    rows[0] = list(gram_rows(place, half[0], swap(half[0], "dp", 1), n_chip))
    for bit in line_bits:
        gram[1] = sum_line(gram[1], bit)
    gram[1] = spread_gram(gram[1])
    gram[0] = sum_plane(rows[0])
    for bit in line_bits:
        gram[0] = sum_line(gram[0], bit)
    out_grad = [None] * 2
    out_grad[0] = out_grad_of(
        place, *gram[1], normed[0], half[0], half[1], inverse[0], after=[gram[0]]
    )
    gram[0] = spread_gram(gram[0], after=[out_grad[0]])
    share = out_grad[0].shape[0] // 2
    out_grad[1] = out_grad_of(place, *gram[0], normed[1], half[1], half[0], inverse[1])
    parts = [one for grad in out_grad for one in (grad[:share], grad[share:])]
    for step in range(len(high)):
        parts = gather_step(parts, step)
    swapped = [swap(part, "dp", 1) for part in parts]
    weight_grad, squares = weight_grad_of(place, turned, parts, 0, weight_squares)
    weight_grad, squares = weight_grad_of(place, turned, swapped, 1, squares, weight_grad)
    return update(sum_everywhere(squares), weight, velocity, weight_grad)


def solution(mesh):
    in_specs = (P(None, "dp", "feat"), P("dp", "feat"), P("dp", "feat"))
    out_specs = (P("dp", "feat"), P("dp", "feat"))
    return jax.shard_map(
        per_device, mesh=mesh, in_specs=in_specs, out_specs=out_specs, check_vma=False
    )
```

```python
import jax
import jax.numpy as jnp
from jax import lax
from jax.experimental import pallas as pl
from jax.experimental.pallas import tpu as pltpu
from jax.sharding import PartitionSpec as P

EPSILON = 1e-05
NORM_EPSILON = 1e-06
REDUNDANCY = 0.0051
MOMENTUM = 0.9
LEARN_RATE = 0.2
ROWS_BY_ROWS = (((1,), (1,)), ((), ()))
MIB = 1024 * 1024
F32, BF16 = jnp.float32, jnp.bfloat16


def swap(value, axis, mask):
    return lax.ppermute(value, axis, [(i, i ^ mask) for i in range(lax.axis_size(axis))])


def bit_value(axis, bit):
    return (lax.axis_index(axis) >> bit) & 1


def join(mine, other, bit):
    return jnp.where(
        bit == 0, jnp.concatenate([mine, other], 0), jnp.concatenate([other, mine], 0)
    )


def sum_everywhere(value):
    axes = ("dp", "feat")
    count = lax.axis_size(axes)
    parts = [value]
    for low in range(0, count.bit_length() - 1, 2):
        masks = [mask << low for mask in range(1, 4) if mask << low < count]
        value = sum(parts[1:], parts[0])
        parts = [value] + [
            lax.ppermute(value, axes, [(i, i ^ mask) for i in range(count)]) for mask in masks
        ]
    return parts


def whole(array):
    return None


def like(shape, kind):
    return jax.ShapeDtypeStruct(shape, kind)


def run(body, scalars, operands, in_specs, outs, out_specs, grid=None, scratch=(), after=(),
        flops=0, moved=0, limit=32, name=None, aliases=None):
    n_in, n_after = len(operands), len(after)
    unread = [pl.BlockSpec(memory_space=pl.ANY)] * n_after
    options = dict(
        out_shape=list(outs),
        compiler_params=pltpu.CompilerParams(vmem_limit_bytes=limit * MIB),
        cost_estimate=pl.CostEstimate(flops=flops, bytes_accessed=moved, transcendentals=0),
        input_output_aliases=aliases or {},
        name=name,
    )

    def kernel(scalars_ref, *refs):
        body(scalars_ref, *refs[:n_in], *refs[n_in + n_after :])

    if grid is None:
        inside = pl.BlockSpec(memory_space=pltpu.VMEM)
        in_specs = [spec or inside for spec in in_specs]
        out_specs = [spec or inside for spec in out_specs]
        call = pl.pallas_call(
            kernel, in_specs=[pl.BlockSpec(memory_space=pltpu.SMEM), *in_specs, *unread],
            out_specs=out_specs, scratch_shapes=list(scratch), **options,
        )
    else:
        call = pl.pallas_call(
            kernel,
            grid_spec=pltpu.PrefetchScalarGridSpec(
                num_scalar_prefetch=1, grid=grid, in_specs=list(in_specs) + unread,
                out_specs=list(out_specs), scratch_shapes=list(scratch),
            ),
            **options,
        )
    return call(scalars, *operands, *after)


def fold(square):
    part = jnp.sum(square.reshape(-1, 8, square.shape[1]), 0)
    return sum(part[:, start : start + 128] for start in range(0, part.shape[1], 128))


def turn_weight(weight, core, after=()):
    depth, width = weight.shape
    quarter = width // 4
    step = min(256, quarter)
    steps = quarter // step

    def body(core_ref, weight_ref, sent_ref, kept_ref, square_ref):
        block = weight_ref[...]
        block_turned = block.T.astype(BF16)
        square = fold(block * block)
        first = (pl.program_id(0) == 0) & (pl.program_id(1) == 0)

        @pl.when(pl.program_id(0) == 0)
        def _():
            sent_ref[...] = block_turned

        @pl.when(pl.program_id(0) == 1)
        def _():
            kept_ref[...] = block_turned

        @pl.when(first)
        def _():
            square_ref[:8, :] = jnp.zeros_like(square)
            square_ref[8:, :] = square

        @pl.when(jnp.logical_not(first))
        def _():
            square_ref[8:, :] += square

    out = like((2 * quarter, depth), BF16)
    return run(
        body, core.reshape(1), [weight],
        [
            pl.BlockSpec(
                (depth, step),
                lambda k, j, c: (0, (2 * (j // steps) + (c[0] ^ (1 - k))) * steps + j % steps),
            )
        ],
        [out, out, like((16, 128), F32)],
        [
            pl.BlockSpec((step, depth), lambda k, j, c: (jnp.where(k == 0, j, 2 * steps - 1), 0)),
            pl.BlockSpec((step, depth), lambda k, j, c: (jnp.where(k == 1, j, 0), 0)),
            pl.BlockSpec((16, 128), lambda k, j, c: (0, 0)),
        ],
        grid=(2, 2 * steps), after=after, flops=2 * depth * width, moved=6 * depth * width, limit=16, name="turn_weight",
    )


def shares_of(view_features):
    _, count, width = view_features.shape
    half = count // 2

    def body(_, rows_ref, first_ref, low_ref, high_ref):
        low_ref[...] = rows_ref[1, :half, :]
        high_ref[...] = rows_ref[1, half:, :]
        first_ref[...] = rows_ref[0]

    outs = [like((rows, width), BF16) for rows in (count, half, half)]
    first, low, high = run(
        body, jnp.zeros((1,), jnp.int32), [view_features], [whole(view_features)],
        outs, [whole(out) for out in outs], moved=8 * count * width, limit=8, name="shares_of",
    )
    return [first], [low, high]


def relay(value, after):
    def body(_, value_ref, out_ref):
        out_ref[...] = value_ref[...]

    (out,) = run(
        body, jnp.zeros((1,), jnp.int32), [value], [whole(value)], [like(value.shape, BF16)],
        [whole(value)], after=after, moved=4 * value.size, limit=8, name="relay",
    )
    return out


def ring_step(share):
    n_feat = lax.axis_size("feat")
    return lax.ppermute(share, "feat", [(i, (i + 1) % n_feat) for i in range(n_feat)])


def choose(shares, n_chip, after=()):
    n_feat = len(shares)
    chip = lax.axis_index("dp") >> 1
    back = [lax.rem(lax.axis_index("feat") - (chip ^ mask) + n_feat, n_feat) for mask in range(n_chip)]

    def body(back_ref, *refs):
        for mask in range(n_chip):
            for place in range(n_feat):

                @pl.when(back_ref[mask] == place)
                def _():
                    refs[n_feat + mask][...] = refs[place][...]

    shape = shares[0].shape
    return run(
        body, jnp.stack(back), shares, [whole(share) for share in shares],
        [like(shape, BF16)] * n_chip, [whole(shares[0])] * n_chip,
        after=after, moved=4 * n_chip * shape[0] * shape[1], limit=10, name="choose",
    )


def collect(place, own, after=()):
    n_part, n_chip = len(own), len(own[0])
    count, width = own[0][0].shape
    operands = [piece for pieces in own for piece in pieces]

    def body(place_ref, *refs):
        for part in range(n_part):
            for mask in range(n_chip):
                row = ((place_ref[0] ^ mask) * n_part + part) * count
                rows = pl.ds(pl.multiple_of(row, count), count)
                refs[-1][rows, :] = refs[part * n_chip + mask][...]

    out = like((len(operands) * count, width), BF16)
    (images,) = run(
        body, place, operands, [whole(piece) for piece in operands], [out], [whole(out)],
        after=after, moved=4 * len(operands) * count * width, limit=10, name="collect",
    )
    return images


def assemble(place, own, other, count, after=()):
    n_chip = own.shape[0] // count
    width = own.shape[1]
    half = width // 2

    def body(place_ref, own_ref, other_ref, out_ref):
        core = place_ref[1]
        for flip, ref in ((0, own_ref), (1, other_ref)):
            for chip in range(n_chip):
                rows = pl.ds(pl.multiple_of((chip * 2 + (core ^ flip)) * count, count), count)
                for side in range(2):
                    lane = pl.multiple_of((core ^ side) * half, half)
                    out_ref[rows, side * half : (side + 1) * half] = ref[
                        chip * count : (chip + 1) * count, pl.ds(lane, half)
                    ]

    out = like((2 * n_chip * count, width), BF16)
    (columns,) = run(
        body, place, [own, other], [whole(own), whole(other)], [out], [whole(out)], after=after,
        moved=8 * n_chip * count * width, limit=12, name="assemble",
    )
    return columns


def turn_columns(columns):
    batch, width = columns.shape
    depth = width // 2
    step = 256

    def body(_, columns_ref, out_ref):
        out_ref[...] = columns_ref[...].astype(F32).T.astype(BF16)

    (turned,) = run(
        body, jnp.zeros((1,), jnp.int32), [columns],
        [pl.BlockSpec((step, depth), lambda i, s: (i, 0))],
        [like((depth, batch), BF16)], [pl.BlockSpec((depth, step), lambda i, s: (0, i))],
        grid=(batch // step,), moved=4 * batch * depth, limit=8, name="turn_columns",
    )
    return turned


def forward(bits, turned_own, turned_other, columns, after=()):
    rows, depth = turned_own.shape
    batch = columns.shape[0]
    out_rows = rows // 4

    def body(bits_ref, own_ref, other_ref, columns_ref, out_a, out_b):
        starts = [pl.multiple_of((2 * p + bits_ref[p]) * out_rows, out_rows) for p in range(2)]
        own = jnp.concatenate([own_ref[pl.ds(start, out_rows), :] for start in starts], 0)
        other = jnp.concatenate([other_ref[pl.ds(start, out_rows), :] for start in starts], 0)
        block = lax.dot_general(
            own, columns_ref[:, :depth], ROWS_BY_ROWS, preferred_element_type=F32
        )
        block += lax.dot_general(
            other, columns_ref[:, depth:], ROWS_BY_ROWS, preferred_element_type=F32
        )
        block = (block - jnp.mean(block, 1, keepdims=True)).astype(BF16)
        out_a[...] = block[:out_rows]
        out_b[...] = block[out_rows:]

    return run(
        body, bits, [turned_own, turned_other, columns], [None] * 3,
        [like((out_rows, batch), BF16)] * 2, [None] * 2, after=after,
        flops=8 * out_rows * depth * batch, moved=8 * out_rows * depth + 4 * batch * depth,
        limit=16, name="forward",
    )


def add_halves(bits, kept, got, after=()):
    rows, batch = kept[0].shape
    half = rows // 2

    def body(bits_ref, kept_a, got_a, kept_b, got_b, send_a, send_b, keep_a, keep_b):
        for path, (kept_ref, got_ref, send_ref, keep_ref) in enumerate(
            ((kept_a, got_a, send_a, keep_a), (kept_b, got_b, send_b, keep_b))
        ):
            for flip, out_ref in ((1, send_ref), (0, keep_ref)):
                rows_of = pl.ds(pl.multiple_of((bits_ref[path] ^ flip) * half, half), half)
                total = kept_ref[rows_of, :].astype(F32) + got_ref[rows_of, :].astype(F32)
                out_ref[...] = total.astype(BF16)

    operands = [kept[0], got[0], kept[1], got[1]]
    out = like((half, batch), BF16)
    outs = run(
        body, bits, operands, [whole(one) for one in operands],
        [out] * 4, [whole(out)] * 4, after=after, moved=12 * rows * batch, limit=16, name="add_halves",
    )
    return outs[:2], outs[2:]


def normalise(kept, got, after=()):
    rows, batch = kept[0].shape

    def body(_, kept_a, got_a, kept_b, got_b, normed_ref, half_ref, inverse_ref):
        for path, (kept_ref, got_ref) in enumerate(((kept_a, got_a), (kept_b, got_b))):
            total = kept_ref[...].astype(F32) + got_ref[...].astype(F32)
            total -= jnp.mean(total, 1, keepdims=True)
            inverse = lax.rsqrt(jnp.mean(total * total, 1, keepdims=True) + EPSILON)
            normed = total * inverse
            place = slice(path * rows, (path + 1) * rows)
            normed_ref[place, :] = normed
            half_ref[place, :] = normed.astype(BF16)
            inverse_ref[place, :] = jnp.broadcast_to(inverse, (rows, 128))

    operands = [kept[0], got[0], kept[1], got[1]]
    outs = [like((2 * rows, width), kind) for width, kind in ((batch, F32), (batch, BF16), (128, F32))]
    return run(
        body, jnp.zeros((1,), jnp.int32), operands, [whole(one) for one in operands],
        outs, [whole(out) for out in outs], after=after, moved=20 * rows * batch, limit=16, name="normalise",
    )


def gram_rows(place, own, other, n_chip, after=()):
    rows, batch = own.shape
    blocks = 2 * n_chip
    size = batch // blocks
    width = (blocks // 2 + 1) * size

    def body(place_ref, own_ref, other_ref, *refs):
        twice_ref = refs[-1]
        for start, ref in ((0, own_ref), (rows, other_ref)):
            twice_ref[start : start + rows, :batch] = ref[...]
            twice_ref[start : start + rows, batch:] = ref[...]
        for mask in range(n_chip):
            row = pl.multiple_of(((place_ref[0] ^ mask) * 2 + place_ref[1]) * size, size)
            left = twice_ref[:, pl.ds(row, size)].astype(F32).T.astype(BF16)
            right = twice_ref[:, pl.ds(row, width)]
            refs[mask][...] = jnp.dot(left, right, preferred_element_type=F32).astype(BF16)

    out = like((size, width), BF16)
    return run(
        body, place, [own, other], [whole(own), whole(other)],
        [out] * n_chip, [whole(out)] * n_chip,
        scratch=[pltpu.VMEM((2 * rows, 2 * batch), BF16)], after=after,
        flops=4 * rows * width * batch // 2, moved=8 * rows * batch, limit=24, name="gram_rows",
    )


def join_all(mine, other, bits, after=()):
    count = len(mine)

    def body(bits_ref, *refs):
        for index in range(count):
            rows = mine[index].shape[0]
            bit = bits_ref[index]
            first = pl.multiple_of(bit * rows, rows)
            second = pl.multiple_of((1 - bit) * rows, rows)
            out_ref = refs[2 * count + index]
            out_ref[pl.ds(first, rows), :] = refs[index][...]
            out_ref[pl.ds(second, rows), :] = refs[count + index][...]

    outs = [like((2 * one.shape[0], one.shape[1]), BF16) for one in mine]
    return run(
        body, jnp.stack(bits), [*mine, *other], [whole(one) for one in [*mine, *other]],
        outs, [whole(out) for out in outs], after=after,
        moved=8 * sum(one.size for one in mine), limit=12, name="join_all",
    )


def add_up(parts, after=()):
    def body(_, *refs):
        total = refs[0][...].astype(F32)
        for ref in refs[1:-1]:
            total += ref[...].astype(F32)
        refs[-1][...] = total.astype(BF16)

    (out,) = run(
        body, jnp.zeros((1,), jnp.int32), parts, [whole(part) for part in parts],
        [like(parts[0].shape, BF16)], [whole(parts[0])], after=after,
        moved=4 * len(parts) * parts[0].size, limit=8, name="add_up",
    )
    return out


def pile(parts, after=()):
    rows, width = parts[0].shape

    def body(_, *refs):
        for index in range(len(parts)):
            refs[-1][index] = refs[index][...]

    out = like((len(parts), rows, width), BF16)
    (stack,) = run(
        body, jnp.zeros((1,), jnp.int32), parts, [whole(part) for part in parts],
        [out], [whole(out)], after=after, moved=4 * len(parts) * rows * width, limit=8, name="pile",
    )
    return stack


def out_grad_of(place, gram_own, gram_other, normed, half, half_other, inverse, after=()):
    rows, batch = half.shape
    n_chip = gram_own.shape[0]
    blocks = 2 * n_chip
    size = batch // blocks

    def body(place_ref, own_ref, other_ref, normed_ref, half_ref, half_other_ref, inverse_ref,
             out_ref, gram_ref):
        for flip, ref in ((0, own_ref), (1, other_ref)):
            for mask in range(n_chip):
                row = (place_ref[0] ^ mask) * 2 + (place_ref[1] ^ flip)
                down = pl.ds(pl.multiple_of(row * size, size), size)
                for ahead in range(blocks // 2 + 1):
                    col = lax.rem(row + ahead, blocks)
                    along = pl.ds(pl.multiple_of(col * size, size), size)
                    tile = ref[mask, :, ahead * size : (ahead + 1) * size]
                    gram_ref[down, along] = tile
                    if 0 < ahead < blocks // 2:
                        gram_ref[along, down] = tile.astype(F32).T.astype(BF16)
        normed = normed_ref[...]
        other = half_other_ref[...].astype(F32)
        diagonal = jnp.mean(half_ref[...].astype(F32) * other, 1, keepdims=True)
        extra = (-2.0 * (1.0 - diagonal) - 2.0 * REDUNDANCY * diagonal) / batch
        grads = lax.dot_general(
            half_ref[...], gram_ref[...], ROWS_BY_ROWS, preferred_element_type=F32
        )
        grads = grads * (2.0 * REDUNDANCY / (batch * batch)) + extra * other
        grad_mean = jnp.mean(grads, 1, keepdims=True)
        grad_cross = jnp.mean(grads * normed, 1, keepdims=True)
        out_ref[...] = (
            inverse_ref[:, :1] * (grads - grad_mean - normed * grad_cross)
        ).astype(BF16)

    operands = [gram_own, gram_other, normed, half, half_other, inverse]
    out = like((rows, batch), BF16)
    (out_grad,) = run(
        body, place, operands, [whole(one) for one in operands], [out], [whole(out)],
        scratch=[pltpu.VMEM((batch, batch), BF16)], after=after,
        flops=2 * rows * batch * batch, moved=12 * rows * batch + 2 * batch * batch, limit=24, name="out_grad_of",
    )
    return out_grad


def weight_grad_of(place, turned, pieces, flip, squares, done=None):
    depth, batch = turned[0].shape
    cols = pieces[0].shape[0]
    n_path = len(pieces) // 2

    def body(place_ref, first_ref, second_ref, *refs):
        square_in_ref = refs[len(pieces)]
        out_ref, square_ref, total_ref, sems = refs[-4:]
        core = place_ref[1]
        square_ref[...] = square_in_ref[...]
        copies = []
        for path in range(n_path):
            total = lax.dot_general(
                first_ref[...], refs[path][...], ROWS_BY_ROWS, preferred_element_type=F32
            )
            total += lax.dot_general(
                second_ref[...], refs[n_path + path][...], ROWS_BY_ROWS,
                preferred_element_type=F32,
            )
            total_ref[path] = total
            start = pl.multiple_of((2 * path + (core ^ flip)) * cols, cols)
            copies.append(
                pltpu.make_async_copy(
                    total_ref.at[path], out_ref.at[:, pl.ds(start, cols)], sems.at[path]
                )
            )
            copies[-1].start()
            square_ref[:8, :] += fold(total * total)
        for copy in copies:
            copy.wait()

    operands = [*turned, *pieces, squares] + ([] if done is None else [done])
    hbm = pl.BlockSpec(memory_space=pl.ANY)
    return run(
        body, place, operands, [None] * (3 + len(pieces)) + ([] if done is None else [hbm]),
        [like((depth, 2 * n_path * cols), F32), like(squares.shape, F32)], [hbm, None],
        scratch=[pltpu.VMEM((n_path, depth, cols), F32), pltpu.SemaphoreType.DMA((n_path,))],
        flops=4 * n_path * cols * batch * depth, moved=4 * n_path * depth * cols,
        limit=20, aliases={len(operands): 0} if done is not None else {}, name="weight_grad_of",
    )


def update(sums, weight, velocity, weight_grad):
    depth, width = weight.shape
    step = min(128, depth)
    n_sum = len(sums)

    def body(_, *refs):
        weight_ref, velocity_ref, grad_ref, new_weight_ref, new_velocity_ref = refs[n_sum:]
        total = refs[0][...]
        for ref in refs[1:n_sum]:
            total += ref[...]
        grad_norm = jnp.sqrt(jnp.sum(total[:8], keepdims=True))
        weight_norm = jnp.sqrt(jnp.sum(total[8:], keepdims=True))
        trust = weight_norm / (grad_norm + NORM_EPSILON)
        new_velocity = MOMENTUM * velocity_ref[...] + trust * grad_ref[...]
        new_velocity_ref[...] = new_velocity
        new_weight_ref[...] = weight_ref[...] - LEARN_RATE * new_velocity

    tile = pl.BlockSpec((step, width), lambda i, s: (i, 0))
    out = like((depth, width), F32)
    return run(
        body, jnp.zeros((1,), jnp.int32), [*sums, weight, velocity, weight_grad],
        [pl.BlockSpec(one.shape, lambda i, s: (0, 0)) for one in sums] + [tile] * 3, [out, out], [tile, tile],
        grid=(depth // step,), flops=4 * depth * width, moved=20 * depth * width, limit=16, name="update",
    )


def per_device(view_features, weight, velocity):
    n_dp, n_feat = lax.axis_size("dp"), lax.axis_size("feat")
    n_chip = n_dp // 2
    assert n_chip == n_feat and view_features.shape[2] == 2 * weight.shape[0]
    high = list(range(1, n_dp.bit_length() - 1))
    orders = (high, high[::-1])
    chip, core = lax.axis_index("dp") >> 1, bit_value("dp", 0)
    place = jnp.stack([chip, core])

    def bits_at(level):
        return jnp.stack([bit_value("dp", order[level]) for order in orders])

    shares = [[[part] for part in parts] for parts in shares_of(view_features)]
    for step in range(1, n_feat):
        if step == 2:
            sent, turned_own, weight_squares = turn_weight(weight, core, after=[shares[1][0][-1]])
            shares[1][0][-1] = relay(shares[1][0][-1], [turned_own])
        for part in shares[1] + shares[0]:
            part.append(ring_step(part[-1]))
    turned_other = swap(sent, "dp", 1)

    def cross_plane(part, after=()):
        own = list(choose(part, n_chip, after=after))
        for mask in range(1, n_chip):
            own[mask] = swap(own[mask], "dp", 2 * mask)
        return own

    def both_cores(own, collect_after=(), after=()):
        images = collect(place, own, after=collect_after)
        other = swap(images, "dp", 1)
        return assemble(place, images, other, view_features.shape[1], after=after)

    def send_on(v, level, send):
        return [swap(send[p], "dp", 1 << orders[p][level]) for p in range(2)]

    def sum_plane(rows):
        total = rows[0].astype(F32)
        for mask in range(1, n_chip):
            total += swap(rows[mask], "dp", 2 * mask).astype(F32)
        return total.astype(BF16)

    def sum_line(total, bit):
        return (total.astype(F32) + swap(total, "feat", 1 << bit).astype(F32)).astype(BF16)

    def spread_gram(total, after=()):
        parts = [total] + [swap(total, "dp", 2 * mask) for mask in range(1, n_chip)]
        own = pile(parts, after=after)
        return own, swap(own, "dp", 1)

    def gather_step(parts, step, after=()):
        bits = [order[len(order) - 1 - step] for order in orders] * (len(parts) // 2)
        other = [swap(part, "dp", 1 << bit) for part, bit in zip(parts, bits)]
        return join_all(parts, other, [bit_value("dp", bit) for bit in bits], after=after)

    columns, turned, send, keep, got, gram, normed, half, inverse, rows = (
        [None] * 2 for _ in range(10)
    )
    bits = bits_at(0)
    line_bits = range(n_feat.bit_length() - 1)
    pieces = [cross_plane(part) for part in shares[1]]
    columns[1] = both_cores(pieces, collect_after=[turned_own, shares[0][0][-2]])
    turned[1] = turn_columns(columns[1])
    send[1] = forward(1 - bits, turned_own, turned_other, columns[1])
    got[1] = send_on(1, 0, send[1])
    pieces = [cross_plane(part, [send[1][0]]) for part in shares[0]]
    keep[1] = forward(bits, turned_own, turned_other, columns[1], after=[turned[1], send[1][0]])
    for level in range(1, len(high)):
        send[1], keep[1] = add_halves(bits_at(level), keep[1], got[1])
        got[1] = send_on(1, level, send[1])
    columns[0] = both_cores(pieces, [send[1][0]])
    turned[0] = turn_columns(columns[0])
    send[0] = forward(1 - bits, turned_own, turned_other, columns[0])
    ahead = [send[0][0]]
    got[0] = send_on(0, 0, send[0])
    normed[1], half[1], inverse[1] = normalise(keep[1], got[1], after=ahead)
    rows[1] = list(gram_rows(place, half[1], swap(half[1], "dp", 1), n_chip))
    keep[0] = forward(bits, turned_own, turned_other, columns[0], after=[turned[0], send[1][0]])
    for level in range(1, len(high)):
        send[0], keep[0] = add_halves(bits_at(level), keep[0], got[0], after=[rows[1][0]])
        got[0] = send_on(0, level, send[0])
    gram[1] = sum_plane(rows[1])
    normed[0], half[0], inverse[0] = normalise(keep[0], got[0], after=[gram[1]])
    rows[0] = list(gram_rows(place, half[0], swap(half[0], "dp", 1), n_chip))
    for bit in line_bits:
        gram[1] = sum_line(gram[1], bit)
    gram[1] = spread_gram(gram[1])
    gram[0] = sum_plane(rows[0])
    for bit in line_bits:
        gram[0] = sum_line(gram[0], bit)
    out_grad = [None] * 2
    out_grad[0] = out_grad_of(
        place, *gram[1], normed[0], half[0], half[1], inverse[0], after=[gram[0]]
    )
    gram[0] = spread_gram(gram[0], after=[out_grad[0]])
    share = out_grad[0].shape[0] // 2
    out_grad[1] = out_grad_of(place, *gram[0], normed[1], half[1], half[0], inverse[1])
    parts = [one for grad in out_grad for one in (grad[:share], grad[share:])]
    for step in range(len(high)):
        parts = gather_step(parts, step)
    swapped = [swap(part, "dp", 1) for part in parts]
    weight_grad, squares = weight_grad_of(place, turned, parts, 0, weight_squares)
    weight_grad, squares = weight_grad_of(place, turned, swapped, 1, squares, weight_grad)
    return update(sum_everywhere(squares), weight, velocity, weight_grad)


def solution(mesh):
    in_specs = (P(None, "dp", "feat"), P("dp", "feat"), P("dp", "feat"))
    out_specs = (P("dp", "feat"), P("dp", "feat"))
    return jax.shard_map(
        per_device, mesh=mesh, in_specs=in_specs, out_specs=out_specs, check_vma=False
    )
```

```python
import jax
import jax.numpy as jnp
from jax import lax
from jax.experimental import pallas as pl
from jax.experimental.pallas import tpu as pltpu
from jax.sharding import PartitionSpec as P

EPSILON = 1e-05
NORM_EPSILON = 1e-06
REDUNDANCY = 0.0051
MOMENTUM = 0.9
LEARN_RATE = 0.2
ROWS_BY_ROWS = (((1,), (1,)), ((), ()))
MIB = 1024 * 1024
F32, BF16 = jnp.float32, jnp.bfloat16


def swap(value, axis, mask):
    return lax.ppermute(value, axis, [(i, i ^ mask) for i in range(lax.axis_size(axis))])


def bit_value(axis, bit):
    return (lax.axis_index(axis) >> bit) & 1


def join(mine, other, bit):
    return jnp.where(
        bit == 0, jnp.concatenate([mine, other], 0), jnp.concatenate([other, mine], 0)
    )


def sum_everywhere(value):
    axes = ("dp", "feat")
    count = lax.axis_size(axes)
    parts = [value]
    for low in range(0, count.bit_length() - 1, 2):
        masks = [mask << low for mask in range(1, 4) if mask << low < count]
        value = sum(parts[1:], parts[0])
        parts = [value] + [
            lax.ppermute(value, axes, [(i, i ^ mask) for i in range(count)]) for mask in masks
        ]
    return parts


def whole(array):
    return None


def like(shape, kind):
    return jax.ShapeDtypeStruct(shape, kind)


def run(body, scalars, operands, in_specs, outs, out_specs, grid=None, scratch=(), after=(),
        flops=0, moved=0, limit=32, name=None, aliases=None):
    n_in, n_after = len(operands), len(after)
    unread = [pl.BlockSpec(memory_space=pl.ANY)] * n_after
    options = dict(
        out_shape=list(outs),
        compiler_params=pltpu.CompilerParams(vmem_limit_bytes=limit * MIB),
        cost_estimate=pl.CostEstimate(flops=flops, bytes_accessed=moved, transcendentals=0),
        input_output_aliases=aliases or {},
        name=name,
    )

    def kernel(scalars_ref, *refs):
        body(scalars_ref, *refs[:n_in], *refs[n_in + n_after :])

    if grid is None:
        inside = pl.BlockSpec(memory_space=pltpu.VMEM)
        in_specs = [spec or inside for spec in in_specs]
        out_specs = [spec or inside for spec in out_specs]
        call = pl.pallas_call(
            kernel, in_specs=[pl.BlockSpec(memory_space=pltpu.SMEM), *in_specs, *unread],
            out_specs=out_specs, scratch_shapes=list(scratch), **options,
        )
    else:
        call = pl.pallas_call(
            kernel,
            grid_spec=pltpu.PrefetchScalarGridSpec(
                num_scalar_prefetch=1, grid=grid, in_specs=list(in_specs) + unread,
                out_specs=list(out_specs), scratch_shapes=list(scratch),
            ),
            **options,
        )
    return call(scalars, *operands, *after)


def fold(square):
    part = jnp.sum(square.reshape(-1, 8, square.shape[1]), 0)
    return sum(part[:, start : start + 128] for start in range(0, part.shape[1], 128))


def turn_weight(weight, core, after=()):
    depth, width = weight.shape
    quarter = width // 4
    step = min(256, quarter)
    steps = quarter // step

    def body(core_ref, weight_ref, sent_ref, kept_ref, square_ref):
        block = weight_ref[...]
        block_turned = block.T.astype(BF16)
        square = fold(block * block)
        first = (pl.program_id(0) == 0) & (pl.program_id(1) == 0)

        @pl.when(pl.program_id(0) == 0)
        def _():
            sent_ref[...] = block_turned

        @pl.when(pl.program_id(0) == 1)
        def _():
            kept_ref[...] = block_turned

        @pl.when(first)
        def _():
            square_ref[:8, :] = jnp.zeros_like(square)
            square_ref[8:, :] = square

        @pl.when(jnp.logical_not(first))
        def _():
            square_ref[8:, :] += square

    out = like((2 * quarter, depth), BF16)
    return run(
        body, core.reshape(1), [weight],
        [
            pl.BlockSpec(
                (depth, step),
                lambda k, j, c: (0, (2 * (j // steps) + (c[0] ^ (1 - k))) * steps + j % steps),
            )
        ],
        [out, out, like((16, 128), F32)],
        [
            pl.BlockSpec((step, depth), lambda k, j, c: (jnp.where(k == 0, j, 2 * steps - 1), 0)),
            pl.BlockSpec((step, depth), lambda k, j, c: (jnp.where(k == 1, j, 0), 0)),
            pl.BlockSpec((16, 128), lambda k, j, c: (0, 0)),
        ],
        grid=(2, 2 * steps), after=after, flops=2 * depth * width, moved=6 * depth * width, limit=16, name="turn_weight",
    )


def shares_of(view_features):
    _, count, width = view_features.shape
    half = count // 2

    def body(_, rows_ref, first_ref, low_ref, high_ref):
        low_ref[...] = rows_ref[1, :half, :]
        high_ref[...] = rows_ref[1, half:, :]
        first_ref[...] = rows_ref[0]

    outs = [like((rows, width), BF16) for rows in (count, half, half)]
    first, low, high = run(
        body, jnp.zeros((1,), jnp.int32), [view_features], [whole(view_features)],
        outs, [whole(out) for out in outs], moved=8 * count * width, limit=8, name="shares_of",
    )
    return [first], [low, high]


def relay(value, after):
    def body(_, value_ref, out_ref):
        out_ref[...] = value_ref[...]

    (out,) = run(
        body, jnp.zeros((1,), jnp.int32), [value], [whole(value)], [like(value.shape, BF16)],
        [whole(value)], after=after, moved=4 * value.size, limit=8, name="relay",
    )
    return out


def ring_step(share):
    n_feat = lax.axis_size("feat")
    return lax.ppermute(share, "feat", [(i, (i + 1) % n_feat) for i in range(n_feat)])


def choose(shares, n_chip, after=()):
    n_feat = len(shares)
    chip = lax.axis_index("dp") >> 1
    back = [lax.rem(lax.axis_index("feat") - (chip ^ mask) + n_feat, n_feat) for mask in range(n_chip)]

    def body(back_ref, *refs):
        for mask in range(n_chip):
            for place in range(n_feat):

                @pl.when(back_ref[mask] == place)
                def _():
                    refs[n_feat + mask][...] = refs[place][...]

    shape = shares[0].shape
    return run(
        body, jnp.stack(back), shares, [whole(share) for share in shares],
        [like(shape, BF16)] * n_chip, [whole(shares[0])] * n_chip,
        after=after, moved=4 * n_chip * shape[0] * shape[1], limit=10, name="choose",
    )


def collect(place, own, after=()):
    n_part, n_chip = len(own), len(own[0])
    count, width = own[0][0].shape
    operands = [piece for pieces in own for piece in pieces]

    def body(place_ref, *refs):
        for part in range(n_part):
            for mask in range(n_chip):
                row = ((place_ref[0] ^ mask) * n_part + part) * count
                rows = pl.ds(pl.multiple_of(row, count), count)
                refs[-1][rows, :] = refs[part * n_chip + mask][...]

    out = like((len(operands) * count, width), BF16)
    (images,) = run(
        body, place, operands, [whole(piece) for piece in operands], [out], [whole(out)],
        after=after, moved=4 * len(operands) * count * width, limit=10, name="collect",
    )
    return images


def assemble(place, own, other, count, after=()):
    n_chip = own.shape[0] // count
    width = own.shape[1]
    half = width // 2

    def body(place_ref, own_ref, other_ref, out_ref):
        core = place_ref[1]
        for flip, ref in ((0, own_ref), (1, other_ref)):
            for chip in range(n_chip):
                rows = pl.ds(pl.multiple_of((chip * 2 + (core ^ flip)) * count, count), count)
                for side in range(2):
                    lane = pl.multiple_of((core ^ side) * half, half)
                    out_ref[rows, side * half : (side + 1) * half] = ref[
                        chip * count : (chip + 1) * count, pl.ds(lane, half)
                    ]

    out = like((2 * n_chip * count, width), BF16)
    (columns,) = run(
        body, place, [own, other], [whole(own), whole(other)], [out], [whole(out)], after=after,
        moved=8 * n_chip * count * width, limit=12, name="assemble",
    )
    return columns


def turn_columns(columns):
    batch, width = columns.shape
    depth = width // 2
    step = 256

    def body(_, columns_ref, out_ref):
        out_ref[...] = columns_ref[...].astype(F32).T.astype(BF16)

    (turned,) = run(
        body, jnp.zeros((1,), jnp.int32), [columns],
        [pl.BlockSpec((step, depth), lambda i, s: (i, 0))],
        [like((depth, batch), BF16)], [pl.BlockSpec((depth, step), lambda i, s: (0, i))],
        grid=(batch // step,), moved=4 * batch * depth, limit=8, name="turn_columns",
    )
    return turned


def forward(bits, turned_own, turned_other, columns, after=()):
    rows, depth = turned_own.shape
    batch = columns.shape[0]
    out_rows = rows // 4

    def body(bits_ref, own_ref, other_ref, columns_ref, out_a, out_b):
        starts = [pl.multiple_of((2 * p + bits_ref[p]) * out_rows, out_rows) for p in range(2)]
        own = jnp.concatenate([own_ref[pl.ds(start, out_rows), :] for start in starts], 0)
        other = jnp.concatenate([other_ref[pl.ds(start, out_rows), :] for start in starts], 0)
        block = lax.dot_general(
            own, columns_ref[:, :depth], ROWS_BY_ROWS, preferred_element_type=F32
        )
        block += lax.dot_general(
            other, columns_ref[:, depth:], ROWS_BY_ROWS, preferred_element_type=F32
        )
        block = (block - jnp.mean(block, 1, keepdims=True)).astype(BF16)
        out_a[...] = block[:out_rows]
        out_b[...] = block[out_rows:]

    return run(
        body, bits, [turned_own, turned_other, columns], [None] * 3,
        [like((out_rows, batch), BF16)] * 2, [None] * 2, after=after,
        flops=8 * out_rows * depth * batch, moved=8 * out_rows * depth + 4 * batch * depth,
        limit=16, name="forward",
    )


def add_halves(bits, kept, got, after=()):
    rows, batch = kept[0].shape
    half = rows // 2

    def body(bits_ref, kept_a, got_a, kept_b, got_b, send_a, send_b, keep_a, keep_b):
        for path, (kept_ref, got_ref, send_ref, keep_ref) in enumerate(
            ((kept_a, got_a, send_a, keep_a), (kept_b, got_b, send_b, keep_b))
        ):
            for flip, out_ref in ((1, send_ref), (0, keep_ref)):
                rows_of = pl.ds(pl.multiple_of((bits_ref[path] ^ flip) * half, half), half)
                total = kept_ref[rows_of, :].astype(F32) + got_ref[rows_of, :].astype(F32)
                out_ref[...] = total.astype(BF16)

    operands = [kept[0], got[0], kept[1], got[1]]
    out = like((half, batch), BF16)
    outs = run(
        body, bits, operands, [whole(one) for one in operands],
        [out] * 4, [whole(out)] * 4, after=after, moved=12 * rows * batch, limit=16, name="add_halves",
    )
    return outs[:2], outs[2:]


def normalise(kept, got, after=()):
    rows, batch = kept[0].shape

    def body(_, kept_a, got_a, kept_b, got_b, normed_ref, half_ref, inverse_ref):
        for path, (kept_ref, got_ref) in enumerate(((kept_a, got_a), (kept_b, got_b))):
            total = kept_ref[...].astype(F32) + got_ref[...].astype(F32)
            total -= jnp.mean(total, 1, keepdims=True)
            inverse = lax.rsqrt(jnp.mean(total * total, 1, keepdims=True) + EPSILON)
            normed = total * inverse
            place = slice(path * rows, (path + 1) * rows)
            normed_ref[place, :] = normed
            half_ref[place, :] = normed.astype(BF16)
            inverse_ref[place, :] = jnp.broadcast_to(inverse, (rows, 128))

    operands = [kept[0], got[0], kept[1], got[1]]
    outs = [like((2 * rows, width), kind) for width, kind in ((batch, F32), (batch, BF16), (128, F32))]
    return run(
        body, jnp.zeros((1,), jnp.int32), operands, [whole(one) for one in operands],
        outs, [whole(out) for out in outs], after=after, moved=20 * rows * batch, limit=16, name="normalise",
    )


def gram_rows(place, own, other, n_chip, after=()):
    rows, batch = own.shape
    blocks = 2 * n_chip
    size = batch // blocks
    width = (blocks // 2 + 1) * size

    def body(place_ref, own_ref, other_ref, *refs):
        twice_ref = refs[-1]
        for start, ref in ((0, own_ref), (rows, other_ref)):
            twice_ref[start : start + rows, :batch] = ref[...]
            twice_ref[start : start + rows, batch:] = ref[...]
        for mask in range(n_chip):
            row = pl.multiple_of(((place_ref[0] ^ mask) * 2 + place_ref[1]) * size, size)
            left = twice_ref[:, pl.ds(row, size)].astype(F32).T.astype(BF16)
            right = twice_ref[:, pl.ds(row, width)]
            refs[mask][...] = jnp.dot(left, right, preferred_element_type=F32).astype(BF16)

    out = like((size, width), BF16)
    return run(
        body, place, [own, other], [whole(own), whole(other)],
        [out] * n_chip, [whole(out)] * n_chip,
        scratch=[pltpu.VMEM((2 * rows, 2 * batch), BF16)], after=after,
        flops=4 * rows * width * batch // 2, moved=8 * rows * batch, limit=24, name="gram_rows",
    )


def join_all(mine, other, bits, after=()):
    count = len(mine)

    def body(bits_ref, *refs):
        for index in range(count):
            rows = mine[index].shape[0]
            bit = bits_ref[index]
            first = pl.multiple_of(bit * rows, rows)
            second = pl.multiple_of((1 - bit) * rows, rows)
            out_ref = refs[2 * count + index]
            out_ref[pl.ds(first, rows), :] = refs[index][...]
            out_ref[pl.ds(second, rows), :] = refs[count + index][...]

    outs = [like((2 * one.shape[0], one.shape[1]), BF16) for one in mine]
    return run(
        body, jnp.stack(bits), [*mine, *other], [whole(one) for one in [*mine, *other]],
        outs, [whole(out) for out in outs], after=after,
        moved=8 * sum(one.size for one in mine), limit=12, name="join_all",
    )


def add_up(parts, after=()):
    def body(_, *refs):
        total = refs[0][...].astype(F32)
        for ref in refs[1:-1]:
            total += ref[...].astype(F32)
        refs[-1][...] = total.astype(BF16)

    (out,) = run(
        body, jnp.zeros((1,), jnp.int32), parts, [whole(part) for part in parts],
        [like(parts[0].shape, BF16)], [whole(parts[0])], after=after,
        moved=4 * len(parts) * parts[0].size, limit=8, name="add_up",
    )
    return out


def pile(parts, after=()):
    rows, width = parts[0].shape

    def body(_, *refs):
        for index in range(len(parts)):
            refs[-1][index] = refs[index][...]

    out = like((len(parts), rows, width), BF16)
    (stack,) = run(
        body, jnp.zeros((1,), jnp.int32), parts, [whole(part) for part in parts],
        [out], [whole(out)], after=after, moved=4 * len(parts) * rows * width, limit=8, name="pile",
    )
    return stack


def out_grad_of(place, gram_own, gram_other, normed, half, half_other, inverse, after=()):
    rows, batch = half.shape
    n_chip = gram_own.shape[0]
    blocks = 2 * n_chip
    size = batch // blocks

    def body(place_ref, own_ref, other_ref, normed_ref, half_ref, half_other_ref, inverse_ref,
             out_ref, gram_ref):
        for flip, ref in ((0, own_ref), (1, other_ref)):
            for mask in range(n_chip):
                row = (place_ref[0] ^ mask) * 2 + (place_ref[1] ^ flip)
                down = pl.ds(pl.multiple_of(row * size, size), size)
                for ahead in range(blocks // 2 + 1):
                    col = lax.rem(row + ahead, blocks)
                    along = pl.ds(pl.multiple_of(col * size, size), size)
                    tile = ref[mask, :, ahead * size : (ahead + 1) * size]
                    gram_ref[down, along] = tile
                    if 0 < ahead < blocks // 2:
                        gram_ref[along, down] = tile.astype(F32).T.astype(BF16)
        normed = normed_ref[...]
        other = half_other_ref[...].astype(F32)
        diagonal = jnp.mean(half_ref[...].astype(F32) * other, 1, keepdims=True)
        extra = (-2.0 * (1.0 - diagonal) - 2.0 * REDUNDANCY * diagonal) / batch
        grads = lax.dot_general(
            half_ref[...], gram_ref[...], ROWS_BY_ROWS, preferred_element_type=F32
        )
        grads = grads * (2.0 * REDUNDANCY / (batch * batch)) + extra * other
        grad_mean = jnp.mean(grads, 1, keepdims=True)
        grad_cross = jnp.mean(grads * normed, 1, keepdims=True)
        out_ref[...] = (
            inverse_ref[:, :1] * (grads - grad_mean - normed * grad_cross)
        ).astype(BF16)

    operands = [gram_own, gram_other, normed, half, half_other, inverse]
    out = like((rows, batch), BF16)
    (out_grad,) = run(
        body, place, operands, [whole(one) for one in operands], [out], [whole(out)],
        scratch=[pltpu.VMEM((batch, batch), BF16)], after=after,
        flops=2 * rows * batch * batch, moved=12 * rows * batch + 2 * batch * batch, limit=24, name="out_grad_of",
    )
    return out_grad


def weight_grad_of(place, turned, pieces, flip, squares, done=None):
    depth, batch = turned[0].shape
    cols = pieces[0].shape[0]
    n_path = len(pieces) // 2

    def body(place_ref, first_ref, second_ref, *refs):
        square_in_ref = refs[len(pieces)]
        out_ref, square_ref = refs[-2:]
        core = place_ref[1]
        square_ref[...] = square_in_ref[...]
        for path in range(n_path):
            total = lax.dot_general(
                first_ref[...], refs[path][...], ROWS_BY_ROWS, preferred_element_type=F32
            )
            total += lax.dot_general(
                second_ref[...], refs[n_path + path][...], ROWS_BY_ROWS,
                preferred_element_type=F32,
            )
            start = pl.multiple_of((2 * path + (core ^ flip)) * cols, cols)
            out_ref[:, pl.ds(start, cols)] = total
            square_ref[:8, :] += fold(total * total)

    operands = [*turned, *pieces, squares] + ([] if done is None else [done])
    return run(
        body, place, operands, [None] * len(operands),
        [like((depth, 2 * n_path * cols), F32), like(squares.shape, F32)], [None, None],
        flops=4 * n_path * cols * batch * depth, moved=4 * n_path * depth * cols,
        limit=16, aliases={len(operands): 0} if done is not None else {}, name="weight_grad_of",
    )


def update(sums, weight, velocity, weight_grad):
    depth, width = weight.shape
    step = min(128, depth)
    n_sum = len(sums)

    def body(_, *refs):
        weight_ref, velocity_ref, grad_ref, new_weight_ref, new_velocity_ref = refs[n_sum:]
        total = refs[0][...]
        for ref in refs[1:n_sum]:
            total += ref[...]
        grad_norm = jnp.sqrt(jnp.sum(total[:8], keepdims=True))
        weight_norm = jnp.sqrt(jnp.sum(total[8:], keepdims=True))
        trust = weight_norm / (grad_norm + NORM_EPSILON)
        new_velocity = MOMENTUM * velocity_ref[...] + trust * grad_ref[...]
        new_velocity_ref[...] = new_velocity
        new_weight_ref[...] = weight_ref[...] - LEARN_RATE * new_velocity

    tile = pl.BlockSpec((step, width), lambda i, s: (i, 0))
    out = like((depth, width), F32)
    return run(
        body, jnp.zeros((1,), jnp.int32), [*sums, weight, velocity, weight_grad],
        [pl.BlockSpec(one.shape, lambda i, s: (0, 0)) for one in sums] + [tile] * 3, [out, out], [tile, tile],
        grid=(depth // step,), flops=4 * depth * width, moved=20 * depth * width, limit=16, name="update",
    )


def per_device(view_features, weight, velocity):
    n_dp, n_feat = lax.axis_size("dp"), lax.axis_size("feat")
    n_chip = n_dp // 2
    assert n_chip == n_feat and view_features.shape[2] == 2 * weight.shape[0]
    high = list(range(1, n_dp.bit_length() - 1))
    orders = (high, high[::-1])
    chip, core = lax.axis_index("dp") >> 1, bit_value("dp", 0)
    place = jnp.stack([chip, core])

    def bits_at(level):
        return jnp.stack([bit_value("dp", order[level]) for order in orders])

    shares = [[[part] for part in parts] for parts in shares_of(view_features)]
    for step in range(1, n_feat):
        if step == 2:
            sent, turned_own, weight_squares = turn_weight(weight, core, after=[shares[1][0][-1]])
            shares[1][0][-1] = relay(shares[1][0][-1], [turned_own])
        for part in shares[1] + shares[0]:
            part.append(ring_step(part[-1]))
    turned_other = swap(sent, "dp", 1)

    def cross_plane(part, after=()):
        own = list(choose(part, n_chip, after=after))
        for mask in range(1, n_chip):
            own[mask] = swap(own[mask], "dp", 2 * mask)
        return own

    def both_cores(own, collect_after=(), after=()):
        images = collect(place, own, after=collect_after)
        other = swap(images, "dp", 1)
        return assemble(place, images, other, view_features.shape[1], after=after)

    def send_on(v, level, send):
        return [swap(send[p], "dp", 1 << orders[p][level]) for p in range(2)]

    def sum_plane(rows):
        total = rows[0].astype(F32)
        for mask in range(1, n_chip):
            total += swap(rows[mask], "dp", 2 * mask).astype(F32)
        return total.astype(BF16)

    def sum_line(total, bit):
        return (total.astype(F32) + swap(total, "feat", 1 << bit).astype(F32)).astype(BF16)

    def spread_gram(total, after=()):
        parts = [total] + [swap(total, "dp", 2 * mask) for mask in range(1, n_chip)]
        own = pile(parts, after=after)
        return own, swap(own, "dp", 1)

    def gather_step(parts, step, after=()):
        bits = [order[len(order) - 1 - step] for order in orders] * (len(parts) // 2)
        other = [swap(part, "dp", 1 << bit) for part, bit in zip(parts, bits)]
        return join_all(parts, other, [bit_value("dp", bit) for bit in bits], after=after)

    columns, turned, send, keep, got, gram, normed, half, inverse, rows = (
        [None] * 2 for _ in range(10)
    )
    bits = bits_at(0)
    line_bits = range(n_feat.bit_length() - 1)
    pieces = [cross_plane(part) for part in shares[1]]
    columns[1] = both_cores(pieces, collect_after=[turned_own, shares[0][0][-2]])
    turned[1] = turn_columns(columns[1])
    send[1] = forward(1 - bits, turned_own, turned_other, columns[1])
    got[1] = send_on(1, 0, send[1])
    pieces = [cross_plane(part, [send[1][0]]) for part in shares[0]]
    keep[1] = forward(bits, turned_own, turned_other, columns[1], after=[turned[1], send[1][0]])
    for level in range(1, len(high)):
        send[1], keep[1] = add_halves(bits_at(level), keep[1], got[1])
        got[1] = send_on(1, level, send[1])
    columns[0] = both_cores(pieces, [send[1][0]])
    turned[0] = turn_columns(columns[0])
    send[0] = forward(1 - bits, turned_own, turned_other, columns[0])
    ahead = [send[0][0]]
    got[0] = send_on(0, 0, send[0])
    normed[1], half[1], inverse[1] = normalise(keep[1], got[1], after=ahead)
    rows[1] = list(gram_rows(place, half[1], swap(half[1], "dp", 1), n_chip))
    keep[0] = forward(bits, turned_own, turned_other, columns[0], after=[turned[0], send[1][0]])
    for level in range(1, len(high)):
        send[0], keep[0] = add_halves(bits_at(level), keep[0], got[0], after=[rows[1][0]])
        got[0] = send_on(0, level, send[0])
    gram[1] = sum_plane(rows[1])
    normed[0], half[0], inverse[0] = normalise(keep[0], got[0], after=[gram[1]])
    rows[0] = list(gram_rows(place, half[0], swap(half[0], "dp", 1), n_chip))
    for bit in line_bits:
        gram[1] = sum_line(gram[1], bit)
    gram[1] = spread_gram(gram[1])
    gram[0] = sum_plane(rows[0])
    for bit in line_bits:
        gram[0] = sum_line(gram[0], bit)
    out_grad = [None] * 2
    out_grad[0] = out_grad_of(
        place, *gram[1], normed[0], half[0], half[1], inverse[0], after=[gram[0]]
    )
    gram[0] = spread_gram(gram[0], after=[out_grad[0]])
    share = out_grad[0].shape[0] // 2
    out_grad[1] = out_grad_of(place, *gram[0], normed[1], half[1], half[0], inverse[1])
    parts = [one for grad in out_grad for one in (grad[:share], grad[share:])]
    for step in range(len(high)):
        parts = gather_step(parts, step)
    swapped = [swap(part, "dp", 1) for part in parts]
    weight_grad, squares = weight_grad_of(place, turned, parts, 0, weight_squares)
    weight_grad, squares = weight_grad_of(place, turned, swapped, 1, squares, weight_grad)
    return update(sum_everywhere(squares), weight, velocity, weight_grad)


def solution(mesh):
    in_specs = (P(None, "dp", "feat"), P("dp", "feat"), P("dp", "feat"))
    out_specs = (P("dp", "feat"), P("dp", "feat"))
    return jax.shard_map(
        per_device, mesh=mesh, in_specs=in_specs, out_specs=out_specs, check_vma=False
    )
```

```python
import jax
import jax.numpy as jnp
from jax import lax
from jax.experimental import pallas as pl
from jax.experimental.pallas import tpu as pltpu
from jax.sharding import PartitionSpec as P

EPSILON = 1e-05
NORM_EPSILON = 1e-06
REDUNDANCY = 0.0051
MOMENTUM = 0.9
LEARN_RATE = 0.2
ROWS_BY_ROWS = (((1,), (1,)), ((), ()))
MIB = 1024 * 1024
F32, BF16 = jnp.float32, jnp.bfloat16


def swap(value, axis, mask):
    return lax.ppermute(value, axis, [(i, i ^ mask) for i in range(lax.axis_size(axis))])


def bit_value(axis, bit):
    return (lax.axis_index(axis) >> bit) & 1


def join(mine, other, bit):
    return jnp.where(
        bit == 0, jnp.concatenate([mine, other], 0), jnp.concatenate([other, mine], 0)
    )


def sum_everywhere(value):
    axes = ("dp", "feat")
    count = lax.axis_size(axes)
    parts = [value]
    for low in range(0, count.bit_length() - 1, 2):
        masks = [mask << low for mask in range(1, 4) if mask << low < count]
        value = sum(parts[1:], parts[0])
        parts = [value] + [
            lax.ppermute(value, axes, [(i, i ^ mask) for i in range(count)]) for mask in masks
        ]
    return parts


def whole(array):
    return None


def like(shape, kind):
    return jax.ShapeDtypeStruct(shape, kind)


def run(body, scalars, operands, in_specs, outs, out_specs, grid=None, scratch=(), after=(),
        flops=0, moved=0, limit=32, name=None, aliases=None):
    n_in, n_after = len(operands), len(after)
    unread = [pl.BlockSpec(memory_space=pl.ANY)] * n_after
    options = dict(
        out_shape=list(outs),
        compiler_params=pltpu.CompilerParams(vmem_limit_bytes=limit * MIB),
        cost_estimate=pl.CostEstimate(flops=flops, bytes_accessed=moved, transcendentals=0),
        input_output_aliases=aliases or {},
        name=name,
    )

    def kernel(scalars_ref, *refs):
        body(scalars_ref, *refs[:n_in], *refs[n_in + n_after :])

    if grid is None:
        inside = pl.BlockSpec(memory_space=pltpu.VMEM)
        in_specs = [spec or inside for spec in in_specs]
        out_specs = [spec or inside for spec in out_specs]
        call = pl.pallas_call(
            kernel, in_specs=[pl.BlockSpec(memory_space=pltpu.SMEM), *in_specs, *unread],
            out_specs=out_specs, scratch_shapes=list(scratch), **options,
        )
    else:
        call = pl.pallas_call(
            kernel,
            grid_spec=pltpu.PrefetchScalarGridSpec(
                num_scalar_prefetch=1, grid=grid, in_specs=list(in_specs) + unread,
                out_specs=list(out_specs), scratch_shapes=list(scratch),
            ),
            **options,
        )
    return call(scalars, *operands, *after)


def fold(square):
    part = jnp.sum(square.reshape(-1, 8, square.shape[1]), 0)
    return sum(part[:, start : start + 128] for start in range(0, part.shape[1], 128))


def turn_weight(weight, core, after=()):
    depth, width = weight.shape
    quarter = width // 4
    step = min(256, quarter)
    steps = quarter // step

    def body(core_ref, weight_ref, sent_ref, kept_ref, square_ref):
        block = weight_ref[...]
        block_turned = block.T.astype(BF16)
        square = fold(block * block)
        first = (pl.program_id(0) == 0) & (pl.program_id(1) == 0)

        @pl.when(pl.program_id(0) == 0)
        def _():
            sent_ref[...] = block_turned

        @pl.when(pl.program_id(0) == 1)
        def _():
            kept_ref[...] = block_turned

        @pl.when(first)
        def _():
            square_ref[:8, :] = jnp.zeros_like(square)
            square_ref[8:, :] = square

        @pl.when(jnp.logical_not(first))
        def _():
            square_ref[8:, :] += square

    out = like((2 * quarter, depth), BF16)
    return run(
        body, core.reshape(1), [weight],
        [
            pl.BlockSpec(
                (depth, step),
                lambda k, j, c: (0, (2 * (j // steps) + (c[0] ^ (1 - k))) * steps + j % steps),
            )
        ],
        [out, out, like((16, 128), F32)],
        [
            pl.BlockSpec((step, depth), lambda k, j, c: (jnp.where(k == 0, j, 2 * steps - 1), 0)),
            pl.BlockSpec((step, depth), lambda k, j, c: (jnp.where(k == 1, j, 0), 0)),
            pl.BlockSpec((16, 128), lambda k, j, c: (0, 0)),
        ],
        grid=(2, 2 * steps), after=after, flops=2 * depth * width, moved=6 * depth * width, limit=16, name="turn_weight",
    )


def shares_of(view_features):
    _, count, width = view_features.shape
    half = count // 2

    def body(_, rows_ref, first_ref, low_ref, high_ref):
        low_ref[...] = rows_ref[1, :half, :]
        high_ref[...] = rows_ref[1, half:, :]
        first_ref[...] = rows_ref[0]

    outs = [like((rows, width), BF16) for rows in (count, half, half)]
    first, low, high = run(
        body, jnp.zeros((1,), jnp.int32), [view_features], [whole(view_features)],
        outs, [whole(out) for out in outs], moved=8 * count * width, limit=8, name="shares_of",
    )
    return [first], [low, high]


def relay(value, after):
    def body(_, value_ref, out_ref):
        out_ref[...] = value_ref[...]

    (out,) = run(
        body, jnp.zeros((1,), jnp.int32), [value], [whole(value)], [like(value.shape, BF16)],
        [whole(value)], after=after, moved=4 * value.size, limit=8, name="relay",
    )
    return out


def ring_step(share):
    n_feat = lax.axis_size("feat")
    return lax.ppermute(share, "feat", [(i, (i + 1) % n_feat) for i in range(n_feat)])


def choose(shares, n_chip, after=()):
    n_feat = len(shares)
    chip = lax.axis_index("dp") >> 1
    back = [lax.rem(lax.axis_index("feat") - (chip ^ mask) + n_feat, n_feat) for mask in range(n_chip)]

    def body(back_ref, *refs):
        for mask in range(n_chip):
            for place in range(n_feat):

                @pl.when(back_ref[mask] == place)
                def _():
                    refs[n_feat + mask][...] = refs[place][...]

    shape = shares[0].shape
    return run(
        body, jnp.stack(back), shares, [whole(share) for share in shares],
        [like(shape, BF16)] * n_chip, [whole(shares[0])] * n_chip,
        after=after, moved=4 * n_chip * shape[0] * shape[1], limit=10, name="choose",
    )


def collect(place, own, after=()):
    n_part, n_chip = len(own), len(own[0])
    count, width = own[0][0].shape
    operands = [piece for pieces in own for piece in pieces]

    def body(place_ref, *refs):
        for part in range(n_part):
            for mask in range(n_chip):
                row = ((place_ref[0] ^ mask) * n_part + part) * count
                rows = pl.ds(pl.multiple_of(row, count), count)
                refs[-1][rows, :] = refs[part * n_chip + mask][...]

    out = like((len(operands) * count, width), BF16)
    (images,) = run(
        body, place, operands, [whole(piece) for piece in operands], [out], [whole(out)],
        after=after, moved=4 * len(operands) * count * width, limit=10, name="collect",
    )
    return images


def assemble(place, own, other, count, after=()):
    n_chip = own.shape[0] // count
    width = own.shape[1]
    half = width // 2

    def body(place_ref, own_ref, other_ref, out_ref):
        core = place_ref[1]
        for flip, ref in ((0, own_ref), (1, other_ref)):
            for chip in range(n_chip):
                rows = pl.ds(pl.multiple_of((chip * 2 + (core ^ flip)) * count, count), count)
                for side in range(2):
                    lane = pl.multiple_of((core ^ side) * half, half)
                    out_ref[rows, side * half : (side + 1) * half] = ref[
                        chip * count : (chip + 1) * count, pl.ds(lane, half)
                    ]

    out = like((2 * n_chip * count, width), BF16)
    (columns,) = run(
        body, place, [own, other], [whole(own), whole(other)], [out], [whole(out)], after=after,
        moved=8 * n_chip * count * width, limit=12, name="assemble",
    )
    return columns


def turn_columns(columns):
    batch, width = columns.shape
    depth = width // 2
    step = 256

    def body(_, columns_ref, out_ref):
        out_ref[...] = columns_ref[...].astype(F32).T.astype(BF16)

    (turned,) = run(
        body, jnp.zeros((1,), jnp.int32), [columns],
        [pl.BlockSpec((step, depth), lambda i, s: (i, 0))],
        [like((depth, batch), BF16)], [pl.BlockSpec((depth, step), lambda i, s: (0, i))],
        grid=(batch // step,), moved=4 * batch * depth, limit=8, name="turn_columns",
    )
    return turned


def forward(bits, turned_own, turned_other, columns, after=()):
    rows, depth = turned_own.shape
    batch = columns.shape[0]
    out_rows = rows // 4

    def body(bits_ref, own_ref, other_ref, columns_ref, out_a, out_b):
        starts = [pl.multiple_of((2 * p + bits_ref[p]) * out_rows, out_rows) for p in range(2)]
        own = jnp.concatenate([own_ref[pl.ds(start, out_rows), :] for start in starts], 0)
        other = jnp.concatenate([other_ref[pl.ds(start, out_rows), :] for start in starts], 0)
        block = lax.dot_general(
            own, columns_ref[:, :depth], ROWS_BY_ROWS, preferred_element_type=F32
        )
        block += lax.dot_general(
            other, columns_ref[:, depth:], ROWS_BY_ROWS, preferred_element_type=F32
        )
        block = (block - jnp.mean(block, 1, keepdims=True)).astype(BF16)
        out_a[...] = block[:out_rows]
        out_b[...] = block[out_rows:]

    return run(
        body, bits, [turned_own, turned_other, columns], [None] * 3,
        [like((out_rows, batch), BF16)] * 2, [None] * 2, after=after,
        flops=8 * out_rows * depth * batch, moved=8 * out_rows * depth + 4 * batch * depth,
        limit=16, name="forward",
    )


def add_halves(bits, kept, got, after=()):
    rows, batch = kept[0].shape
    half = rows // 2

    def body(bits_ref, kept_a, got_a, kept_b, got_b, send_a, send_b, keep_a, keep_b):
        for path, (kept_ref, got_ref, send_ref, keep_ref) in enumerate(
            ((kept_a, got_a, send_a, keep_a), (kept_b, got_b, send_b, keep_b))
        ):
            for flip, out_ref in ((1, send_ref), (0, keep_ref)):
                rows_of = pl.ds(pl.multiple_of((bits_ref[path] ^ flip) * half, half), half)
                total = kept_ref[rows_of, :].astype(F32) + got_ref[rows_of, :].astype(F32)
                out_ref[...] = total.astype(BF16)

    operands = [kept[0], got[0], kept[1], got[1]]
    out = like((half, batch), BF16)
    outs = run(
        body, bits, operands, [whole(one) for one in operands],
        [out] * 4, [whole(out)] * 4, after=after, moved=12 * rows * batch, limit=16, name="add_halves",
    )
    return outs[:2], outs[2:]


def normalise(kept, got, after=()):
    rows, batch = kept[0].shape

    def body(_, kept_a, got_a, kept_b, got_b, normed_ref, half_ref, inverse_ref):
        for path, (kept_ref, got_ref) in enumerate(((kept_a, got_a), (kept_b, got_b))):
            total = kept_ref[...].astype(F32) + got_ref[...].astype(F32)
            total -= jnp.mean(total, 1, keepdims=True)
            inverse = lax.rsqrt(jnp.mean(total * total, 1, keepdims=True) + EPSILON)
            normed = total * inverse
            place = slice(path * rows, (path + 1) * rows)
            normed_ref[place, :] = normed
            half_ref[place, :] = normed.astype(BF16)
            inverse_ref[place, :] = jnp.broadcast_to(inverse, (rows, 128))

    operands = [kept[0], got[0], kept[1], got[1]]
    outs = [like((2 * rows, width), kind) for width, kind in ((batch, F32), (batch, BF16), (128, F32))]
    return run(
        body, jnp.zeros((1,), jnp.int32), operands, [whole(one) for one in operands],
        outs, [whole(out) for out in outs], after=after, moved=20 * rows * batch, limit=16, name="normalise",
    )


def gram_rows(place, own, other, n_chip, after=()):
    rows, batch = own.shape
    blocks = 2 * n_chip
    size = batch // blocks
    width = (blocks // 2 + 1) * size

    def body(place_ref, own_ref, other_ref, *refs):
        twice_ref = refs[-1]
        for start, ref in ((0, own_ref), (rows, other_ref)):
            twice_ref[start : start + rows, :batch] = ref[...]
            twice_ref[start : start + rows, batch:] = ref[...]
        for mask in range(n_chip):
            row = pl.multiple_of(((place_ref[0] ^ mask) * 2 + place_ref[1]) * size, size)
            left = twice_ref[:, pl.ds(row, size)].astype(F32).T.astype(BF16)
            right = twice_ref[:, pl.ds(row, width)]
            refs[mask][...] = jnp.dot(left, right, preferred_element_type=F32).astype(BF16)

    out = like((size, width), BF16)
    return run(
        body, place, [own, other], [whole(own), whole(other)],
        [out] * n_chip, [whole(out)] * n_chip,
        scratch=[pltpu.VMEM((2 * rows, 2 * batch), BF16)], after=after,
        flops=4 * rows * width * batch // 2, moved=8 * rows * batch, limit=24, name="gram_rows",
    )


def join_all(mine, other, bits, after=()):
    count = len(mine)

    def body(bits_ref, *refs):
        for index in range(count):
            rows = mine[index].shape[0]
            bit = bits_ref[index]
            first = pl.multiple_of(bit * rows, rows)
            second = pl.multiple_of((1 - bit) * rows, rows)
            out_ref = refs[2 * count + index]
            out_ref[pl.ds(first, rows), :] = refs[index][...]
            out_ref[pl.ds(second, rows), :] = refs[count + index][...]

    outs = [like((2 * one.shape[0], one.shape[1]), BF16) for one in mine]
    return run(
        body, jnp.stack(bits), [*mine, *other], [whole(one) for one in [*mine, *other]],
        outs, [whole(out) for out in outs], after=after,
        moved=8 * sum(one.size for one in mine), limit=12, name="join_all",
    )


def add_up(parts, after=()):
    def body(_, *refs):
        total = refs[0][...].astype(F32)
        for ref in refs[1:-1]:
            total += ref[...].astype(F32)
        refs[-1][...] = total.astype(BF16)

    (out,) = run(
        body, jnp.zeros((1,), jnp.int32), parts, [whole(part) for part in parts],
        [like(parts[0].shape, BF16)], [whole(parts[0])], after=after,
        moved=4 * len(parts) * parts[0].size, limit=8, name="add_up",
    )
    return out


def pile(parts, after=()):
    rows, width = parts[0].shape

    def body(_, *refs):
        for index in range(len(parts)):
            refs[-1][index] = refs[index][...]

    out = like((len(parts), rows, width), BF16)
    (stack,) = run(
        body, jnp.zeros((1,), jnp.int32), parts, [whole(part) for part in parts],
        [out], [whole(out)], after=after, moved=4 * len(parts) * rows * width, limit=8, name="pile",
    )
    return stack


def out_grad_of(place, gram_own, gram_other, normed, half, half_other, inverse, after=()):
    rows, batch = half.shape
    n_chip = gram_own.shape[0]
    blocks = 2 * n_chip
    size = batch // blocks

    def body(place_ref, own_ref, other_ref, normed_ref, half_ref, half_other_ref, inverse_ref,
             out_ref, gram_ref):
        for flip, ref in ((0, own_ref), (1, other_ref)):
            for mask in range(n_chip):
                row = (place_ref[0] ^ mask) * 2 + (place_ref[1] ^ flip)
                down = pl.ds(pl.multiple_of(row * size, size), size)
                for ahead in range(blocks // 2 + 1):
                    col = lax.rem(row + ahead, blocks)
                    along = pl.ds(pl.multiple_of(col * size, size), size)
                    tile = ref[mask, :, ahead * size : (ahead + 1) * size]
                    gram_ref[down, along] = tile
                    if 0 < ahead < blocks // 2:
                        gram_ref[along, down] = tile.astype(F32).T.astype(BF16)
        normed = normed_ref[...]
        other = half_other_ref[...].astype(F32)
        diagonal = jnp.mean(half_ref[...].astype(F32) * other, 1, keepdims=True)
        extra = (-2.0 * (1.0 - diagonal) - 2.0 * REDUNDANCY * diagonal) / batch
        grads = lax.dot_general(
            half_ref[...], gram_ref[...], ROWS_BY_ROWS, preferred_element_type=F32
        )
        grads = grads * (2.0 * REDUNDANCY / (batch * batch)) + extra * other
        grad_mean = jnp.mean(grads, 1, keepdims=True)
        grad_cross = jnp.mean(grads * normed, 1, keepdims=True)
        out_ref[...] = (
            inverse_ref[:, :1] * (grads - grad_mean - normed * grad_cross)
        ).astype(BF16)

    operands = [gram_own, gram_other, normed, half, half_other, inverse]
    out = like((rows, batch), BF16)
    (out_grad,) = run(
        body, place, operands, [whole(one) for one in operands], [out], [whole(out)],
        scratch=[pltpu.VMEM((batch, batch), BF16)], after=after,
        flops=2 * rows * batch * batch, moved=12 * rows * batch + 2 * batch * batch, limit=24, name="out_grad_of",
    )
    return out_grad


def weight_grad_of(place, views, flip, squares=None, done=None, add=False):
    depth, batch = views[0][0].shape
    n_path = len(views[0][1])
    cols = views[0][1][0].shape[0]
    operands = [one for turned, pieces in views for one in (turned, *pieces)]
    n_product = len(operands)

    def body(place_ref, *refs):
        n_out = 1 if squares is None else 2
        out_ref = refs[-n_out]
        core = place_ref[1]
        if squares is not None:
            square_ref = refs[-1]
            square_ref[...] = refs[n_product][...]
        for path in range(n_path):
            start = pl.multiple_of((2 * path + (core ^ flip)) * cols, cols)
            place_of = (slice(None), pl.ds(start, cols))
            total = refs[-n_out - 1][place_of] if add else None
            for first in range(0, n_product, n_path + 1):
                product = lax.dot_general(
                    refs[first][...], refs[first + 1 + path][...], ROWS_BY_ROWS,
                    preferred_element_type=F32,
                )
                total = product if total is None else total + product
            out_ref[place_of] = total
            if squares is not None:
                square_ref[:8, :] += fold(total * total)

    operands += [one for one in (squares, done) if one is not None]
    out = [like((depth, 2 * n_path * cols), F32)]
    if squares is not None:
        out.append(like(squares.shape, F32))
    return run(
        body, place, operands, [None] * len(operands), out, [None] * len(out),
        flops=2 * len(views) * n_path * cols * batch * depth, moved=4 * n_path * depth * cols,
        limit=16, aliases={len(operands): 0} if done is not None else {}, name="weight_grad_of",
    )


def update(sums, weight, velocity, weight_grad):
    depth, width = weight.shape
    step = min(128, depth)
    n_sum = len(sums)

    def body(_, *refs):
        weight_ref, velocity_ref, grad_ref, new_weight_ref, new_velocity_ref = refs[n_sum:]
        total = refs[0][...]
        for ref in refs[1:n_sum]:
            total += ref[...]
        grad_norm = jnp.sqrt(jnp.sum(total[:8], keepdims=True))
        weight_norm = jnp.sqrt(jnp.sum(total[8:], keepdims=True))
        trust = weight_norm / (grad_norm + NORM_EPSILON)
        new_velocity = MOMENTUM * velocity_ref[...] + trust * grad_ref[...]
        new_velocity_ref[...] = new_velocity
        new_weight_ref[...] = weight_ref[...] - LEARN_RATE * new_velocity

    tile = pl.BlockSpec((step, width), lambda i, s: (i, 0))
    out = like((depth, width), F32)
    return run(
        body, jnp.zeros((1,), jnp.int32), [*sums, weight, velocity, weight_grad],
        [pl.BlockSpec(one.shape, lambda i, s: (0, 0)) for one in sums] + [tile] * 3, [out, out], [tile, tile],
        grid=(depth // step,), flops=4 * depth * width, moved=20 * depth * width, limit=16, name="update",
    )


def per_device(view_features, weight, velocity):
    n_dp, n_feat = lax.axis_size("dp"), lax.axis_size("feat")
    n_chip = n_dp // 2
    assert n_chip == n_feat and view_features.shape[2] == 2 * weight.shape[0]
    high = list(range(1, n_dp.bit_length() - 1))
    orders = (high, high[::-1])
    chip, core = lax.axis_index("dp") >> 1, bit_value("dp", 0)
    place = jnp.stack([chip, core])

    def bits_at(level):
        return jnp.stack([bit_value("dp", order[level]) for order in orders])

    shares = [[[part] for part in parts] for parts in shares_of(view_features)]
    for step in range(1, n_feat):
        if step == 2:
            sent, turned_own, weight_squares = turn_weight(weight, core, after=[shares[1][0][-1]])
            shares[1][0][-1] = relay(shares[1][0][-1], [turned_own])
        for part in shares[1] + shares[0]:
            part.append(ring_step(part[-1]))
    turned_other = swap(sent, "dp", 1)

    def cross_plane(part, after=()):
        own = list(choose(part, n_chip, after=after))
        for mask in range(1, n_chip):
            own[mask] = swap(own[mask], "dp", 2 * mask)
        return own

    def both_cores(own, collect_after=(), after=()):
        images = collect(place, own, after=collect_after)
        other = swap(images, "dp", 1)
        return assemble(place, images, other, view_features.shape[1], after=after)

    def send_on(v, level, send):
        return [swap(send[p], "dp", 1 << orders[p][level]) for p in range(2)]

    def sum_plane(rows):
        total = rows[0].astype(F32)
        for mask in range(1, n_chip):
            total += swap(rows[mask], "dp", 2 * mask).astype(F32)
        return total.astype(BF16)

    def sum_line(total, bit):
        return (total.astype(F32) + swap(total, "feat", 1 << bit).astype(F32)).astype(BF16)

    def spread_gram(total, after=()):
        parts = [total] + [swap(total, "dp", 2 * mask) for mask in range(1, n_chip)]
        own = pile(parts, after=after)
        return own, swap(own, "dp", 1)

    def gather_step(parts, step, after=()):
        bits = [order[len(order) - 1 - step] for order in orders] * (len(parts) // 2)
        other = [swap(part, "dp", 1 << bit) for part, bit in zip(parts, bits)]
        return join_all(parts, other, [bit_value("dp", bit) for bit in bits], after=after)

    columns, turned, send, keep, got, gram, normed, half, inverse, rows = (
        [None] * 2 for _ in range(10)
    )
    bits = bits_at(0)
    line_bits = range(n_feat.bit_length() - 1)
    pieces = [cross_plane(part) for part in shares[1]]
    columns[1] = both_cores(pieces, collect_after=[turned_own, shares[0][0][-2]])
    turned[1] = turn_columns(columns[1])
    send[1] = forward(1 - bits, turned_own, turned_other, columns[1])
    got[1] = send_on(1, 0, send[1])
    pieces = [cross_plane(part, [send[1][0]]) for part in shares[0]]
    keep[1] = forward(bits, turned_own, turned_other, columns[1], after=[turned[1], send[1][0]])
    for level in range(1, len(high)):
        send[1], keep[1] = add_halves(bits_at(level), keep[1], got[1])
        got[1] = send_on(1, level, send[1])
    columns[0] = both_cores(pieces, [send[1][0]])
    turned[0] = turn_columns(columns[0])
    send[0] = forward(1 - bits, turned_own, turned_other, columns[0])
    ahead = [send[0][0]]
    got[0] = send_on(0, 0, send[0])
    normed[1], half[1], inverse[1] = normalise(keep[1], got[1], after=ahead)
    rows[1] = list(gram_rows(place, half[1], swap(half[1], "dp", 1), n_chip))
    keep[0] = forward(bits, turned_own, turned_other, columns[0], after=[turned[0], send[1][0]])
    for level in range(1, len(high)):
        send[0], keep[0] = add_halves(bits_at(level), keep[0], got[0], after=[rows[1][0]])
        got[0] = send_on(0, level, send[0])
    gram[1] = sum_plane(rows[1])
    normed[0], half[0], inverse[0] = normalise(keep[0], got[0], after=[gram[1]])
    rows[0] = list(gram_rows(place, half[0], swap(half[0], "dp", 1), n_chip))
    for bit in line_bits:
        gram[1] = sum_line(gram[1], bit)
    gram[1] = spread_gram(gram[1])
    gram[0] = sum_plane(rows[0])
    for bit in line_bits:
        gram[0] = sum_line(gram[0], bit)
    out_grad = [None] * 2
    out_grad[0] = out_grad_of(
        place, *gram[1], normed[0], half[0], half[1], inverse[0], after=[gram[0]]
    )
    gram[0] = spread_gram(gram[0], after=[out_grad[0]])
    share = out_grad[0].shape[0] // 2
    out_grad[1] = out_grad_of(place, *gram[0], normed[1], half[1], half[0], inverse[1])
    parts = [one for grad in out_grad for one in (grad[:share], grad[share:])]
    for step in range(len(high) - 1):
        parts = gather_step(parts, step)
    step = len(high) - 1
    first_parts = gather_step(parts[:2], step)
    (weight_grad,) = weight_grad_of(place, [(turned[0], first_parts)], 0)
    second_parts = gather_step(parts[2:], step, after=[weight_grad])
    swapped = [[swap(part, "dp", 1) for part in one] for one in (first_parts, second_parts)]
    weight_grad, squares = weight_grad_of(
        place, [(turned[1], second_parts)], 0, weight_squares, weight_grad, add=True
    )
    weight_grad, squares = weight_grad_of(
        place, list(zip(turned, swapped)), 1, squares, weight_grad
    )
    return update(sum_everywhere(squares), weight, velocity, weight_grad)


def solution(mesh):
    in_specs = (P(None, "dp", "feat"), P("dp", "feat"), P("dp", "feat"))
    out_specs = (P("dp", "feat"), P("dp", "feat"))
    return jax.shard_map(
        per_device, mesh=mesh, in_specs=in_specs, out_specs=out_specs, check_vma=False
    )
```

```python
import jax
import jax.numpy as jnp
from jax import lax
from jax.experimental import pallas as pl
from jax.experimental.pallas import tpu as pltpu
from jax.sharding import PartitionSpec as P

EPSILON = 1e-05
NORM_EPSILON = 1e-06
REDUNDANCY = 0.0051
MOMENTUM = 0.9
LEARN_RATE = 0.2
ROWS_BY_ROWS = (((1,), (1,)), ((), ()))
MIB = 1024 * 1024
F32, BF16 = jnp.float32, jnp.bfloat16


def swap(value, axis, mask):
    return lax.ppermute(value, axis, [(i, i ^ mask) for i in range(lax.axis_size(axis))])


def bit_value(axis, bit):
    return (lax.axis_index(axis) >> bit) & 1


def join(mine, other, bit):
    return jnp.where(
        bit == 0, jnp.concatenate([mine, other], 0), jnp.concatenate([other, mine], 0)
    )


def sum_everywhere(value):
    axes = ("dp", "feat")
    count = lax.axis_size(axes)
    parts = [value]
    for low in range(0, count.bit_length() - 1, 2):
        masks = [mask << low for mask in range(1, 4) if mask << low < count]
        value = sum(parts[1:], parts[0])
        parts = [value] + [
            lax.ppermute(value, axes, [(i, i ^ mask) for i in range(count)]) for mask in masks
        ]
    return parts


def whole(array):
    return None


def like(shape, kind):
    return jax.ShapeDtypeStruct(shape, kind)


def run(body, scalars, operands, in_specs, outs, out_specs, grid=None, scratch=(), after=(),
        flops=0, moved=0, limit=32, name=None, aliases=None):
    n_in, n_after = len(operands), len(after)
    unread = [pl.BlockSpec(memory_space=pl.ANY)] * n_after
    options = dict(
        out_shape=list(outs),
        compiler_params=pltpu.CompilerParams(vmem_limit_bytes=limit * MIB),
        cost_estimate=pl.CostEstimate(flops=flops, bytes_accessed=moved, transcendentals=0),
        input_output_aliases=aliases or {},
        name=name,
    )

    def kernel(scalars_ref, *refs):
        body(scalars_ref, *refs[:n_in], *refs[n_in + n_after :])

    if grid is None:
        inside = pl.BlockSpec(memory_space=pltpu.VMEM)
        in_specs = [spec or inside for spec in in_specs]
        out_specs = [spec or inside for spec in out_specs]
        call = pl.pallas_call(
            kernel, in_specs=[pl.BlockSpec(memory_space=pltpu.SMEM), *in_specs, *unread],
            out_specs=out_specs, scratch_shapes=list(scratch), **options,
        )
    else:
        call = pl.pallas_call(
            kernel,
            grid_spec=pltpu.PrefetchScalarGridSpec(
                num_scalar_prefetch=1, grid=grid, in_specs=list(in_specs) + unread,
                out_specs=list(out_specs), scratch_shapes=list(scratch),
            ),
            **options,
        )
    return call(scalars, *operands, *after)


def fold(square):
    part = jnp.sum(square.reshape(-1, 8, square.shape[1]), 0)
    return sum(part[:, start : start + 128] for start in range(0, part.shape[1], 128))


def turn_weight(weight, core, after=()):
    depth, width = weight.shape
    quarter = width // 4
    step = min(256, quarter)
    steps = quarter // step

    def body(core_ref, weight_ref, sent_ref, kept_ref, square_ref):
        block = weight_ref[...]
        block_turned = block.T.astype(BF16)
        square = fold(block * block)
        first = (pl.program_id(0) == 0) & (pl.program_id(1) == 0)

        @pl.when(pl.program_id(0) == 0)
        def _():
            sent_ref[...] = block_turned

        @pl.when(pl.program_id(0) == 1)
        def _():
            kept_ref[...] = block_turned

        @pl.when(first)
        def _():
            square_ref[:8, :] = jnp.zeros_like(square)
            square_ref[8:, :] = square

        @pl.when(jnp.logical_not(first))
        def _():
            square_ref[8:, :] += square

    out = like((2 * quarter, depth), BF16)
    return run(
        body, core.reshape(1), [weight],
        [
            pl.BlockSpec(
                (depth, step),
                lambda k, j, c: (0, (2 * (j // steps) + (c[0] ^ (1 - k))) * steps + j % steps),
            )
        ],
        [out, out, like((16, 128), F32)],
        [
            pl.BlockSpec((step, depth), lambda k, j, c: (jnp.where(k == 0, j, 2 * steps - 1), 0)),
            pl.BlockSpec((step, depth), lambda k, j, c: (jnp.where(k == 1, j, 0), 0)),
            pl.BlockSpec((16, 128), lambda k, j, c: (0, 0)),
        ],
        grid=(2, 2 * steps), after=after, flops=2 * depth * width, moved=6 * depth * width, limit=16, name="turn_weight",
    )


def shares_of(view_features):
    _, count, width = view_features.shape
    half = count // 2

    def body(_, rows_ref, first_ref, low_ref, high_ref):
        low_ref[...] = rows_ref[1, :half, :]
        high_ref[...] = rows_ref[1, half:, :]
        first_ref[...] = rows_ref[0]

    outs = [like((rows, width), BF16) for rows in (count, half, half)]
    first, low, high = run(
        body, jnp.zeros((1,), jnp.int32), [view_features], [whole(view_features)],
        outs, [whole(out) for out in outs], moved=8 * count * width, limit=8, name="shares_of",
    )
    return [first], [low, high]


def relay(value, after):
    def body(_, value_ref, out_ref):
        out_ref[...] = value_ref[...]

    (out,) = run(
        body, jnp.zeros((1,), jnp.int32), [value], [whole(value)], [like(value.shape, BF16)],
        [whole(value)], after=after, moved=4 * value.size, limit=8, name="relay",
    )
    return out


def ring_step(share):
    n_feat = lax.axis_size("feat")
    return lax.ppermute(share, "feat", [(i, (i + 1) % n_feat) for i in range(n_feat)])


def choose(shares, n_chip, after=()):
    n_feat = len(shares)
    chip = lax.axis_index("dp") >> 1
    back = [lax.rem(lax.axis_index("feat") - (chip ^ mask) + n_feat, n_feat) for mask in range(n_chip)]

    def body(back_ref, *refs):
        for mask in range(n_chip):
            for place in range(n_feat):

                @pl.when(back_ref[mask] == place)
                def _():
                    refs[n_feat + mask][...] = refs[place][...]

    shape = shares[0].shape
    return run(
        body, jnp.stack(back), shares, [whole(share) for share in shares],
        [like(shape, BF16)] * n_chip, [whole(shares[0])] * n_chip,
        after=after, moved=4 * n_chip * shape[0] * shape[1], limit=10, name="choose",
    )


def collect(place, own, after=()):
    n_part, n_chip = len(own), len(own[0])
    count, width = own[0][0].shape
    operands = [piece for pieces in own for piece in pieces]

    def body(place_ref, *refs):
        for part in range(n_part):
            for mask in range(n_chip):
                row = ((place_ref[0] ^ mask) * n_part + part) * count
                rows = pl.ds(pl.multiple_of(row, count), count)
                refs[-1][rows, :] = refs[part * n_chip + mask][...]

    out = like((len(operands) * count, width), BF16)
    (images,) = run(
        body, place, operands, [whole(piece) for piece in operands], [out], [whole(out)],
        after=after, moved=4 * len(operands) * count * width, limit=10, name="collect",
    )
    return images


def assemble(place, own, other, count, after=()):
    n_chip = own.shape[0] // count
    width = own.shape[1]
    half = width // 2

    def body(place_ref, own_ref, other_ref, out_ref):
        core = place_ref[1]
        for flip, ref in ((0, own_ref), (1, other_ref)):
            for chip in range(n_chip):
                rows = pl.ds(pl.multiple_of((chip * 2 + (core ^ flip)) * count, count), count)
                for side in range(2):
                    lane = pl.multiple_of((core ^ side) * half, half)
                    out_ref[rows, side * half : (side + 1) * half] = ref[
                        chip * count : (chip + 1) * count, pl.ds(lane, half)
                    ]

    out = like((2 * n_chip * count, width), BF16)
    (columns,) = run(
        body, place, [own, other], [whole(own), whole(other)], [out], [whole(out)], after=after,
        moved=8 * n_chip * count * width, limit=12, name="assemble",
    )
    return columns


def turn_columns(columns):
    batch, width = columns.shape
    depth = width // 2
    step = 256

    def body(_, columns_ref, out_ref):
        out_ref[...] = columns_ref[...].astype(F32).T.astype(BF16)

    (turned,) = run(
        body, jnp.zeros((1,), jnp.int32), [columns],
        [pl.BlockSpec((step, depth), lambda i, s: (i, 0))],
        [like((depth, batch), BF16)], [pl.BlockSpec((depth, step), lambda i, s: (0, i))],
        grid=(batch // step,), moved=4 * batch * depth, limit=8, name="turn_columns",
    )
    return turned


def forward(bits, turned_own, turned_other, columns, after=()):
    rows, depth = turned_own.shape
    batch = columns.shape[0]
    out_rows = rows // 4

    def body(bits_ref, own_ref, other_ref, columns_ref, out_a, out_b):
        starts = [pl.multiple_of((2 * p + bits_ref[p]) * out_rows, out_rows) for p in range(2)]
        own = jnp.concatenate([own_ref[pl.ds(start, out_rows), :] for start in starts], 0)
        other = jnp.concatenate([other_ref[pl.ds(start, out_rows), :] for start in starts], 0)
        block = lax.dot_general(
            own, columns_ref[:, :depth], ROWS_BY_ROWS, preferred_element_type=F32
        )
        block += lax.dot_general(
            other, columns_ref[:, depth:], ROWS_BY_ROWS, preferred_element_type=F32
        )
        block = (block - jnp.mean(block, 1, keepdims=True)).astype(BF16)
        out_a[...] = block[:out_rows]
        out_b[...] = block[out_rows:]

    return run(
        body, bits, [turned_own, turned_other, columns], [None] * 3,
        [like((out_rows, batch), BF16)] * 2, [None] * 2, after=after,
        flops=8 * out_rows * depth * batch, moved=8 * out_rows * depth + 4 * batch * depth,
        limit=16, name="forward",
    )


def add_halves(bits, kept, got, after=()):
    rows, batch = kept[0].shape
    half = rows // 2

    def body(bits_ref, kept_a, got_a, kept_b, got_b, send_a, send_b, keep_a, keep_b):
        for path, (kept_ref, got_ref, send_ref, keep_ref) in enumerate(
            ((kept_a, got_a, send_a, keep_a), (kept_b, got_b, send_b, keep_b))
        ):
            for flip, out_ref in ((1, send_ref), (0, keep_ref)):
                rows_of = pl.ds(pl.multiple_of((bits_ref[path] ^ flip) * half, half), half)
                total = kept_ref[rows_of, :].astype(F32) + got_ref[rows_of, :].astype(F32)
                out_ref[...] = total.astype(BF16)

    operands = [kept[0], got[0], kept[1], got[1]]
    out = like((half, batch), BF16)
    outs = run(
        body, bits, operands, [whole(one) for one in operands],
        [out] * 4, [whole(out)] * 4, after=after, moved=12 * rows * batch, limit=16, name="add_halves",
    )
    return outs[:2], outs[2:]


def normalise(kept, got, after=()):
    rows, batch = kept[0].shape

    def body(_, kept_a, got_a, kept_b, got_b, normed_ref, half_ref, inverse_ref):
        for path, (kept_ref, got_ref) in enumerate(((kept_a, got_a), (kept_b, got_b))):
            total = kept_ref[...].astype(F32) + got_ref[...].astype(F32)
            total -= jnp.mean(total, 1, keepdims=True)
            inverse = lax.rsqrt(jnp.mean(total * total, 1, keepdims=True) + EPSILON)
            normed = total * inverse
            place = slice(path * rows, (path + 1) * rows)
            normed_ref[place, :] = normed
            half_ref[place, :] = normed.astype(BF16)
            inverse_ref[place, :] = jnp.broadcast_to(inverse, (rows, 128))

    operands = [kept[0], got[0], kept[1], got[1]]
    outs = [like((2 * rows, width), kind) for width, kind in ((batch, F32), (batch, BF16), (128, F32))]
    return run(
        body, jnp.zeros((1,), jnp.int32), operands, [whole(one) for one in operands],
        outs, [whole(out) for out in outs], after=after, moved=20 * rows * batch, limit=16, name="normalise",
    )


def gram_rows(place, own, other, n_chip, after=()):
    rows, batch = own.shape
    blocks = 2 * n_chip
    size = batch // blocks
    width = (blocks // 2 + 1) * size

    def body(place_ref, own_ref, other_ref, *refs):
        twice_ref = refs[-1]
        for start, ref in ((0, own_ref), (rows, other_ref)):
            twice_ref[start : start + rows, :batch] = ref[...]
            twice_ref[start : start + rows, batch:] = ref[...]
        for mask in range(n_chip):
            row = pl.multiple_of(((place_ref[0] ^ mask) * 2 + place_ref[1]) * size, size)
            left = twice_ref[:, pl.ds(row, size)].astype(F32).T.astype(BF16)
            right = twice_ref[:, pl.ds(row, width)]
            refs[mask][...] = jnp.dot(left, right, preferred_element_type=F32).astype(BF16)

    out = like((size, width), BF16)
    return run(
        body, place, [own, other], [whole(own), whole(other)],
        [out] * n_chip, [whole(out)] * n_chip,
        scratch=[pltpu.VMEM((2 * rows, 2 * batch), BF16)], after=after,
        flops=4 * rows * width * batch // 2, moved=8 * rows * batch, limit=24, name="gram_rows",
    )


def join_all(mine, other, bits, after=()):
    count = len(mine)

    def body(bits_ref, *refs):
        for index in range(count):
            rows = mine[index].shape[0]
            bit = bits_ref[index]
            first = pl.multiple_of(bit * rows, rows)
            second = pl.multiple_of((1 - bit) * rows, rows)
            out_ref = refs[2 * count + index]
            out_ref[pl.ds(first, rows), :] = refs[index][...]
            out_ref[pl.ds(second, rows), :] = refs[count + index][...]

    outs = [like((2 * one.shape[0], one.shape[1]), BF16) for one in mine]
    return run(
        body, jnp.stack(bits), [*mine, *other], [whole(one) for one in [*mine, *other]],
        outs, [whole(out) for out in outs], after=after,
        moved=8 * sum(one.size for one in mine), limit=12, name="join_all",
    )


def add_up(parts, after=()):
    def body(_, *refs):
        total = refs[0][...].astype(F32)
        for ref in refs[1:-1]:
            total += ref[...].astype(F32)
        refs[-1][...] = total.astype(BF16)

    (out,) = run(
        body, jnp.zeros((1,), jnp.int32), parts, [whole(part) for part in parts],
        [like(parts[0].shape, BF16)], [whole(parts[0])], after=after,
        moved=4 * len(parts) * parts[0].size, limit=8, name="add_up",
    )
    return out


def pile(parts, after=()):
    rows, width = parts[0].shape

    def body(_, *refs):
        for index in range(len(parts)):
            refs[-1][index] = refs[index][...]

    out = like((len(parts), rows, width), BF16)
    (stack,) = run(
        body, jnp.zeros((1,), jnp.int32), parts, [whole(part) for part in parts],
        [out], [whole(out)], after=after, moved=4 * len(parts) * rows * width, limit=8, name="pile",
    )
    return stack


def out_grad_of(place, gram_own, gram_other, normed, half, half_other, inverse, after=()):
    rows, batch = half.shape
    n_chip = gram_own.shape[0]
    blocks = 2 * n_chip
    size = batch // blocks

    def body(place_ref, own_ref, other_ref, normed_ref, half_ref, half_other_ref, inverse_ref,
             out_ref, gram_ref):
        for flip, ref in ((0, own_ref), (1, other_ref)):
            for mask in range(n_chip):
                row = (place_ref[0] ^ mask) * 2 + (place_ref[1] ^ flip)
                down = pl.ds(pl.multiple_of(row * size, size), size)
                for ahead in range(blocks // 2 + 1):
                    col = lax.rem(row + ahead, blocks)
                    along = pl.ds(pl.multiple_of(col * size, size), size)
                    tile = ref[mask, :, ahead * size : (ahead + 1) * size]
                    gram_ref[down, along] = tile
                    if 0 < ahead < blocks // 2:
                        gram_ref[along, down] = tile.astype(F32).T.astype(BF16)
        normed = normed_ref[...]
        other = half_other_ref[...].astype(F32)
        diagonal = jnp.mean(half_ref[...].astype(F32) * other, 1, keepdims=True)
        extra = (-2.0 * (1.0 - diagonal) - 2.0 * REDUNDANCY * diagonal) / batch
        grads = lax.dot_general(
            half_ref[...], gram_ref[...], ROWS_BY_ROWS, preferred_element_type=F32
        )
        grads = grads * (2.0 * REDUNDANCY / (batch * batch)) + extra * other
        grad_mean = jnp.mean(grads, 1, keepdims=True)
        grad_cross = jnp.mean(grads * normed, 1, keepdims=True)
        out_ref[...] = (
            inverse_ref[:, :1] * (grads - grad_mean - normed * grad_cross)
        ).astype(BF16)

    operands = [gram_own, gram_other, normed, half, half_other, inverse]
    out = like((rows, batch), BF16)
    (out_grad,) = run(
        body, place, operands, [whole(one) for one in operands], [out], [whole(out)],
        scratch=[pltpu.VMEM((batch, batch), BF16)], after=after,
        flops=2 * rows * batch * batch, moved=12 * rows * batch + 2 * batch * batch, limit=24, name="out_grad_of",
    )
    return out_grad


def weight_grad_of(place, views, flip, squares=None, done=None, add=False):
    depth, batch = views[0][0].shape
    n_path = len(views[0][1])
    cols = views[0][1][0].shape[0]
    operands = [one for turned, pieces in views for one in (turned, *pieces)]
    n_product = len(operands)

    def body(place_ref, *refs):
        n_out = 1 if squares is None else 2
        out_ref = refs[-n_out]
        core = place_ref[1]
        if squares is not None:
            square_ref = refs[-1]
            square_ref[...] = refs[n_product][...]
        for path in range(n_path):
            start = pl.multiple_of((2 * path + (core ^ flip)) * cols, cols)
            place_of = (slice(None), pl.ds(start, cols))
            total = refs[-n_out - 1][place_of] if add else None
            for first in range(0, n_product, n_path + 1):
                product = lax.dot_general(
                    refs[first][...], refs[first + 1 + path][...], ROWS_BY_ROWS,
                    preferred_element_type=F32,
                )
                total = product if total is None else total + product
            out_ref[place_of] = total
            if squares is not None:
                square_ref[:8, :] += fold(total * total)

    operands += [one for one in (squares, done) if one is not None]
    out = [like((depth, 2 * n_path * cols), F32)]
    if squares is not None:
        out.append(like(squares.shape, F32))
    return run(
        body, place, operands, [None] * len(operands), out, [None] * len(out),
        flops=2 * len(views) * n_path * cols * batch * depth, moved=4 * n_path * depth * cols,
        limit=16, aliases={len(operands): 0} if done is not None else {}, name="weight_grad_of",
    )


def update(sums, weight, velocity, weight_grad):
    depth, width = weight.shape
    step = min(128, depth)
    n_sum = len(sums)

    def body(_, *refs):
        weight_ref, velocity_ref, grad_ref = refs[n_sum : n_sum + 3]
        outs, (slots_ref, sems) = refs[n_sum + 3 : n_sum + 5], refs[n_sum + 5 :]
        total = refs[0][...]
        for ref in refs[1:n_sum]:
            total += ref[...]
        grad_norm = jnp.sqrt(jnp.sum(total[:8], keepdims=True))
        weight_norm = jnp.sqrt(jnp.sum(total[8:], keepdims=True))
        trust = weight_norm / (grad_norm + NORM_EPSILON)
        copies = []
        for index in range(depth // step):
            rows, slot = slice(index * step, (index + 1) * step), index % 2
            for copy in copies[2 * (index - 2) : 2 * (index - 1)] if index > 1 else ():
                copy.wait()
            new_velocity = MOMENTUM * velocity_ref[rows, :] + trust * grad_ref[rows, :]
            slots_ref[slot, 0] = weight_ref[rows, :] - LEARN_RATE * new_velocity
            slots_ref[slot, 1] = new_velocity
            for which, out_ref in enumerate(outs):
                copies.append(
                    pltpu.make_async_copy(
                        slots_ref.at[slot, which], out_ref.at[rows, :], sems.at[slot, which]
                    )
                )
                copies[-1].start()
        for copy in copies[-4:]:
            copy.wait()

    out = like((depth, width), F32)
    hbm = pl.BlockSpec(memory_space=pl.ANY)
    return run(
        body, jnp.zeros((1,), jnp.int32), [*sums, weight, velocity, weight_grad],
        [None] * (n_sum + 3), [out, out], [hbm, hbm],
        scratch=[pltpu.VMEM((2, 2, step, width), F32), pltpu.SemaphoreType.DMA((2, 2))],
        flops=4 * depth * width, moved=20 * depth * width, limit=10, name="update",
    )


def per_device(view_features, weight, velocity):
    n_dp, n_feat = lax.axis_size("dp"), lax.axis_size("feat")
    n_chip = n_dp // 2
    assert n_chip == n_feat and view_features.shape[2] == 2 * weight.shape[0]
    high = list(range(1, n_dp.bit_length() - 1))
    orders = (high, high[::-1])
    chip, core = lax.axis_index("dp") >> 1, bit_value("dp", 0)
    place = jnp.stack([chip, core])

    def bits_at(level):
        return jnp.stack([bit_value("dp", order[level]) for order in orders])

    shares = [[[part] for part in parts] for parts in shares_of(view_features)]
    for step in range(1, n_feat):
        if step == 2:
            sent, turned_own, weight_squares = turn_weight(weight, core, after=[shares[1][0][-1]])
            shares[1][0][-1] = relay(shares[1][0][-1], [turned_own])
        for part in shares[1] + shares[0]:
            part.append(ring_step(part[-1]))
    turned_other = swap(sent, "dp", 1)

    def cross_plane(part, after=()):
        own = list(choose(part, n_chip, after=after))
        for mask in range(1, n_chip):
            own[mask] = swap(own[mask], "dp", 2 * mask)
        return own

    def both_cores(own, collect_after=(), after=()):
        images = collect(place, own, after=collect_after)
        other = swap(images, "dp", 1)
        return assemble(place, images, other, view_features.shape[1], after=after)

    def send_on(v, level, send):
        return [swap(send[p], "dp", 1 << orders[p][level]) for p in range(2)]

    def sum_plane(rows):
        total = rows[0].astype(F32)
        for mask in range(1, n_chip):
            total += swap(rows[mask], "dp", 2 * mask).astype(F32)
        return total.astype(BF16)

    def sum_line(total, bit):
        return (total.astype(F32) + swap(total, "feat", 1 << bit).astype(F32)).astype(BF16)

    def spread_gram(total, after=()):
        parts = [total] + [swap(total, "dp", 2 * mask) for mask in range(1, n_chip)]
        own = pile(parts, after=after)
        return own, swap(own, "dp", 1)

    def gather_step(parts, step, after=()):
        bits = [order[len(order) - 1 - step] for order in orders] * (len(parts) // 2)
        other = [swap(part, "dp", 1 << bit) for part, bit in zip(parts, bits)]
        return join_all(parts, other, [bit_value("dp", bit) for bit in bits], after=after)

    columns, turned, send, keep, got, gram, normed, half, inverse, rows = (
        [None] * 2 for _ in range(10)
    )
    bits = bits_at(0)
    line_bits = range(n_feat.bit_length() - 1)
    pieces = [cross_plane(part) for part in shares[1]]
    columns[1] = both_cores(pieces, collect_after=[turned_own, shares[0][0][-2]])
    turned[1] = turn_columns(columns[1])
    send[1] = forward(1 - bits, turned_own, turned_other, columns[1])
    got[1] = send_on(1, 0, send[1])
    pieces = [cross_plane(part, [send[1][0]]) for part in shares[0]]
    keep[1] = forward(bits, turned_own, turned_other, columns[1], after=[turned[1], send[1][0]])
    for level in range(1, len(high)):
        send[1], keep[1] = add_halves(bits_at(level), keep[1], got[1])
        got[1] = send_on(1, level, send[1])
    columns[0] = both_cores(pieces, [send[1][0]])
    turned[0] = turn_columns(columns[0])
    send[0] = forward(1 - bits, turned_own, turned_other, columns[0])
    ahead = [send[0][0]]
    got[0] = send_on(0, 0, send[0])
    normed[1], half[1], inverse[1] = normalise(keep[1], got[1], after=ahead)
    rows[1] = list(gram_rows(place, half[1], swap(half[1], "dp", 1), n_chip))
    keep[0] = forward(bits, turned_own, turned_other, columns[0], after=[turned[0], send[1][0]])
    for level in range(1, len(high)):
        send[0], keep[0] = add_halves(bits_at(level), keep[0], got[0], after=[rows[1][0]])
        got[0] = send_on(0, level, send[0])
    gram[1] = sum_plane(rows[1])
    normed[0], half[0], inverse[0] = normalise(keep[0], got[0], after=[gram[1]])
    rows[0] = list(gram_rows(place, half[0], swap(half[0], "dp", 1), n_chip))
    for bit in line_bits:
        gram[1] = sum_line(gram[1], bit)
    gram[1] = spread_gram(gram[1])
    gram[0] = sum_plane(rows[0])
    for bit in line_bits:
        gram[0] = sum_line(gram[0], bit)
    out_grad = [None] * 2
    out_grad[0] = out_grad_of(
        place, *gram[1], normed[0], half[0], half[1], inverse[0], after=[gram[0]]
    )
    gram[0] = spread_gram(gram[0], after=[out_grad[0]])
    share = out_grad[0].shape[0] // 2
    out_grad[1] = out_grad_of(place, *gram[0], normed[1], half[1], half[0], inverse[1])
    parts = [one for grad in out_grad for one in (grad[:share], grad[share:])]
    for step in range(len(high) - 1):
        parts = gather_step(parts, step)
    step = len(high) - 1
    first_parts = gather_step(parts[:2], step)
    (weight_grad,) = weight_grad_of(place, [(turned[0], first_parts)], 0)
    second_parts = gather_step(parts[2:], step, after=[weight_grad])
    swapped = [[swap(part, "dp", 1) for part in one] for one in (first_parts, second_parts)]
    weight_grad, squares = weight_grad_of(
        place, [(turned[1], second_parts)], 0, weight_squares, weight_grad, add=True
    )
    weight_grad, squares = weight_grad_of(
        place, list(zip(turned, swapped)), 1, squares, weight_grad
    )
    return update(sum_everywhere(squares), weight, velocity, weight_grad)


def solution(mesh):
    in_specs = (P(None, "dp", "feat"), P("dp", "feat"), P("dp", "feat"))
    out_specs = (P("dp", "feat"), P("dp", "feat"))
    return jax.shard_map(
        per_device, mesh=mesh, in_specs=in_specs, out_specs=out_specs, check_vma=False
    )
```
